32 devices in a mesh: rep: 8 (over y, x, core), shard: 4 (over z).
Axes of the slice: x: 2, y: 2, z: 4, core: 2. Of those that a mesh axis runs over, the one named last changes fastest.
Arguments:
- hidden_in: bfloat16 [8192, 1024], P(('rep', 'shard')), may hold values from -6 to 6
- valid_mask: int32 [8192], P(('rep', 'shard')), may hold values from 0 to 1
- teacher: bfloat16 [8192, 1024], P(('rep', 'shard')), may hold values from -9 to 9
- routes: int32 [8192, 8], P(('rep', 'shard')), may hold values from 0 to 15, all different within a row; in each aligned block of 256 rows (0 to 255, 256 to 511, ...) at most 160 rows name the same one
- attn_norm: bfloat16 [1024], P('shard'), may hold values from 0.5 to 1.5
- w_query: bfloat16 [1024, 1024], P('shard'), may hold values from -0.75 to 0.75
- w_key: bfloat16 [1024, 512], P('shard'), may hold values from -0.75 to 0.75
- w_value: bfloat16 [1024, 512], P('shard'), may hold values from -0.1875 to 0.1875
- w_output: bfloat16 [1024, 1024], P('shard'), may hold values from -4 to 4
- ffn_norm: bfloat16 [1024], P('shard'), may hold values from 0.5 to 1.5
- router: bfloat16 [1024, 16], P('shard'), may hold values from -0.09375 to 0.09375
- w_in: bfloat16 [16, 1024, 1024], P('shard'), may hold values from -0.1875 to 0.1875
- w_out: bfloat16 [16, 512, 1024], P('shard'), may hold values from -4 to 4
Outputs:
- output: bfloat16 [8192, 1024], P(('rep', 'shard'))
- loss: float32 [], replicated
- input_grad: float32 [8192, 1024], P(('rep', 'shard'))
- grad_attn_norm: float32 [1024], P('shard')
- grad_w_query: float32 [1024, 1024], P('shard')
- grad_w_key: float32 [1024, 512], P('shard')
- grad_w_value: float32 [1024, 512], P('shard')
- grad_w_output: float32 [1024, 1024], P('shard')
- grad_ffn_norm: float32 [1024], P('shard')
- grad_router: float32 [1024, 16], P('shard')
- grad_w_in: float32 [16, 1024, 1024], P('shard')
- grad_w_out: float32 [16, 512, 1024], P('shard')
The draws below stay inside these ranges and needn't reach their ends.
Inputs may be any that keep to these rules, and one draw needn't show every extreme that they name: `routes`: each row names 8 different experts. Among one device's 256 rows (aligned blocks of the token order) no expert is named by more than 160 rows, a bound that some block reaches.
All inputs are finite; a program needn't handle non-finite values.
Results may differ from the reference program's by a relative error of at most 0.013.
The reference program's roundings to bfloat16 on the way count: a program that leaves them out, or rounds other values in their place, can miss the bound.
Values may be sent and summed in bfloat16 or wider, within the bound.
No kernel may reach another device: no remote copies, remote signals or barrier semaphores. Data moves between devices by JAX's collectives and lax.ppermute only.
A program may use at most 512 MiB of HBM per device.

```python
import math
import jax
import jax.numpy as jnp
import numpy as np
from jax import lax

D = 1024
HEADS = 16
KV_HEADS = 8
HEAD_DIM = 64
FF = 512
EXPERTS = 16
TOP = 8
BLOCK = 256
SEQ_LEN = 1024
ROWS = 256
TOKENS = 8192
CAP = 160
N_SHARD = 4


def draw_valid_mask(key, part):
    positions = jnp.arange(TOKENS, dtype=jnp.int32)
    draws = jax.random.randint(key, (TOKENS,), 0, 2 * TOKENS, dtype=jnp.int32)
    return (draws < TOKENS // 2 + positions * 3 // 2 + 1).astype(jnp.int32)


def block_levels(stream_key, dims, cuts, smallest, top_value):
    def one(axis_at, shards_of):
        steps = jax.random.uniform(jax.random.fold_in(jax.random.fold_in(stream_key, 6), axis_at), (shards_of,), jnp.float32, smallest / len(cuts), top_value / len(cuts))
        return jnp.repeat(jnp.exp(steps), dims[axis_at] // shards_of).reshape((-1,) + (1,) * (len(dims) - axis_at - 1))

    gain = one(*cuts[0])
    for cut in cuts[1:]:
        gain = gain * one(*cut)
    return gain


def deal_out(key, own, number, rows, number_of, top, reach, lean):
    order = jax.random.permutation(key, number_of)
    packed, common = shares(number_of, rows * top, reach, lean, True), shares(number_of, rows * top, reach, lean, False)
    places = jnp.arange(number_of)

    def named(lengths, rotation):
        used = int((lengths > 0).sum())
        fixed = max(1, used // 4)
        moved = fixed + (places - fixed + rotation * (used - fixed)) % max(1, number_of - fixed)
        return jnp.zeros((number_of,), jnp.int32).at[order[jnp.where(places < fixed, places, moved)]].set(jnp.asarray(lengths, jnp.int32))

    lengths = jnp.where(number % 4 == 0, named(packed, number // 4), named(common, number - number // 4 - 1))
    mixed = jax.random.permutation(jax.random.fold_in(own, 3), number_of)
    source_of, sink = mixed[0:number_of // 2 * 2:2], mixed[1:number_of // 2 * 2:2]
    slack = jnp.minimum(lengths[source_of] - 1, reach - lengths[sink]) // 2
    slack = jnp.where((source_of == order[0]) | (sink == order[0]) | (lengths[sink] == 0), 0, jnp.maximum(slack, 0))
    moved = jax.random.randint(jax.random.fold_in(own, 4), (number_of // 2,), 0, 1 << 20) % (slack + 1)
    lengths = lengths.at[source_of].add(-moved).at[sink].add(moved)
    labels = jnp.searchsorted(jnp.cumsum(lengths), jnp.arange(rows * top), side="right").astype(jnp.int32)
    listing = labels.reshape(top, rows).T
    listing = listing[jax.random.permutation(jax.random.fold_in(own, 1), rows)]
    rotation = jax.random.randint(jax.random.fold_in(own, 2), (rows, 1), 0, top)
    return jnp.take_along_axis(listing, (jnp.arange(top)[None, :] + rotation) % top, axis=1)


def shares(count, total, limit, slope, full):
    loads = [(1 << 20) // math.isqrt(grade ** slope) + 1 for grade in range(1, count + 1)]
    largest = limit if full else min(limit, max(-(-total // count), total * loads[0] // sum(loads)))
    least = 1 if total - largest >= count - 1 else 0
    counts, spare = [largest] + [least] * (count - 1), total - largest - least * (count - 1)
    while spare > 0:
        movable = [i for i in range(1, count) if counts[i] < largest] or [i for i in range(1, count) if counts[i] < limit]
        whole, left = sum([loads[i] for i in movable]), spare
        for i in movable:
            extra = min(limit - counts[i], max(1, left * loads[i] // whole), spare)
            counts[i] = counts[i] + extra
            spare = spare - extra
    return np.array(counts)


def noise(rng, shape, width, bound, split=(), held_as=jnp.bfloat16):
    drawn = jax.random.normal(rng, shape, jnp.float32) * width
    if len(split) > 0:
        drawn = block_levels(rng, shape, split, -0.22, 0.18) * drawn
    return jnp.clip(drawn, min=-bound, max=bound).astype(held_as)


def setup_inputs(seed: int = 0) -> dict:
    splits = jax.random.split(jax.random.key(seed), 14)
    hidden_in = noise(splits[0], (TOKENS, D), 1.0, 6.0, ((0, 32),))
    valid_mask = draw_valid_mask(jax.random.fold_in(splits[13], 71), 0)
    teacher = noise(splits[2], (TOKENS, D), 1.5, 9.0, ((0, 32),))
    routes_keys = jax.random.split(jax.random.fold_in(splits[3], 1), TOKENS // ROWS)
    routes_turns = jax.random.permutation(jax.random.fold_in(splits[3], 3), TOKENS // ROWS)
    routes = jax.vmap(lambda own, number: deal_out(jax.random.fold_in(splits[3], 2), own, number, ROWS, EXPERTS, TOP, CAP, 1))(routes_keys, routes_turns).reshape((TOKENS, TOP))
    attn_norm = jnp.clip(1.0 + 0.1 * jax.random.normal(splits[4], (D,), jnp.float32), 0.5, 1.5).astype(jnp.bfloat16)
    w_query = noise(splits[5], (D, HEADS * HEAD_DIM), HEAD_DIM ** -0.5, 0.75, ((0, 4),))
    w_key = noise(splits[6], (D, KV_HEADS * HEAD_DIM), HEAD_DIM ** -0.5, 0.75, ((0, 4),))
    w_value = noise(splits[7], (D, KV_HEADS * HEAD_DIM), D ** -0.5, 0.1875, ((0, 4),))
    w_output = noise(splits[8], (HEADS * HEAD_DIM, D), 2 ** -0.5, 4.0, ((0, 4),))
    ffn_norm = jnp.clip(1.0 + 0.1 * jax.random.normal(splits[9], (D,), jnp.float32), 0.5, 1.5).astype(jnp.bfloat16)
    router = noise(splits[10], (D, EXPERTS), (4 * D) ** -0.5, 0.09375, ((0, 4),))
    w_in = noise(splits[11], (EXPERTS, D, 2 * FF), D ** -0.5, 0.1875, ((0, 4),))
    w_out = noise(splits[12], (EXPERTS, FF, D), 2 ** -0.5, 4.0, ((0, 4),))
    return dict(hidden_in=hidden_in, valid_mask=valid_mask, teacher=teacher, routes=routes, attn_norm=attn_norm, w_query=w_query, w_key=w_key, w_value=w_value, w_output=w_output, ffn_norm=ffn_norm, router=router, w_in=w_in, w_out=w_out)


@jax.custom_vjp
def low(v):
    return lax.optimization_barrier(v.astype(jnp.bfloat16)).astype(jnp.float32)

@jax.custom_vjp
def low_back(v):
    return v

def low_keep(v):
    return (low(v), None)

def low_pass(kept, grad):
    return (grad,)

def back_keep(v):
    return (v, None)

def back_low(kept, grad):
    return (low(grad),)
low.defvjp(low_keep, low_pass)
low_back.defvjp(back_keep, back_low)
norm_eps = 1e-06
resid_mult = 0.22
attn_mult = 0.015625
rope_base = 10000.0
very_low = -1e+30
exact = lax.Precision.HIGHEST

def rms_norm(values, gain_vec):
    return values * lax.rsqrt(lax.optimization_barrier(jnp.mean(values * values, axis=-1, keepdims=True)) + norm_eps) * gain_vec

def rope_tables(positions, half_dim):
    frequency = rope_base ** (-jnp.arange(half_dim, dtype=jnp.float32) / half_dim)
    angles = positions.astype(jnp.float32)[:, None] * frequency[None, :]
    return (jnp.cos(angles), jnp.sin(angles))

def rotate(values, cosine, sine_table):
    half_dim = values.shape[-1] // 2
    first_half = values[..., :half_dim]
    second_half = values[..., half_dim:]
    cos_wide = cosine[:, None, :]
    sin_wide = sine_table[:, None, :]
    return jnp.concatenate([first_half * cos_wide - second_half * sin_wide, second_half * cos_wide + first_half * sin_wide], -1)

def attend_sequence(queries, keys, values_in):
    seq_count = queries.shape[0]
    blocks = jnp.arange(seq_count) // BLOCK
    allowed = blocks[None, :] <= blocks[:, None]
    group_size = HEADS // KV_HEADS
    query_groups = queries.reshape(seq_count, KV_HEADS, group_size, HEAD_DIM).transpose(1, 2, 0, 3)
    key_groups = keys.transpose(1, 0, 2)
    value_groups = values_in.transpose(1, 0, 2)

    def one_group(inputs):
        query_part, key_part, value_part = inputs
        score_vals = low_back(jnp.einsum('hqd,kd->hqk', query_part, key_part, precision=exact) * attn_mult)
        score_vals = jnp.where(allowed[None], score_vals, very_low)
        row_max = lax.optimization_barrier(jnp.max(score_vals, -1, keepdims=True))
        expo_vals = jnp.exp(score_vals - row_max)
        prob_vals = low(expo_vals / lax.optimization_barrier(jnp.sum(expo_vals, -1, keepdims=True)))
        return jnp.einsum('hqk,kd->hqd', prob_vals, value_part, precision=exact)
    outputs = lax.map(jax.checkpoint(one_group), (query_groups, key_groups, value_groups))
    return outputs.transpose(2, 0, 1, 3).reshape(seq_count, HEADS * HEAD_DIM)

def reference(hidden_in, valid_mask, teacher, routes, attn_norm, w_query, w_key, w_value, w_output, ffn_norm, router, w_in, w_out):
    floats = tuple((operand.astype(jnp.float32) for operand in (hidden_in, attn_norm, w_query, w_key, w_value, w_output, ffn_norm, router, w_in, w_out)))
    teacher_f = teacher.astype(jnp.float32)
    valid_f = valid_mask.astype(jnp.float32)
    valid_count = jnp.sum(valid_f)
    seq_total = TOKENS // SEQ_LEN

    def forward(hidden_f, gain_attn, query_w, key_w, value_w, output_w, gain_ffn, router_w, in_w, out_w):

        def experts_block(block_rows, block_routes):
            logits = low_back(jnp.dot(block_rows, router_w, precision=exact))
            hits = (block_routes[..., None] == jnp.arange(EXPERTS, dtype=jnp.int32)).astype(jnp.int32)
            chosen = lax.optimization_barrier(jnp.sum(hits.astype(jnp.float32) * logits[:, None, :], -1))
            gates = jax.nn.softmax(chosen, axis=-1)
            flat_hits = hits.reshape(ROWS * TOP, EXPERTS)
            slot_pos = lax.optimization_barrier(jnp.sum((jnp.cumsum(flat_hits, 0) - flat_hits) * flat_hits, -1)).astype(jnp.int32)
            expert_ids = block_routes.reshape(-1).astype(jnp.int32)
            repeated = jnp.broadcast_to(block_rows[:, None, :], (ROWS, TOP, D)).reshape(ROWS * TOP, D)
            slots = jnp.zeros((EXPERTS, CAP, D), jnp.float32).at[expert_ids, slot_pos].set(repeated)
            slots = low_back(slots)
            gate_up = low_back(jnp.einsum('ecd,edf->ecf', slots, in_w, precision=exact))
            hidden_vals = low(jax.nn.silu(gate_up[..., :FF]) * gate_up[..., FF:])
            slots_out = low(low_back(jnp.einsum('ecf,efd->ecd', hidden_vals, out_w, precision=exact)))
            picked = slots_out[expert_ids, slot_pos].reshape(ROWS, TOP, D)
            return lax.optimization_barrier(jnp.sum(gates[..., None] * picked, 1))

        def one_sequence(inputs):
            seq_hidden, seq_teacher, seq_valid, seq_routes = inputs
            normed_attn = low(rms_norm(seq_hidden, gain_attn))
            query_lin = low_back(jnp.dot(normed_attn, query_w, precision=exact)).reshape(SEQ_LEN, HEADS, HEAD_DIM)
            key_lin = low_back(jnp.dot(normed_attn, key_w, precision=exact)).reshape(SEQ_LEN, KV_HEADS, HEAD_DIM)
            value_lin = low(low_back(jnp.dot(normed_attn, value_w, precision=exact))).reshape(SEQ_LEN, KV_HEADS, HEAD_DIM)
            cosine, sine_table = rope_tables(jnp.arange(SEQ_LEN, dtype=jnp.int32), HEAD_DIM // 2)
            queries = low(rotate(query_lin, cosine, sine_table))
            keys = low(rotate(key_lin, cosine, sine_table))
            attended = low(low_back(attend_sequence(queries, keys, value_lin)))
            branch = low_back(jnp.dot(attended, output_w, precision=exact))
            middle = seq_hidden + resid_mult * branch
            normed_ffn = low(rms_norm(middle, gain_ffn))
            mixture = jax.vmap(experts_block)(normed_ffn.reshape(N_SHARD, ROWS, D), seq_routes.reshape(N_SHARD, ROWS, TOP)).reshape(SEQ_LEN, D)
            result = middle + resid_mult * mixture
            deviation = result - seq_teacher
            return (result, jnp.sum(seq_valid[:, None] * deviation * deviation))
        results, parts = lax.map(jax.checkpoint(one_sequence), (hidden_f.reshape(seq_total, SEQ_LEN, D), teacher_f.reshape(seq_total, SEQ_LEN, D), valid_f.reshape(seq_total, SEQ_LEN), routes.reshape(seq_total, SEQ_LEN, TOP)))
        return (results.reshape(TOKENS, D), jnp.sum(parts) / (D * valid_count))
    (result, loss), pull = jax.vjp(forward, *floats)
    grads = pull((jnp.zeros_like(result), jnp.asarray(TOKENS * D / 4.0, dtype=jnp.float32)))
    return (result.astype(jnp.bfloat16), loss, grads[0], grads[1], grads[2], grads[3], grads[4], grads[5], grads[6], grads[7], grads[8], grads[9])
```

```python
import jax
import jax.numpy as jnp
from jax import lax
from jax.experimental import pallas as pl
from jax.experimental.pallas import tpu as pltpu
from jax.sharding import PartitionSpec as P

HEADS = 16
KV_HEADS = 8
HEAD_DIM = 64
TOP = 8
BLOCK = 256


norm_eps = 1e-06
resid_mult = 0.22
attn_mult = 0.015625
rope_base = 10000.0
very_low = -1e30


def rope_tables(positions, half_dim):
    frequency = rope_base ** (-jnp.arange(half_dim, dtype=jnp.float32) / half_dim)
    angles = positions.astype(jnp.float32)[:, None] * frequency[None, :]
    return (jnp.cos(angles), jnp.sin(angles))


def rotate(values, cosine, sine_table):
    half_dim = values.shape[-1] // 2
    first_half = values[..., :half_dim]
    second_half = values[..., half_dim:]
    cos_wide = cosine[:, None, :]
    sin_wide = sine_table[:, None, :]
    return jnp.concatenate(
        [
            first_half * cos_wide - second_half * sin_wide,
            second_half * cos_wide + first_half * sin_wide,
        ],
        -1,
    )


def rotate_back(grad_vals, cosine, sine_table):
    half_dim = grad_vals.shape[-1] // 2
    first_half = grad_vals[..., :half_dim]
    second_half = grad_vals[..., half_dim:]
    cos_wide = cosine[:, None, :]
    sin_wide = sine_table[:, None, :]
    return jnp.concatenate(
        [
            first_half * cos_wide + second_half * sin_wide,
            second_half * cos_wide - first_half * sin_wide,
        ],
        -1,
    )


def rms_scale(values):
    return lax.rsqrt(jnp.mean(values * values, axis=-1, keepdims=True) + norm_eps)


def norm_back(d_normed, values, scale_vals, gain_vec):
    scaled_grad = d_normed * gain_vec
    d_gain = jnp.sum(d_normed * values * scale_vals, 0)
    d_values = scale_vals * (
        scaled_grad
        - values * scale_vals * scale_vals * jnp.mean(scaled_grad * values, axis=-1, keepdims=True)
    )
    return (d_values, d_gain)


LANES = 128
ROW_STEP = 256


def row_chunks(count):
    step = min(count, ROW_STEP)
    return [pl.ds(at, step) for at in range(0, count, step)]


def pick_lane(values, lane):
    lanes = lax.broadcasted_iota(jnp.int32, values.shape, 1)
    return jnp.sum(jnp.where(lanes == lane, values, 0.0), axis=1, keepdims=True)


def dot_nn(left, right):
    return jnp.dot(left, right, preferred_element_type=jnp.float32)


def dot_nt(left, right):
    return lax.dot_general(left, right, (((1,), (1,)), ((), ())), preferred_element_type=jnp.float32)


def dot_tn(left, right):
    return lax.dot_general(left, right, (((0,), (0,)), ((), ())), preferred_element_type=jnp.float32)


def experts_forward_kernel(x_ref, gate_ref, in_ref, out_ref, mix_ref, gate_up_ref, hidden_ref, total):
    expert = pl.program_id(0)
    units = out_ref.shape[1]
    for rows in row_chunks(x_ref.shape[0]):
        gate_up = dot_nn(x_ref[rows, :], in_ref[0])
        gate_up_ref[0, rows, :] = gate_up
        gate_vals = gate_up[:, :units]
        silu_gate = gate_vals / (1.0 + jnp.exp(-gate_vals))
        weight = pick_lane(gate_ref[rows, :], expert)
        hidden = (silu_gate * gate_up[:, units:] * weight).astype(jnp.bfloat16)
        hidden_ref[0, rows, :] = hidden
        part = dot_nn(hidden, out_ref[0])

        @pl.when(expert == 0)
        def _():
            total[rows, :] = part

        @pl.when(expert > 0)
        def _():
            total[rows, :] += part

    @pl.when(expert == pl.num_programs(0) - 1)
    def _():
        mix_ref[...] = total[...].astype(mix_ref.dtype)


def experts_forward(tokens, gates_own, w_in, w_out):
    count, width = tokens.shape
    experts, units = w_out.shape[0], w_out.shape[1]
    return pl.pallas_call(
        experts_forward_kernel,
        grid=(experts,),
        in_specs=[
            pl.BlockSpec((count, width), lambda e: (0, 0)),
            pl.BlockSpec((count, LANES), lambda e: (0, 0)),
            pl.BlockSpec((1, width, 2 * units), lambda e: (e, 0, 0)),
            pl.BlockSpec((1, units, width), lambda e: (e, 0, 0)),
        ],
        out_specs=[
            pl.BlockSpec((count, width), lambda e: (0, 0)),
            pl.BlockSpec((1, count, 2 * units), lambda e: (e, 0, 0)),
            pl.BlockSpec((1, count, units), lambda e: (e, 0, 0)),
        ],
        out_shape=[
            jax.ShapeDtypeStruct((count, width), jnp.bfloat16),
            jax.ShapeDtypeStruct((experts, count, 2 * units), jnp.float32),
            jax.ShapeDtypeStruct((experts, count, units), jnp.bfloat16),
        ],
        scratch_shapes=[pltpu.VMEM((count, width), jnp.float32)],
        compiler_params=pltpu.CompilerParams(vmem_limit_bytes=VMEM_BYTES),
        cost_estimate=pl.CostEstimate(
            flops=6 * count * width * units * experts,
            bytes_accessed=experts * units * (6 * width + 10 * count) + 6 * count * width,
            transcendentals=experts * count * units,
        ),
        name="experts_forward",
    )(tokens, gates_own, w_in, w_out)


def experts_backward_kernel(
    dmix_ref, gate_ref, gate_up_ref, in_ref, out_ref, drows_ref, dgate_up_ref, dgates_ref, total
):
    expert = pl.program_id(0)
    units = out_ref.shape[1]
    lanes = lax.broadcasted_iota(jnp.int32, (1, LANES), 1)
    for rows in row_chunks(dmix_ref.shape[0]):
        pulled = dot_nt(dmix_ref[rows, :], out_ref[0])
        gate_vals = gate_up_ref[0, rows, :units]
        up_vals = gate_up_ref[0, rows, units:]
        sigmoid = 1.0 / (1.0 + jnp.exp(-gate_vals))
        silu_gate = gate_vals * sigmoid
        weight = pick_lane(gate_ref[rows, :], expert)
        own = jnp.sum(pulled * silu_gate * up_vals, axis=1, keepdims=True)
        own = jnp.where(lanes == expert, own, 0.0)
        d_hidden = pulled * weight
        d_gate = d_hidden * up_vals * sigmoid * (1.0 + gate_vals * (1.0 - sigmoid))
        d_up = d_hidden * silu_gate
        dgate_up_ref[0, rows, :units] = d_gate.astype(jnp.bfloat16)
        dgate_up_ref[0, rows, units:] = d_up.astype(jnp.bfloat16)
        part = dot_nt(dgate_up_ref[0, rows, :], in_ref[0])

        @pl.when(expert == 0)
        def _():
            total[rows, :] = part
            dgates_ref[rows, :] = own

        @pl.when(expert > 0)
        def _():
            total[rows, :] += part
            dgates_ref[rows, :] += own

    @pl.when(expert == pl.num_programs(0) - 1)
    def _():
        drows_ref[...] = total[...].astype(drows_ref.dtype)


def experts_backward(d_mix, gates_own, gate_up, w_in, w_out):
    count, width = d_mix.shape
    experts, units = w_out.shape[0], w_out.shape[1]
    return pl.pallas_call(
        experts_backward_kernel,
        grid=(experts,),
        in_specs=[
            pl.BlockSpec((count, width), lambda e: (0, 0)),
            pl.BlockSpec((count, LANES), lambda e: (0, 0)),
            pl.BlockSpec((1, count, 2 * units), lambda e: (e, 0, 0)),
            pl.BlockSpec((1, width, 2 * units), lambda e: (e, 0, 0)),
            pl.BlockSpec((1, units, width), lambda e: (e, 0, 0)),
        ],
        out_specs=[
            pl.BlockSpec((count, width), lambda e: (0, 0)),
            pl.BlockSpec((1, count, 2 * units), lambda e: (e, 0, 0)),
            pl.BlockSpec((count, LANES), lambda e: (0, 0)),
        ],
        out_shape=[
            jax.ShapeDtypeStruct((count, width), jnp.bfloat16),
            jax.ShapeDtypeStruct((experts, count, 2 * units), jnp.bfloat16),
            jax.ShapeDtypeStruct((count, LANES), jnp.float32),
        ],
        scratch_shapes=[pltpu.VMEM((count, width), jnp.float32)],
        compiler_params=pltpu.CompilerParams(vmem_limit_bytes=VMEM_BYTES),
        cost_estimate=pl.CostEstimate(
            flops=6 * count * width * units * experts,
            bytes_accessed=experts * units * (6 * width + 12 * count) + 4 * count * width,
            transcendentals=experts * count * units,
        ),
        name="experts_backward",
    )(d_mix, gates_own, gate_up, w_in, w_out)


def experts_grads_kernel(x_ref, dmix_ref, dgate_up_ref, hidden_ref, gin_ref, gout_ref):
    gin_ref[0] = dot_tn(x_ref[...], dgate_up_ref[0]).astype(gin_ref.dtype)
    gout_ref[0] = dot_tn(hidden_ref[0], dmix_ref[...]).astype(gout_ref.dtype)


def experts_grads(tokens, d_mix, dgate_up, hidden):
    count, width = tokens.shape
    experts, units = hidden.shape[0], hidden.shape[2]
    return pl.pallas_call(
        experts_grads_kernel,
        grid=(experts,),
        in_specs=[
            pl.BlockSpec((count, width), lambda e: (0, 0)),
            pl.BlockSpec((count, width), lambda e: (0, 0)),
            pl.BlockSpec((1, count, 2 * units), lambda e: (e, 0, 0)),
            pl.BlockSpec((1, count, units), lambda e: (e, 0, 0)),
        ],
        out_specs=[
            pl.BlockSpec((1, width, 2 * units), lambda e: (e, 0, 0)),
            pl.BlockSpec((1, units, width), lambda e: (e, 0, 0)),
        ],
        out_shape=[
            jax.ShapeDtypeStruct((experts, width, 2 * units), jnp.bfloat16),
            jax.ShapeDtypeStruct((experts, units, width), jnp.bfloat16),
        ],
        compiler_params=pltpu.CompilerParams(vmem_limit_bytes=VMEM_BYTES),
        cost_estimate=pl.CostEstimate(
            flops=6 * count * width * units * experts,
            bytes_accessed=experts * units * (6 * width + 6 * count) + 4 * count * width,
            transcendentals=0,
        ),
        name="experts_grads",
    )(tokens, d_mix, dgate_up, hidden)


VMEM_BYTES = 60 * 1024 * 1024


def body(
    hidden_in,
    valid_mask,
    teacher,
    routes,
    attn_norm,
    w_query,
    w_key,
    w_value,
    w_output,
    ffn_norm,
    router,
    w_in,
    w_out,
):
    row_count, model_width = hidden_in.shape
    shard_count = lax.axis_size("shard")
    seq_tokens = row_count * shard_count
    all_tokens = seq_tokens * lax.axis_size("rep")
    group_size = HEADS // KV_HEADS
    shard_at = lax.axis_index("shard")
    positions = shard_at * row_count + jnp.arange(row_count, dtype=jnp.int32)
    seq_positions = jnp.arange(seq_tokens, dtype=jnp.int32)
    cosine, sine_table = rope_tables(positions, HEAD_DIM // 2)
    cosine_all, sine_all = rope_tables(seq_positions, HEAD_DIM // 2)

    def gather(block):
        return lax.all_gather(block, "shard", axis=0, tiled=True)

    def scatter(block):
        return lax.psum_scatter(block, "shard", scatter_dimension=0, tiled=True)

    input_all = gather(hidden_in)
    valid_float = valid_mask.astype(jnp.float32)
    valid_count = lax.psum(jnp.sum(valid_float), ("rep", "shard"))
    small_full = gather(jnp.concatenate([attn_norm[:, None], ffn_norm[:, None], router], 1))
    gain_attn, gain_ffn, router_full = small_full[:, 0], small_full[:, 1], small_full[:, 2:]
    routes_all = gather(routes)
    kv_width = w_key.shape[1]
    weights_full = gather(jnp.concatenate([w_query, w_key, w_value], 1))
    query_width = w_query.shape[1]
    query_full = weights_full[:, :query_width]
    kv_full = weights_full[:, query_width:]
    output_full = gather(w_output)
    input_float = hidden_in.astype(jnp.float32)
    scale_attn = rms_scale(input_float)
    normed_attn = (input_float * scale_attn * gain_attn).astype(jnp.bfloat16)
    all_float = input_all.astype(jnp.float32)
    normed_all = (all_float * rms_scale(all_float) * gain_attn).astype(jnp.bfloat16)
    query_lin = dot_nn(normed_attn, query_full).reshape(row_count, HEADS, HEAD_DIM)
    kv_lin = dot_nn(normed_all, kv_full)
    keys_all = rotate(
        kv_lin[:, :kv_width].reshape(seq_tokens, KV_HEADS, HEAD_DIM), cosine_all, sine_all
    ).astype(jnp.bfloat16)
    values_all = kv_lin[:, kv_width:].astype(jnp.bfloat16)
    query_rows = rotate(query_lin, cosine, sine_table).astype(jnp.bfloat16)
    query_groups = query_rows.reshape(row_count, KV_HEADS, group_size, HEAD_DIM).transpose(
        1, 2, 0, 3
    )
    key_groups = keys_all.reshape(seq_tokens, KV_HEADS, HEAD_DIM).transpose(1, 0, 2)
    value_groups = values_all.reshape(seq_tokens, KV_HEADS, HEAD_DIM).transpose(1, 0, 2)
    allowed = (jnp.arange(seq_tokens, dtype=jnp.int32) // BLOCK)[None, :] <= (positions // BLOCK)[
        :, None
    ]

    def scores_of(query_part, key_part):
        score_vals = (
            jnp.einsum("hqd,kd->hqk", query_part, key_part, preferred_element_type=jnp.float32)
            * attn_mult
        )
        return jnp.where(allowed[None], score_vals, very_low)

    def forward_group(inputs):
        query_part, key_part, value_part = inputs
        score_vals = scores_of(query_part, key_part)
        row_max = jnp.max(score_vals, -1, keepdims=True)
        expo_vals = jnp.exp(score_vals - row_max)
        row_total = jnp.sum(expo_vals, -1, keepdims=True)
        prob_vals = (expo_vals / row_total).astype(jnp.bfloat16)
        attended_part = jnp.einsum(
            "hqk,kd->hqd", prob_vals, value_part, preferred_element_type=jnp.float32
        )
        return (attended_part, row_max[..., 0] + jnp.log(row_total[..., 0]))

    attended_groups, log_norm = lax.map(forward_group, (query_groups, key_groups, value_groups))
    attended = (
        attended_groups.transpose(2, 0, 1, 3)
        .reshape(row_count, HEADS * HEAD_DIM)
        .astype(jnp.bfloat16)
    )
    branch = dot_nn(attended, output_full)
    middle = input_float + resid_mult * branch
    scale_ffn = rms_scale(middle)
    normed_ffn = (middle * scale_ffn * gain_ffn).astype(jnp.bfloat16)
    own_experts = w_in.shape[0]
    expert_count = router_full.shape[1]
    expert_ids = jnp.arange(expert_count, dtype=jnp.int32)
    tokens_all = gather(normed_ffn)
    logits_all = dot_nn(tokens_all, router_full)
    chosen_all = jnp.any(routes_all[..., None] == expert_ids, 1)
    masked = jnp.where(chosen_all, logits_all, very_low)
    raised = jnp.where(chosen_all, jnp.exp(masked - jnp.max(masked, -1, keepdims=True)), 0.0)
    gates_all = raised / jnp.sum(raised, -1, keepdims=True)
    gates_own = lax.dynamic_slice_in_dim(gates_all, shard_at * own_experts, own_experts, 1)
    gates_own = jnp.pad(gates_own, ((0, 0), (0, LANES - own_experts)))
    gates = lax.dynamic_slice_in_dim(gates_all, shard_at * row_count, row_count, 0)
    mix_part, gate_up, hidden_gated = experts_forward(tokens_all, gates_own, w_in, w_out)
    mixture = scatter(mix_part).astype(jnp.float32)
    result_f = middle + resid_mult * mixture
    deviation = result_f - teacher.astype(jnp.float32)
    loss_sum = lax.psum(jnp.sum(valid_float[:, None] * deviation * deviation), ("rep", "shard"))
    loss = loss_sum / (model_width * valid_count)
    d_result = valid_float[:, None] * deviation * (all_tokens / (2.0 * valid_count))
    d_mix = (resid_mult * d_result).astype(jnp.bfloat16)
    d_mix_all = gather(d_mix)
    d_rows_part, d_gate_up, d_gates_own = experts_backward(
        d_mix_all, gates_own, gate_up, w_in, w_out
    )
    d_rows = scatter(d_rows_part).astype(jnp.float32)
    d_gates = lax.all_to_all(
        d_gates_own[:, :own_experts], "shard", split_axis=0, concat_axis=1, tiled=True
    )
    grad_in, grad_out = experts_grads(tokens_all, d_mix_all, d_gate_up, hidden_gated)
    d_logits = (gates * (d_gates - jnp.sum(gates * d_gates, -1, keepdims=True))).astype(
        jnp.bfloat16
    )
    d_normed_ffn = d_rows + dot_nt(d_logits, router_full)
    grad_router = dot_tn(normed_ffn, d_logits)
    d_norm_mid, grad_gain_ffn = norm_back(d_normed_ffn, middle, scale_ffn, gain_ffn)
    d_middle = d_result + d_norm_mid
    d_branch = (resid_mult * d_middle).astype(jnp.bfloat16)
    grad_output = jnp.dot(attended.T, d_branch, preferred_element_type=jnp.float32)
    d_attended = dot_nt(d_branch, output_full).astype(
        jnp.bfloat16
    )
    d_att_groups = d_attended.reshape(row_count, KV_HEADS, group_size, HEAD_DIM).transpose(
        1, 2, 0, 3
    )

    def backward_group(inputs):
        query_part, key_part, value_part, norm_part, grad_part = inputs
        score_vals = scores_of(query_part, key_part)
        prob_vals = jnp.exp(score_vals - norm_part[..., None])
        d_probs = jnp.einsum(
            "hqd,kd->hqk", grad_part, value_part, preferred_element_type=jnp.float32
        )
        d_scores = (prob_vals * (d_probs - jnp.sum(prob_vals * d_probs, -1, keepdims=True))).astype(
            jnp.bfloat16
        )
        query_term = (
            jnp.einsum("hqk,kd->hqd", d_scores, key_part, preferred_element_type=jnp.float32)
            * attn_mult
        )
        key_term = (
            jnp.einsum("hqk,hqd->kd", d_scores, query_part, preferred_element_type=jnp.float32)
            * attn_mult
        )
        value_term = jnp.einsum(
            "hqk,hqd->kd",
            prob_vals.astype(jnp.bfloat16),
            grad_part,
            preferred_element_type=jnp.float32,
        )
        return (query_term, jnp.concatenate([key_term, value_term], -1))

    d_query_groups, key_value_terms = lax.map(
        backward_group, (query_groups, key_groups, value_groups, log_norm, d_att_groups)
    )
    kv_terms = key_value_terms.transpose(1, 0, 2).reshape(seq_tokens, KV_HEADS, 2, HEAD_DIM)
    kv_owned = scatter(kv_terms.transpose(0, 2, 1, 3).reshape(seq_tokens, -1).astype(jnp.bfloat16))
    kv_owned = kv_owned.astype(jnp.float32)
    key_grad_rows = (
        rotate_back(
            kv_owned[:, :kv_width].reshape(row_count, KV_HEADS, HEAD_DIM), cosine, sine_table
        )
        .reshape(row_count, kv_width)
        .astype(jnp.bfloat16)
    )
    value_grad_rows = kv_owned[:, kv_width:].astype(jnp.bfloat16)
    query_grad_rows = (
        rotate_back(
            d_query_groups.transpose(2, 0, 1, 3).reshape(row_count, HEADS, HEAD_DIM),
            cosine,
            sine_table,
        )
        .reshape(row_count, HEADS * HEAD_DIM)
        .astype(jnp.bfloat16)
    )
    d_linear = jnp.concatenate([query_grad_rows, key_grad_rows, value_grad_rows], 1)
    grad_linear = dot_tn(normed_attn, d_linear)
    d_normed_attn = dot_nt(d_linear, weights_full)
    d_norm_in, grad_gain_attn = norm_back(d_normed_attn, input_float, scale_attn, gain_attn)
    d_input = d_middle + d_norm_in
    own_weights = scatter(jnp.concatenate([grad_linear, grad_output], 1).astype(jnp.bfloat16))
    own_small = scatter(
        jnp.concatenate([grad_gain_attn[:, None], grad_gain_ffn[:, None], grad_router], 1)
    )
    sum_in, sum_out, sum_weights, sum_small = lax.psum(
        (grad_in, grad_out, own_weights, own_small), "rep"
    )
    sum_weights = sum_weights.astype(jnp.float32)
    return (
        result_f.astype(jnp.bfloat16),
        loss,
        d_input,
        sum_small[:, 0],
        sum_weights[:, :query_width],
        sum_weights[:, query_width : query_width + kv_width],
        sum_weights[:, query_width + kv_width : query_width + 2 * kv_width],
        sum_weights[:, query_width + 2 * kv_width :],
        sum_small[:, 1],
        sum_small[:, 2:],
        sum_in.astype(jnp.float32),
        sum_out.astype(jnp.float32),
    )


def solution(mesh):
    in_specs = (
        P(("rep", "shard"), None),
        P(("rep", "shard")),
        P(("rep", "shard"), None),
        P(("rep", "shard"), None),
        P("shard"),
        P("shard", None),
        P("shard", None),
        P("shard", None),
        P("shard", None),
        P("shard"),
        P("shard", None),
        P("shard", None, None),
        P("shard", None, None),
    )
    out_specs = (
        P(("rep", "shard"), None),
        P(),
        P(("rep", "shard"), None),
        P("shard"),
        P("shard", None),
        P("shard", None),
        P("shard", None),
        P("shard", None),
        P("shard"),
        P("shard", None),
        P("shard", None, None),
        P("shard", None, None),
    )
    return jax.shard_map(body, mesh=mesh, in_specs=in_specs, out_specs=out_specs, check_vma=False)
```

```python
import jax
import jax.numpy as jnp
from jax import lax
from jax.experimental import pallas as pl
from jax.experimental.pallas import tpu as pltpu
from jax.sharding import PartitionSpec as P

HEADS = 16
KV_HEADS = 8
HEAD_DIM = 64
TOP = 8
BLOCK = 256


norm_eps = 1e-06
resid_mult = 0.22
attn_mult = 0.015625
rope_base = 10000.0
very_low = -1e30


def rope_tables(positions):
    half_dim = HEAD_DIM // 2
    frequency = rope_base ** (-jnp.arange(half_dim, dtype=jnp.float32) / half_dim)
    angles = positions.astype(jnp.float32)[:, None] * frequency[None, :]
    cosine, sine = jnp.cos(angles), jnp.sin(angles)
    return (
        jnp.concatenate([cosine] * 4, 1),
        jnp.concatenate([-sine, sine, -sine, sine], 1),
    )


def rms_scale(values):
    return lax.rsqrt(jnp.mean(values * values, axis=-1, keepdims=True) + norm_eps)


def norm_back(d_normed, values, scale_vals, gain_vec):
    scaled_grad = d_normed * gain_vec
    d_gain = jnp.sum(d_normed * values * scale_vals, 0)
    d_values = scale_vals * (
        scaled_grad
        - values * scale_vals * scale_vals * jnp.mean(scaled_grad * values, axis=-1, keepdims=True)
    )
    return (d_values, d_gain)


LANES = 128
ROW_STEP = 256


def row_chunks(count):
    step = min(count, ROW_STEP)
    return [pl.ds(at, step) for at in range(0, count, step)]


def pick_lane(values, lane):
    lanes = lax.broadcasted_iota(jnp.int32, values.shape, 1)
    return jnp.sum(jnp.where(lanes == lane, values, 0.0), axis=1, keepdims=True)


def dot_nn(left, right):
    return jnp.dot(left, right, preferred_element_type=jnp.float32)


def dot_nt(left, right):
    return lax.dot_general(left, right, (((1,), (1,)), ((), ())), preferred_element_type=jnp.float32)


def dot_tn(left, right):
    return lax.dot_general(left, right, (((0,), (0,)), ((), ())), preferred_element_type=jnp.float32)


def experts_forward_kernel(x_ref, gate_ref, in_ref, out_ref, mix_ref, gate_up_ref, hidden_ref, total):
    expert = pl.program_id(0)
    units = out_ref.shape[1]
    for rows in row_chunks(x_ref.shape[0]):
        gate_up = dot_nn(x_ref[rows, :], in_ref[0])
        gate_up_ref[0, rows, :] = gate_up
        gate_vals = gate_up[:, :units]
        silu_gate = gate_vals / (1.0 + jnp.exp(-gate_vals))
        weight = pick_lane(gate_ref[rows, :], expert)
        hidden = (silu_gate * gate_up[:, units:] * weight).astype(jnp.bfloat16)
        hidden_ref[0, rows, :] = hidden
        part = dot_nn(hidden, out_ref[0])

        @pl.when(expert == 0)
        def _():
            total[rows, :] = part

        @pl.when(expert > 0)
        def _():
            total[rows, :] += part

    @pl.when(expert == pl.num_programs(0) - 1)
    def _():
        mix_ref[...] = total[...].astype(mix_ref.dtype)


def experts_forward(tokens, gates_own, w_in, w_out):
    count, width = tokens.shape
    experts, units = w_out.shape[0], w_out.shape[1]
    return pl.pallas_call(
        experts_forward_kernel,
        grid=(experts,),
        in_specs=[
            pl.BlockSpec((count, width), lambda e: (0, 0)),
            pl.BlockSpec((count, LANES), lambda e: (0, 0)),
            pl.BlockSpec((1, width, 2 * units), lambda e: (e, 0, 0)),
            pl.BlockSpec((1, units, width), lambda e: (e, 0, 0)),
        ],
        out_specs=[
            pl.BlockSpec((count, width), lambda e: (0, 0)),
            pl.BlockSpec((1, count, 2 * units), lambda e: (e, 0, 0)),
            pl.BlockSpec((1, count, units), lambda e: (e, 0, 0)),
        ],
        out_shape=[
            jax.ShapeDtypeStruct((count, width), jnp.bfloat16),
            jax.ShapeDtypeStruct((experts, count, 2 * units), jnp.float32),
            jax.ShapeDtypeStruct((experts, count, units), jnp.bfloat16),
        ],
        scratch_shapes=[pltpu.VMEM((count, width), jnp.float32)],
        compiler_params=pltpu.CompilerParams(vmem_limit_bytes=VMEM_BYTES),
        cost_estimate=pl.CostEstimate(
            flops=6 * count * width * units * experts,
            bytes_accessed=experts * units * (6 * width + 10 * count) + 6 * count * width,
            transcendentals=experts * count * units,
        ),
        name="experts_forward",
    )(tokens, gates_own, w_in, w_out)


def experts_backward_kernel(
    dmix_ref, gate_ref, gate_up_ref, in_ref, out_ref, drows_ref, dgate_up_ref, dgates_ref, total
):
    expert = pl.program_id(0)
    units = out_ref.shape[1]
    lanes = lax.broadcasted_iota(jnp.int32, (1, LANES), 1)
    for rows in row_chunks(dmix_ref.shape[0]):
        pulled = dot_nt(dmix_ref[rows, :], out_ref[0])
        gate_vals = gate_up_ref[0, rows, :units]
        up_vals = gate_up_ref[0, rows, units:]
        sigmoid = 1.0 / (1.0 + jnp.exp(-gate_vals))
        silu_gate = gate_vals * sigmoid
        weight = pick_lane(gate_ref[rows, :], expert)
        own = jnp.sum(pulled * silu_gate * up_vals, axis=1, keepdims=True)
        own = jnp.where(lanes == expert, own, 0.0)
        d_hidden = pulled * weight
        d_gate = d_hidden * up_vals * sigmoid * (1.0 + gate_vals * (1.0 - sigmoid))
        d_up = d_hidden * silu_gate
        dgate_up_ref[0, rows, :units] = d_gate.astype(jnp.bfloat16)
        dgate_up_ref[0, rows, units:] = d_up.astype(jnp.bfloat16)
        part = dot_nt(dgate_up_ref[0, rows, :], in_ref[0])

        @pl.when(expert == 0)
        def _():
            total[rows, :] = part
            dgates_ref[rows, :] = own

        @pl.when(expert > 0)
        def _():
            total[rows, :] += part
            dgates_ref[rows, :] += own

    @pl.when(expert == pl.num_programs(0) - 1)
    def _():
        drows_ref[...] = total[...].astype(drows_ref.dtype)


def experts_backward(d_mix, gates_own, gate_up, w_in, w_out):
    count, width = d_mix.shape
    experts, units = w_out.shape[0], w_out.shape[1]
    return pl.pallas_call(
        experts_backward_kernel,
        grid=(experts,),
        in_specs=[
            pl.BlockSpec((count, width), lambda e: (0, 0)),
            pl.BlockSpec((count, LANES), lambda e: (0, 0)),
            pl.BlockSpec((1, count, 2 * units), lambda e: (e, 0, 0)),
            pl.BlockSpec((1, width, 2 * units), lambda e: (e, 0, 0)),
            pl.BlockSpec((1, units, width), lambda e: (e, 0, 0)),
        ],
        out_specs=[
            pl.BlockSpec((count, width), lambda e: (0, 0)),
            pl.BlockSpec((1, count, 2 * units), lambda e: (e, 0, 0)),
            pl.BlockSpec((count, LANES), lambda e: (0, 0)),
        ],
        out_shape=[
            jax.ShapeDtypeStruct((count, width), jnp.bfloat16),
            jax.ShapeDtypeStruct((experts, count, 2 * units), jnp.bfloat16),
            jax.ShapeDtypeStruct((count, LANES), jnp.float32),
        ],
        scratch_shapes=[pltpu.VMEM((count, width), jnp.float32)],
        compiler_params=pltpu.CompilerParams(vmem_limit_bytes=VMEM_BYTES),
        cost_estimate=pl.CostEstimate(
            flops=6 * count * width * units * experts,
            bytes_accessed=experts * units * (6 * width + 12 * count) + 4 * count * width,
            transcendentals=experts * count * units,
        ),
        name="experts_backward",
    )(d_mix, gates_own, gate_up, w_in, w_out)


def experts_grads_kernel(order_ref, x_ref, dmix_ref, dgate_up_ref, hidden_ref, grads_ref):
    width = x_ref.shape[1]
    grads_ref[0, :width, :] = dot_tn(x_ref[...], dgate_up_ref[0]).astype(grads_ref.dtype)
    grads_ref[0, width:, :] = dot_tn(hidden_ref[0], dmix_ref[...]).astype(grads_ref.dtype)


def experts_grads(order, tokens, d_mix, dgate_up, hidden):
    count, width = tokens.shape
    units = hidden.shape[2]
    experts = order.shape[0]
    return pl.pallas_call(
        experts_grads_kernel,
        grid_spec=pltpu.PrefetchScalarGridSpec(
            num_scalar_prefetch=1,
            grid=(experts,),
            in_specs=[
                pl.BlockSpec((count, width), lambda e, order: (0, 0)),
                pl.BlockSpec((count, width), lambda e, order: (0, 0)),
                pl.BlockSpec((1, count, 2 * units), lambda e, order: (order[e], 0, 0)),
                pl.BlockSpec((1, count, units), lambda e, order: (order[e], 0, 0)),
            ],
            out_specs=pl.BlockSpec((1, width + units, 2 * units), lambda e, order: (e, 0, 0)),
        ),
        out_shape=jax.ShapeDtypeStruct((experts, width + units, 2 * units), jnp.bfloat16),
        compiler_params=pltpu.CompilerParams(vmem_limit_bytes=VMEM_BYTES),
        cost_estimate=pl.CostEstimate(
            flops=6 * count * width * units * experts,
            bytes_accessed=experts * units * (6 * width + 6 * count) + 4 * count * width,
            transcendentals=0,
        ),
        name="experts_grads",
    )(order, tokens, d_mix, dgate_up, hidden)


def widen_kernel(base_ref, piece_ref, *refs):
    gin_ref, gout_ref = refs[-2:]
    width = gin_ref.shape[1]
    gin_ref[...] = piece_ref[:, :width, :].astype(jnp.float32)
    gout_ref[...] = piece_ref[:, width:, :].astype(jnp.float32)


def widen(base, piece, width, total, held):
    count, rows, columns = piece.shape
    shapes = [
        jax.ShapeDtypeStruct((total, width, columns), jnp.float32),
        jax.ShapeDtypeStruct((total, rows - width, columns), jnp.float32),
    ]
    return pl.pallas_call(
        widen_kernel,
        grid_spec=pltpu.PrefetchScalarGridSpec(
            num_scalar_prefetch=1,
            grid=(count,),
            in_specs=[pl.BlockSpec((1, rows, columns), lambda e, base: (e, 0, 0))]
            + [pl.BlockSpec(memory_space=pl.ANY)] * len(held),
            out_specs=[
                pl.BlockSpec((1, width, columns), lambda e, base: (base[0] + e, 0, 0)),
                pl.BlockSpec((1, rows - width, columns), lambda e, base: (base[0] + e, 0, 0)),
            ],
        ),
        out_shape=shapes,
        input_output_aliases={2 + at: at for at in range(len(held))},
        compiler_params=pltpu.CompilerParams(vmem_limit_bytes=VMEM_BYTES),
        cost_estimate=pl.CostEstimate(flops=0, bytes_accessed=6 * piece.size, transcendentals=0),
        name="widen",
    )(base, piece, *held)


def attention_grads_kernel(
    normed_ref, dquery_ref, all_ref, dkv_ref, attended_ref, dbranch_ref, small_ref, first_ref, second_ref
):
    query_width = dquery_ref.shape[1]
    half = dbranch_ref.shape[1] // 2
    kv_width = dkv_ref.shape[1]
    low = jnp.bfloat16
    second_ref[:, :kv_width] = dot_tn(all_ref[...], dkv_ref[...]).astype(low)
    first_ref[:, :query_width] = dot_tn(normed_ref[...], dquery_ref[...]).astype(low)
    grad_output = dot_tn(attended_ref[...], dbranch_ref[...]).astype(low)
    first_ref[:, query_width : query_width + half] = grad_output[:, :half]
    second_ref[:, kv_width:] = grad_output[:, half:]
    first_ref[:, query_width + half :] = small_ref[...].astype(low)


def attention_grads(normed, d_query, normed_all, d_kv, attended, d_branch, small):
    width = normed.shape[1]
    half = d_branch.shape[1] // 2
    return pl.pallas_call(
        attention_grads_kernel,
        in_specs=[whole_spec()] * 7,
        out_specs=[whole_spec()] * 2,
        out_shape=[
            jax.ShapeDtypeStruct((width, d_query.shape[1] + half + LANES), jnp.bfloat16),
            jax.ShapeDtypeStruct((width, d_kv.shape[1] + half), jnp.bfloat16),
        ],
        compiler_params=pltpu.CompilerParams(vmem_limit_bytes=VMEM_BYTES),
        cost_estimate=pl.CostEstimate(
            flops=2 * width * width * (normed_all.shape[0] + 2 * normed.shape[0]),
            bytes_accessed=14 * width * width,
            transcendentals=0,
        ),
        name="attention_grads",
    )(normed, d_query, normed_all, d_kv, attended, d_branch, small)


VMEM_BYTES = 60 * 1024 * 1024


def swap_halves(values):
    lanes = lax.broadcasted_iota(jnp.int32, values.shape, 1)
    ahead = pltpu.roll(values, LANES - HEAD_DIM // 2, 1)
    behind = pltpu.roll(values, HEAD_DIM // 2, 1)
    return jnp.where(lanes % HEAD_DIM < HEAD_DIM // 2, ahead, behind)


def stack_heads(block, parity):
    values = block.astype(jnp.float32)
    lanes = lax.broadcasted_iota(jnp.int32, values.shape, 1)
    low = jnp.where(lanes < HEAD_DIM, values, 0.0)
    high = values - low
    if parity == 0:
        high = pltpu.roll(high, HEAD_DIM, 1)
    else:
        low = pltpu.roll(low, HEAD_DIM, 1)
    return jnp.concatenate([low, high], 0).astype(jnp.bfloat16)


def unstack_heads(stacked, parity):
    rows = stacked.shape[0] // 2
    low, high = stacked[:rows], stacked[rows:]
    if parity == 0:
        high = pltpu.roll(high, HEAD_DIM, 1)
    else:
        low = pltpu.roll(low, HEAD_DIM, 1)
    lanes = lax.broadcasted_iota(jnp.int32, low.shape, 1)
    return jnp.where(lanes < HEAD_DIM, low, high)


def lane_block(at):
    return pl.ds(pl.multiple_of(at * LANES, LANES), LANES)


def attention_forward_kernel(
    bias_ref, all_ref, own_ref, gain_ref, wq_ref, wkv_ref, cos_ref, sin_ref, cos_own_ref, sin_own_ref,
    normed_ref, query_ref, key_ref, value_ref, attended_ref, norm_ref, scores
):
    tokens, width = all_ref.shape
    kv_width = key_ref.shape[1]
    key_rows = tokens // bias_ref.shape[0]

    def normed_rows(block):
        values = block.astype(jnp.float32)
        scale = lax.rsqrt(jnp.mean(values * values, axis=-1, keepdims=True) + norm_eps)
        return (values * scale * gain_ref[...]).astype(jnp.bfloat16)

    def project(at, carry):
        rows = pl.ds(pl.multiple_of(at * ROW_STEP, ROW_STEP), ROW_STEP)
        normed = normed_rows(all_ref[rows, :])
        normed_ref[rows, :] = normed
        linear = dot_nn(normed, wkv_ref[...])
        for col in range(0, kv_width, LANES):
            part = linear[:, col : col + LANES]
            turned = part * cos_ref[rows, :] + swap_halves(part) * sin_ref[rows, :]
            key_ref[rows, col : col + LANES] = turned.astype(jnp.bfloat16)
        value_ref[rows, :] = linear[:, kv_width:].astype(jnp.bfloat16)
        return carry

    lax.fori_loop(0, tokens // ROW_STEP, project, 0)
    linear = dot_nn(normed_rows(own_ref[...]), wq_ref[...])
    for col in range(0, wq_ref.shape[1], LANES):
        part = linear[:, col : col + LANES]
        turned = part * cos_own_ref[...] + swap_halves(part) * sin_own_ref[...]
        query_ref[:, col : col + LANES] = (turned.astype(jnp.bfloat16).astype(jnp.float32) * attn_mult).astype(jnp.bfloat16)

    def attend(pair, carry):
        lanes = lane_block(pair)
        turned_values = value_ref[:, lanes].astype(jnp.float32).T.astype(jnp.bfloat16)
        for parity in range(2):
            group = 2 * pair + parity
            stacked = stack_heads(query_ref[:, lane_block(group)], parity)
            top = None
            for at in range(bias_ref.shape[0]):
                rows = pl.ds(at * key_rows, key_rows)
                part = dot_nt(key_ref[rows, lanes], stacked) + bias_ref[at]
                scores[rows, :] = part
                high = jnp.max(part, axis=0, keepdims=True)
                top = high if top is None else jnp.maximum(top, high)
            total, gathered = None, None
            for at in range(bias_ref.shape[0]):
                rows = pl.ds(at * key_rows, key_rows)
                raised = jnp.exp(scores[rows, :] - top)
                part = jnp.sum(raised, axis=0, keepdims=True)
                mixed = dot_nn(
                    turned_values[:, at * key_rows : (at + 1) * key_rows], raised.astype(jnp.bfloat16)
                )
                total = part if total is None else total + part
                gathered = mixed if gathered is None else gathered + mixed
            gathered = (gathered / total).T
            attended_ref[:, lane_block(group)] = unstack_heads(gathered, parity).astype(jnp.bfloat16)
            norm_ref[pl.ds(group, 1), :] = top + jnp.log(total)
        return carry

    lax.fori_loop(0, kv_width // LANES, attend, 0)


def whole_spec():
    return pl.BlockSpec(memory_space=pltpu.VMEM)


def attention_forward(bias, input_all, hidden_in, gain, w_query, w_kv, tables, tables_own):
    tokens, width = input_all.shape
    rows = hidden_in.shape[0]
    kv_width = w_kv.shape[1] // 2
    return pl.pallas_call(
        attention_forward_kernel,
        in_specs=[pl.BlockSpec(memory_space=pltpu.SMEM)] + [whole_spec()] * 9,
        out_specs=[whole_spec()] * 6,
        out_shape=[
            jax.ShapeDtypeStruct((tokens, width), jnp.bfloat16),
            jax.ShapeDtypeStruct((rows, w_query.shape[1]), jnp.bfloat16),
            jax.ShapeDtypeStruct((tokens, kv_width), jnp.bfloat16),
            jax.ShapeDtypeStruct((tokens, kv_width), jnp.bfloat16),
            jax.ShapeDtypeStruct((rows, w_query.shape[1]), jnp.bfloat16),
            jax.ShapeDtypeStruct((KV_HEADS, 2 * rows), jnp.float32),
        ],
        scratch_shapes=[pltpu.VMEM((tokens, 2 * rows), jnp.float32)],
        compiler_params=pltpu.CompilerParams(vmem_limit_bytes=VMEM_BYTES),
        cost_estimate=pl.CostEstimate(
            flops=2 * (tokens * width * 2 * kv_width + rows * width * width + 4 * rows * tokens * width),
            bytes_accessed=16 * tokens * width,
            transcendentals=rows * tokens * HEADS,
        ),
        name="attention_forward",
    )(bias, input_all, hidden_in, gain, w_query, w_kv, *tables, *tables_own)


def attention_backward_kernel(
    bias_ref, query_ref, key_ref, value_ref, norm_ref, grad_ref, cos_ref, sin_ref, cos_own_ref, sin_own_ref,
    dquery_ref, dkv_ref, probs, dprobs, dkeys, dvalues
):
    tokens, kv_width = key_ref.shape
    key_rows = tokens // bias_ref.shape[0]

    def pull(pair, carry):
        lanes = lane_block(pair)
        turned_keys = key_ref[:, lanes].astype(jnp.float32).T.astype(jnp.bfloat16)
        for parity in range(2):
            group = 2 * pair + parity
            stacked = stack_heads(query_ref[:, lane_block(group)], parity)
            stacked_grad = stack_heads(grad_ref[:, lane_block(group)], parity)
            log_norm = norm_ref[pl.ds(group, 1), :]
            total = None
            for at in range(bias_ref.shape[0]):
                rows = pl.ds(at * key_rows, key_rows)
                part = dot_nt(key_ref[rows, lanes], stacked) + bias_ref[at]
                prob = jnp.exp(part - log_norm)
                d_prob = dot_nt(value_ref[rows, lanes], stacked_grad)
                probs[rows, :] = prob
                dprobs[rows, :] = d_prob
                d_value = dot_nn(prob.astype(jnp.bfloat16), stacked_grad)
                dvalues[rows, :] = d_value if parity == 0 else dvalues[rows, :] + d_value
                weighted = jnp.sum(prob * d_prob, axis=0, keepdims=True)
                total = weighted if total is None else total + weighted
            d_query = None
            for at in range(bias_ref.shape[0]):
                rows = pl.ds(at * key_rows, key_rows)
                d_score = (probs[rows, :] * (dprobs[rows, :] - total)).astype(jnp.bfloat16)
                d_key = dot_nn(d_score, stacked)
                dkeys[rows, :] = d_key if parity == 0 else dkeys[rows, :] + d_key
                part = dot_nn(turned_keys[:, at * key_rows : (at + 1) * key_rows], d_score)
                d_query = part if d_query is None else d_query + part
            part = unstack_heads(d_query.T, parity) * attn_mult
            turned = part * cos_own_ref[...] - swap_halves(part) * sin_own_ref[...]
            dquery_ref[:, lane_block(group)] = turned.astype(jnp.bfloat16)
        part = dkeys[...]
        turned = part * cos_ref[...] - swap_halves(part) * sin_ref[...]
        dkv_ref[:, lanes] = turned.astype(jnp.bfloat16)
        dkv_ref[:, lane_block(pair + kv_width // LANES)] = dvalues[...].astype(jnp.bfloat16)
        return carry

    lax.fori_loop(0, kv_width // LANES, pull, 0)


def attention_backward(bias, query, key, value, log_norm, grad, tables, tables_own):
    tokens, kv_width = key.shape
    rows, width = query.shape
    return pl.pallas_call(
        attention_backward_kernel,
        in_specs=[pl.BlockSpec(memory_space=pltpu.SMEM)] + [whole_spec()] * 9,
        out_specs=[whole_spec()] * 2,
        out_shape=[
            jax.ShapeDtypeStruct((rows, width), jnp.bfloat16),
            jax.ShapeDtypeStruct((tokens, 2 * kv_width), jnp.bfloat16),
        ],
        scratch_shapes=[
            pltpu.VMEM((tokens, 2 * rows), jnp.float32),
            pltpu.VMEM((tokens, 2 * rows), jnp.float32),
            pltpu.VMEM((tokens, LANES), jnp.float32),
            pltpu.VMEM((tokens, LANES), jnp.float32),
        ],
        compiler_params=pltpu.CompilerParams(vmem_limit_bytes=VMEM_BYTES),
        cost_estimate=pl.CostEstimate(
            flops=20 * rows * tokens * width,
            bytes_accessed=8 * tokens * width,
            transcendentals=rows * tokens * HEADS,
        ),
        name="attention_backward",
    )(bias, query, key, value, log_norm, grad, *tables, *tables_own)


def exchange(block, bit):
    count = lax.axis_size("rep")
    return lax.ppermute(block, "rep", [(at, at ^ bit) for at in range(count)])


def side_of(bit):
    return (lax.axis_index("rep") // bit) % 2


def add_pair(left, right):
    return (left.astype(jnp.float32) + right.astype(jnp.float32)).astype(jnp.bfloat16)


def after(value, *others):
    return lax.optimization_barrier((value, *others))[0]


def piece_at(parts, start, size, axis):
    pieces = [lax.dynamic_slice_in_dim(part, start, size, axis) for part in parts]
    if len(pieces) == 1:
        return pieces[0]
    return add_pair(*pieces)


def halve(parts, bit, axis, offset=0, length=None):
    length = parts[0].shape[axis] if length is None else length
    half = length // 2
    side = side_of(bit)
    sent = piece_at(parts, offset + (1 - side) * half, half, axis)
    kept = piece_at(parts, offset + side * half, half, axis)
    return sent, [kept, exchange(sent, bit)]


def double(block, bit, axis):
    size = block.shape[axis]
    side = side_of(bit)
    held = lax.concatenate([block, block], axis)
    return lax.dynamic_update_slice_in_dim(held, exchange(block, bit), (1 - side) * size, axis)


def rep_bits():
    count = lax.axis_size("rep")
    return [1 << at for at in range(count.bit_length() - 1)]


def body(
    hidden_in,
    valid_mask,
    teacher,
    routes,
    attn_norm,
    w_query,
    w_key,
    w_value,
    w_output,
    ffn_norm,
    router,
    w_in,
    w_out,
):
    row_count, model_width = hidden_in.shape
    shard_count = lax.axis_size("shard")
    seq_tokens = row_count * shard_count
    all_tokens = seq_tokens * lax.axis_size("rep")
    shard_at = lax.axis_index("shard")
    tables = rope_tables(jnp.arange(seq_tokens, dtype=jnp.int32))
    tables_own = tuple(
        lax.dynamic_slice_in_dim(table, shard_at * row_count, row_count, 0) for table in tables
    )
    key_blocks = jnp.arange(seq_tokens // BLOCK, dtype=jnp.int32)
    bias = jnp.where(key_blocks <= shard_at * row_count // BLOCK, 0.0, very_low)
    bits = rep_bits()
    near, far = bits[0], bits[1:]

    def gather(block):
        return lax.all_gather(block, "shard", axis=0, tiled=True)

    def scatter(block):
        return lax.psum_scatter(block, "shard", scatter_dimension=0, tiled=True)

    def gather_pair(left, right):
        width = left.shape[1]
        flat = gather(jnp.concatenate([left.reshape(1, -1), right.reshape(1, -1)], 1))
        split = left.size
        return flat[:, :split].reshape(-1, width), flat[:, split:].reshape(-1, right.shape[1])

    kv_width = w_key.shape[1]
    query_width = w_query.shape[1]
    half_width = w_output.shape[1] // 2
    own_rows = w_query.shape[0]
    piece_rows = own_rows // lax.axis_size("rep")

    def piece_of(block, order):
        index = 0
        for at, bit in enumerate(order):
            index = index + side_of(bit) * (1 << at)
        return lax.dynamic_slice_in_dim(block, index * piece_rows, piece_rows, 0)

    order_first, order_second = far + [near], far[::-1] + [near]
    w_kv = jnp.concatenate([w_key, w_value], 1)
    input_all = gather(hidden_in)
    pieces = lax.all_gather(
        jnp.concatenate([piece_of(w_query, order_first), piece_of(w_kv, order_second)], 1),
        "shard",
        axis=0,
    )
    query_full = pieces[..., :query_width]
    kv_full = pieces[..., query_width:]
    for bit_first, bit_second in zip(order_first, order_second):
        query_full = double(query_full, bit_first, 1)
        kv_full = double(kv_full, bit_second, 1)
    query_full = query_full.reshape(own_rows * shard_count, query_width)
    kv_full = kv_full.reshape(own_rows * shard_count, 2 * kv_width)
    near_rows = own_rows // 2
    output_half = lax.dynamic_slice_in_dim(w_output, side_of(near) * near_rows, near_rows, 0)
    output_half = lax.all_gather(after(output_half, input_all), "shard", axis=0)
    expert_count = router.shape[1]
    small_parts = [attn_norm[:, None], ffn_norm[:, None], router]
    small_full, routes_all = gather_pair(
        jnp.concatenate(small_parts, 1), routes.astype(jnp.bfloat16)
    )
    gain_attn, gain_ffn = small_full[:, 0], small_full[:, 1]
    router_full = small_full[:, 2:]
    gain_attn = gain_attn.astype(jnp.float32)
    valid_float = valid_mask.astype(jnp.float32)
    input_float = hidden_in.astype(jnp.float32)
    scale_attn = rms_scale(input_float)
    all_float = input_all.astype(jnp.float32)
    normed_all, query_rows, keys_all, values_all, attended, log_norm = attention_forward(
        bias, input_all, hidden_in, gain_attn[None], query_full, kv_full, tables, tables_own
    )
    normed_attn = lax.dynamic_slice_in_dim(normed_all, shard_at * row_count, row_count, 0)
    output_half, attended = lax.optimization_barrier((output_half, attended))
    output_full = double(output_half, near, 1).reshape(own_rows * shard_count, -1)
    branch = dot_nn(attended, output_full)
    middle = input_float + resid_mult * branch
    scale_ffn = rms_scale(middle)
    normed_ffn = (middle * scale_ffn * gain_ffn).astype(jnp.bfloat16)
    own_experts = w_in.shape[0]
    expert_ids = jnp.arange(expert_count, dtype=jnp.bfloat16)
    valid_count = lax.psum(jnp.sum(after(valid_float, normed_ffn)), ("rep", "shard"))
    tokens_all = gather(normed_ffn)
    logits_all = dot_nn(tokens_all, router_full)
    chosen_all = jnp.any(routes_all[..., None] == expert_ids, 1)
    masked = jnp.where(chosen_all, logits_all, very_low)
    raised = jnp.where(chosen_all, jnp.exp(masked - jnp.max(masked, -1, keepdims=True)), 0.0)
    gates_all = raised / jnp.sum(raised, -1, keepdims=True)
    gates_own = lax.dynamic_slice_in_dim(gates_all, shard_at * own_experts, own_experts, 1)
    gates_own = jnp.pad(gates_own, ((0, 0), (0, LANES - own_experts)))
    gates = lax.dynamic_slice_in_dim(gates_all, shard_at * row_count, row_count, 0)
    gates_own = after(gates_own, valid_count)
    mix_part, gate_up, hidden_gated = experts_forward(tokens_all, gates_own, w_in, w_out)
    mixture = scatter(mix_part).astype(jnp.float32)
    result_f = middle + resid_mult * mixture
    deviation = result_f - teacher.astype(jnp.float32)
    d_result = valid_float[:, None] * deviation * (all_tokens / (2.0 * valid_count))
    d_mix = (resid_mult * d_result).astype(jnp.bfloat16)
    d_mix_all = gather(d_mix)
    own_loss = jnp.sum(valid_float[:, None] * deviation * deviation)
    loss_sum = lax.psum(after(own_loss, d_mix), ("rep", "shard"))
    loss = loss_sum / (model_width * valid_count)
    gates_own = after(gates_own, loss_sum)
    d_rows_part, d_gate_up, d_gates_own = experts_backward(
        d_mix_all, gates_own, gate_up, w_in, w_out
    )
    d_rows = scatter(d_rows_part).astype(jnp.float32)
    d_gates = lax.all_to_all(
        d_gates_own[:, :own_experts], "shard", split_axis=0, concat_axis=1, tiled=True
    )
    kept_experts = own_experts // 2
    grad_rows = model_width + w_out.shape[1]
    flat_rows = kept_experts * grad_rows
    side = side_of(near)
    order = jnp.arange(kept_experts, dtype=jnp.int32)
    order_sent = order + (1 - side) * kept_experts
    order_kept = order + side * kept_experts
    sent = experts_grads(order_sent, tokens_all, d_mix_all, d_gate_up, hidden_gated)
    other = exchange(sent, near).reshape(flat_rows, -1)
    kept = experts_grads(after(order_kept, sent), tokens_all, d_mix_all, d_gate_up, hidden_gated)
    kept = kept.reshape(flat_rows, -1)
    moe_sent_first, moe_first = halve([kept, other], far[0], 0, 0, flat_rows // 2)
    moe_sent_second, moe_second = halve([kept, other], far[-1], 0, flat_rows // 2, flat_rows // 2)
    d_rows = after(d_rows, moe_sent_first, moe_sent_second)
    d_logits = (gates * (d_gates - jnp.sum(gates * d_gates, -1, keepdims=True))).astype(
        jnp.bfloat16
    )
    d_normed_ffn = d_rows + dot_nt(d_logits, router_full)
    grad_router = dot_tn(normed_ffn, d_logits)
    d_norm_mid, grad_gain_ffn = norm_back(d_normed_ffn, middle, scale_ffn, gain_ffn)
    d_middle = d_result + d_norm_mid
    d_branch = (resid_mult * d_middle).astype(jnp.bfloat16)
    d_attended = dot_nt(d_branch, output_full).astype(
        jnp.bfloat16
    )
    query_grad_rows, kv_grad_all = attention_backward(
        bias, query_rows, keys_all, values_all, log_norm, d_attended, tables, tables_own
    )
    d_normed_kv = dot_nt(kv_grad_all, kv_full)
    d_normed_query = dot_nt(query_grad_rows, query_full)
    d_normed_attn = scatter(d_normed_kv.astype(jnp.bfloat16)).astype(jnp.float32) + d_normed_query
    grad_gain_attn = jnp.sum(d_normed_kv * all_float * rms_scale(all_float), 0) + jnp.sum(
        d_normed_query * input_float * scale_attn, 0
    )
    d_norm_in, _ = norm_back(d_normed_attn, input_float, scale_attn, gain_attn)
    d_input = d_middle + d_norm_in
    grad_small = jnp.concatenate(
        [
            grad_gain_attn[:, None],
            grad_gain_ffn[:, None],
            grad_router,
            jnp.zeros((model_width, LANES - 2 - expert_count), jnp.float32),
        ],
        1,
    )

    first, second = attention_grads(
        normed_attn, query_grad_rows, normed_all, kv_grad_all, attended, d_branch, grad_small
    )
    first = [first.reshape(shard_count, own_rows, -1)]
    second = [second.reshape(shard_count, own_rows, -1)]
    for bit_first, bit_second in zip([near] + far, [near] + far[::-1]):
        _, first = halve(first, bit_first, 1)
        _, second = halve(second, bit_second, 1)
    split_at = first[0].shape[2]
    joined = jnp.concatenate([add_pair(*first), add_pair(*second)], 2)
    joined = lax.psum_scatter(joined, "shard", scatter_dimension=0)
    first, second = joined[:, :split_at], joined[:, split_at:]
    for bit_first, bit_second in zip(far[::-1] + [near], far + [near]):
        first = double(first, bit_first, 0)
        second = double(second, bit_second, 0)
    first, second = first.astype(jnp.float32), second.astype(jnp.float32)
    sum_query = first[:, :query_width]
    sum_key = second[:, :kv_width]
    sum_value = second[:, kv_width : 2 * kv_width]
    sum_output = jnp.concatenate(
        [first[:, query_width : query_width + half_width], second[:, 2 * kv_width :]], 1
    )
    sum_small = first[:, query_width + half_width :]
    for bit_first, bit_second in zip(far[1:], far[::-1][1:]):
        _, moe_first = halve(moe_first, bit_first, 0)
        _, moe_second = halve(moe_second, bit_second, 0)
    moe_first, moe_second = add_pair(*moe_first), add_pair(*moe_second)
    for bit_first, bit_second in zip(far[::-1], far):
        moe_first = double(moe_first, bit_first, 0)
        moe_second = double(moe_second, bit_second, 0)
    if kept_experts % 2 == 0:
        pieces = [moe_first, moe_second]
    else:
        pieces = [lax.concatenate([moe_first, moe_second], 0)]
    pieces = [piece.reshape(-1, grad_rows, piece.shape[1]) for piece in pieces]
    others = [exchange(piece, near) for piece in pieces]
    held = []
    for start, group in ((side, pieces), (1 - side, others)):
        base = start * kept_experts
        for piece in group:
            held = widen(jnp.reshape(base, (1,)), piece, model_width, own_experts, held)
            base = base + piece.shape[0]
    sum_in, sum_out = held
    return (
        result_f.astype(jnp.bfloat16),
        loss,
        d_input,
        sum_small[:, 0],
        sum_query,
        sum_key,
        sum_value,
        sum_output,
        sum_small[:, 1],
        sum_small[:, 2 : 2 + expert_count],
        sum_in,
        sum_out,
    )


def solution(mesh):
    in_specs = (
        P(("rep", "shard"), None),
        P(("rep", "shard")),
        P(("rep", "shard"), None),
        P(("rep", "shard"), None),
        P("shard"),
        P("shard", None),
        P("shard", None),
        P("shard", None),
        P("shard", None),
        P("shard"),
        P("shard", None),
        P("shard", None, None),
        P("shard", None, None),
    )
    out_specs = (
        P(("rep", "shard"), None),
        P(),
        P(("rep", "shard"), None),
        P("shard"),
        P("shard", None),
        P("shard", None),
        P("shard", None),
        P("shard", None),
        P("shard"),
        P("shard", None),
        P("shard", None, None),
        P("shard", None, None),
    )
    return jax.shard_map(body, mesh=mesh, in_specs=in_specs, out_specs=out_specs, check_vma=False)
```

```python
import jax
import jax.numpy as jnp
from jax import lax
from jax.experimental import pallas as pl
from jax.experimental.pallas import tpu as pltpu
from jax.sharding import PartitionSpec as P

HEADS = 16
KV_HEADS = 8
HEAD_DIM = 64
TOP = 8
BLOCK = 256
CHUNKS = 2
SMALL_COST = pl.CostEstimate(flops=1000000, bytes_accessed=100000, transcendentals=0)


norm_eps = 1e-06
resid_mult = 0.22
attn_mult = 0.015625
rope_base = 10000.0
very_low = -1e30


def rope_tables(positions):
    half_dim = HEAD_DIM // 2
    frequency = rope_base ** (-jnp.arange(half_dim, dtype=jnp.float32) / half_dim)
    angles = positions.astype(jnp.float32)[:, None] * frequency[None, :]
    cosine, sine = jnp.cos(angles), jnp.sin(angles)
    return (
        jnp.concatenate([cosine] * 4, 1),
        jnp.concatenate([-sine, sine, -sine, sine], 1),
    )


def rms_scale(values):
    return lax.rsqrt(jnp.mean(values * values, axis=-1, keepdims=True) + norm_eps)


def norm_back(d_normed, values, scale_vals, gain_vec):
    scaled_grad = d_normed * gain_vec
    d_gain = jnp.sum(d_normed * values * scale_vals, 0)
    d_values = scale_vals * (
        scaled_grad
        - values * scale_vals * scale_vals * jnp.mean(scaled_grad * values, axis=-1, keepdims=True)
    )
    return (d_values, d_gain)


LANES = 128
ROW_STEP = 256
EXPERT_STEP = 512


def row_chunks(count):
    step = min(count, EXPERT_STEP)
    return [pl.ds(at, step) for at in range(0, count, step)]


def pick_lane(values, lane):
    lanes = lax.broadcasted_iota(jnp.int32, values.shape, 1)
    return jnp.sum(jnp.where(lanes == lane, values, 0.0), axis=1, keepdims=True)


def dot_nn(left, right):
    return jnp.dot(left, right, preferred_element_type=jnp.float32)


def dot_nt(left, right):
    return lax.dot_general(left, right, (((1,), (1,)), ((), ())), preferred_element_type=jnp.float32)


def dot_tn(left, right):
    return lax.dot_general(left, right, (((0,), (0,)), ((), ())), preferred_element_type=jnp.float32)


def experts_forward_kernel(x_ref, gate_ref, in_ref, out_ref, mix_ref, gate_up_ref, hidden_ref, total):
    expert = pl.program_id(0)
    units = out_ref.shape[1]

    @pl.when(expert == 0)
    def _():
        total[...] = jnp.zeros_like(total)

    for rows in row_chunks(x_ref.shape[0]):
        gate_up = dot_nn(x_ref[rows, :], in_ref[0])
        gate_up_ref[0, rows, :] = gate_up
        gate_vals = gate_up[:, :units]
        silu_gate = gate_vals / (1.0 + jnp.exp(-gate_vals))
        weight = pick_lane(gate_ref[rows, :], expert)
        hidden = (silu_gate * gate_up[:, units:] * weight).astype(jnp.bfloat16)
        hidden_ref[0, rows, :] = hidden
        total[rows, :] += dot_nn(hidden, out_ref[0])

    @pl.when(expert == pl.num_programs(0) - 1)
    def _():
        mix_ref[...] = total[...].astype(mix_ref.dtype)


def experts_forward(tokens, gates_own, w_in, w_out):
    count, width = tokens.shape
    experts, units = w_out.shape[0], w_out.shape[1]
    return pl.pallas_call(
        experts_forward_kernel,
        grid=(experts,),
        in_specs=[
            pl.BlockSpec((count, width), lambda e: (0, 0)),
            pl.BlockSpec((count, LANES), lambda e: (0, 0)),
            pl.BlockSpec((1, width, 2 * units), lambda e: (e, 0, 0)),
            pl.BlockSpec((1, units, width), lambda e: (e, 0, 0)),
        ],
        out_specs=[
            pl.BlockSpec((count, width), lambda e: (0, 0)),
            pl.BlockSpec((1, count, 2 * units), lambda e: (e, 0, 0)),
            pl.BlockSpec((1, count, units), lambda e: (e, 0, 0)),
        ],
        out_shape=[
            jax.ShapeDtypeStruct((count, width), jnp.bfloat16),
            jax.ShapeDtypeStruct((experts, count, 2 * units), jnp.float32),
            jax.ShapeDtypeStruct((experts, count, units), jnp.bfloat16),
        ],
        scratch_shapes=[pltpu.VMEM((count, width), jnp.float32)],
        compiler_params=pltpu.CompilerParams(vmem_limit_bytes=VMEM_BYTES),
        cost_estimate=SMALL_COST,
        name="experts_forward",
    )(tokens, gates_own, w_in, w_out)


def experts_backward_kernel(
    dmix_ref, gate_ref, gate_up_ref, in_ref, out_ref, drows_ref, dgate_up_ref, dgates_ref, total
):
    expert = pl.program_id(0)
    units = out_ref.shape[1]
    lanes = lax.broadcasted_iota(jnp.int32, (1, LANES), 1)

    @pl.when(expert == 0)
    def _():
        total[...] = jnp.zeros_like(total)
        dgates_ref[...] = jnp.zeros_like(dgates_ref)

    for rows in row_chunks(dmix_ref.shape[0]):
        pulled = dot_nt(dmix_ref[rows, :], out_ref[0])
        gate_vals = gate_up_ref[0, rows, :units]
        up_vals = gate_up_ref[0, rows, units:]
        sigmoid = 1.0 / (1.0 + jnp.exp(-gate_vals))
        silu_gate = gate_vals * sigmoid
        weight = pick_lane(gate_ref[rows, :], expert)
        d_up = pulled * silu_gate
        own = jnp.sum(d_up * up_vals, axis=1, keepdims=True)
        own = jnp.where(lanes == expert, own, 0.0)
        d_up = d_up * weight
        d_gate = (pulled * weight) * up_vals * (sigmoid + silu_gate * (1.0 - sigmoid))
        dgate_up_ref[0, rows, :units] = d_gate.astype(jnp.bfloat16)
        dgate_up_ref[0, rows, units:] = d_up.astype(jnp.bfloat16)
        total[rows, :] += dot_nt(dgate_up_ref[0, rows, :], in_ref[0])
        dgates_ref[rows, :] += own

    @pl.when(expert == pl.num_programs(0) - 1)
    def _():
        drows_ref[...] = total[...].astype(drows_ref.dtype)


def experts_backward(d_mix, gates_own, gate_up, w_in, w_out):
    count, width = d_mix.shape
    experts, units = w_out.shape[0], w_out.shape[1]
    return pl.pallas_call(
        experts_backward_kernel,
        grid=(experts,),
        in_specs=[
            pl.BlockSpec((count, width), lambda e: (0, 0)),
            pl.BlockSpec((count, LANES), lambda e: (0, 0)),
            pl.BlockSpec((1, count, 2 * units), lambda e: (e, 0, 0)),
            pl.BlockSpec((1, width, 2 * units), lambda e: (e, 0, 0)),
            pl.BlockSpec((1, units, width), lambda e: (e, 0, 0)),
        ],
        out_specs=[
            pl.BlockSpec((count, width), lambda e: (0, 0)),
            pl.BlockSpec((1, count, 2 * units), lambda e: (e, 0, 0)),
            pl.BlockSpec((count, LANES), lambda e: (0, 0)),
        ],
        out_shape=[
            jax.ShapeDtypeStruct((count, width), jnp.bfloat16),
            jax.ShapeDtypeStruct((experts, count, 2 * units), jnp.bfloat16),
            jax.ShapeDtypeStruct((count, LANES), jnp.float32),
        ],
        scratch_shapes=[pltpu.VMEM((count, width), jnp.float32)],
        compiler_params=pltpu.CompilerParams(vmem_limit_bytes=VMEM_BYTES),
        cost_estimate=SMALL_COST,
        name="experts_backward",
    )(d_mix, gates_own, gate_up, w_in, w_out)


def experts_grads_kernel(order_ref, *refs):
    grads_ref = refs[-1]
    count = (len(refs) - 1) // 4
    width = refs[0].shape[1]
    grad_in, grad_out = None, None
    for at in range(count):
        x_ref, dmix_ref, dgate_up_ref, hidden_ref = refs[4 * at : 4 * at + 4]
        part_in = dot_tn(x_ref[...], dgate_up_ref[0])
        part_out = dot_tn(hidden_ref[0], dmix_ref[...])
        grad_in = part_in if grad_in is None else grad_in + part_in
        grad_out = part_out if grad_out is None else grad_out + part_out
    grads_ref[0, :width, :] = grad_in.astype(grads_ref.dtype)
    grads_ref[0, width:, :] = grad_out.astype(grads_ref.dtype)


def experts_grads(order, chunks):
    count, width = chunks[0][0].shape
    units = chunks[0][3].shape[2]
    experts = order.shape[0]
    specs = [
        pl.BlockSpec((count, width), lambda e, order: (0, 0)),
        pl.BlockSpec((count, width), lambda e, order: (0, 0)),
        pl.BlockSpec((1, count, 2 * units), lambda e, order: (order[e], 0, 0)),
        pl.BlockSpec((1, count, units), lambda e, order: (order[e], 0, 0)),
    ]
    return pl.pallas_call(
        experts_grads_kernel,
        grid_spec=pltpu.PrefetchScalarGridSpec(
            num_scalar_prefetch=1,
            grid=(experts,),
            in_specs=specs * len(chunks),
            out_specs=pl.BlockSpec((1, width + units, 2 * units), lambda e, order: (e, 0, 0)),
        ),
        out_shape=jax.ShapeDtypeStruct((experts, width + units, 2 * units), jnp.bfloat16),
        compiler_params=pltpu.CompilerParams(vmem_limit_bytes=VMEM_BYTES),
        cost_estimate=SMALL_COST,
        name="experts_grads",
    )(order, *[part for chunk in chunks for part in chunk])


def widen_kernel(base_ref, piece_ref, *refs):
    gin_ref, gout_ref = refs[-2:]
    width = gin_ref.shape[1]
    gin_ref[...] = piece_ref[:, :width, :].astype(jnp.float32)
    gout_ref[...] = piece_ref[:, width:, :].astype(jnp.float32)


def widen(base, piece, width, total, held):
    count, rows, columns = piece.shape
    shapes = [
        jax.ShapeDtypeStruct((total, width, columns), jnp.float32),
        jax.ShapeDtypeStruct((total, rows - width, columns), jnp.float32),
    ]
    return pl.pallas_call(
        widen_kernel,
        grid_spec=pltpu.PrefetchScalarGridSpec(
            num_scalar_prefetch=1,
            grid=(count,),
            in_specs=[pl.BlockSpec((1, rows, columns), lambda e, base: (e, 0, 0))]
            + [pl.BlockSpec(memory_space=pl.ANY)] * len(held),
            out_specs=[
                pl.BlockSpec((1, width, columns), lambda e, base: (base[0] + e, 0, 0)),
                pl.BlockSpec((1, rows - width, columns), lambda e, base: (base[0] + e, 0, 0)),
            ],
        ),
        out_shape=shapes,
        input_output_aliases={2 + at: at for at in range(len(held))},
        compiler_params=pltpu.CompilerParams(vmem_limit_bytes=VMEM_BYTES),
        cost_estimate=SMALL_COST,
        name="widen",
    )(base, piece, *held)


def attention_grads_kernel(
    normed_ref, dquery_ref, all_ref, dkv_ref, attended_ref, dbranch_ref, small_ref, first_ref, second_ref
):
    query_width = dquery_ref.shape[1]
    half = dbranch_ref.shape[1] // 2
    kv_width = dkv_ref.shape[1]
    low = jnp.bfloat16
    second_ref[:, :kv_width] = dot_tn(all_ref[...], dkv_ref[...]).astype(low)
    first_ref[:, :query_width] = dot_tn(normed_ref[...], dquery_ref[...]).astype(low)
    grad_output = dot_tn(attended_ref[...], dbranch_ref[...]).astype(low)
    first_ref[:, query_width : query_width + half] = grad_output[:, :half]
    second_ref[:, kv_width:] = grad_output[:, half:]
    first_ref[:, query_width + half :] = small_ref[...].astype(low)


def attention_grads(normed, d_query, normed_all, d_kv, attended, d_branch, small):
    width = normed.shape[1]
    half = d_branch.shape[1] // 2
    return pl.pallas_call(
        attention_grads_kernel,
        in_specs=[whole_spec()] * 7,
        out_specs=[whole_spec()] * 2,
        out_shape=[
            jax.ShapeDtypeStruct((width, d_query.shape[1] + half + LANES), jnp.bfloat16),
            jax.ShapeDtypeStruct((width, d_kv.shape[1] + half), jnp.bfloat16),
        ],
        compiler_params=pltpu.CompilerParams(vmem_limit_bytes=VMEM_BYTES),
        cost_estimate=SMALL_COST,
        name="attention_grads",
    )(normed, d_query, normed_all, d_kv, attended, d_branch, small)


VMEM_BYTES = 60 * 1024 * 1024


def swap_halves(values):
    lanes = lax.broadcasted_iota(jnp.int32, values.shape, 1)
    ahead = pltpu.roll(values, LANES - HEAD_DIM // 2, 1)
    behind = pltpu.roll(values, HEAD_DIM // 2, 1)
    return jnp.where(lanes % HEAD_DIM < HEAD_DIM // 2, ahead, behind)


def stack_heads(block, parity):
    values = block.astype(jnp.float32)
    lanes = lax.broadcasted_iota(jnp.int32, values.shape, 1)
    low = jnp.where(lanes < HEAD_DIM, values, 0.0)
    high = values - low
    if parity == 0:
        high = pltpu.roll(high, HEAD_DIM, 1)
    else:
        low = pltpu.roll(low, HEAD_DIM, 1)
    return jnp.concatenate([low, high], 0).astype(jnp.bfloat16)


def unstack_heads(stacked, parity):
    rows = stacked.shape[0] // 2
    low, high = stacked[:rows], stacked[rows:]
    if parity == 0:
        high = pltpu.roll(high, HEAD_DIM, 1)
    else:
        low = pltpu.roll(low, HEAD_DIM, 1)
    lanes = lax.broadcasted_iota(jnp.int32, low.shape, 1)
    return jnp.where(lanes < HEAD_DIM, low, high)


def lane_block(at):
    return pl.ds(pl.multiple_of(at * LANES, LANES), LANES)


def attention_forward_kernel(
    bias_ref, all_ref, own_ref, gain_ref, wq_ref, wkv_ref, cos_ref, sin_ref, cos_own_ref, sin_own_ref,
    normed_ref, query_ref, key_ref, value_ref, attended_ref, norm_ref, scores
):
    tokens, width = all_ref.shape
    kv_width = key_ref.shape[1]
    key_rows = tokens // bias_ref.shape[0]

    def normed_rows(block):
        values = block.astype(jnp.float32)
        scale = lax.rsqrt(jnp.mean(values * values, axis=-1, keepdims=True) + norm_eps)
        return (values * scale * gain_ref[...]).astype(jnp.bfloat16)

    def project(at, carry):
        rows = pl.ds(pl.multiple_of(at * ROW_STEP, ROW_STEP), ROW_STEP)
        normed = normed_rows(all_ref[rows, :])
        normed_ref[rows, :] = normed
        linear = dot_nn(normed, wkv_ref[...])
        for col in range(0, kv_width, LANES):
            part = linear[:, col : col + LANES]
            turned = part * cos_ref[rows, :] + swap_halves(part) * sin_ref[rows, :]
            key_ref[rows, col : col + LANES] = turned.astype(jnp.bfloat16)
        value_ref[rows, :] = linear[:, kv_width:].astype(jnp.bfloat16)
        return carry

    lax.fori_loop(0, tokens // ROW_STEP, project, 0)
    linear = dot_nn(normed_rows(own_ref[...]), wq_ref[...])
    for col in range(0, wq_ref.shape[1], LANES):
        part = linear[:, col : col + LANES]
        turned = part * cos_own_ref[...] + swap_halves(part) * sin_own_ref[...]
        query_ref[:, col : col + LANES] = (turned.astype(jnp.bfloat16).astype(jnp.float32) * attn_mult).astype(jnp.bfloat16)

    def attend(pair, carry):
        lanes = lane_block(pair)
        turned_values = value_ref[:, lanes].astype(jnp.float32).T.astype(jnp.bfloat16)
        for parity in range(2):
            group = 2 * pair + parity
            stacked = stack_heads(query_ref[:, lane_block(group)], parity)
            top = None
            for at in range(bias_ref.shape[0]):
                rows = pl.ds(at * key_rows, key_rows)
                part = dot_nt(key_ref[rows, lanes], stacked) + bias_ref[at]
                scores[rows, :] = part
                high = jnp.max(part, axis=0, keepdims=True)
                top = high if top is None else jnp.maximum(top, high)
            total, gathered = None, None
            for at in range(bias_ref.shape[0]):
                rows = pl.ds(at * key_rows, key_rows)
                raised = jnp.exp(scores[rows, :] - top)
                part = jnp.sum(raised, axis=0, keepdims=True)
                mixed = dot_nn(
                    turned_values[:, at * key_rows : (at + 1) * key_rows], raised.astype(jnp.bfloat16)
                )
                total = part if total is None else total + part
                gathered = mixed if gathered is None else gathered + mixed
            gathered = (gathered / total).T
            attended_ref[:, lane_block(group)] = unstack_heads(gathered, parity).astype(jnp.bfloat16)
            norm_ref[pl.ds(group, 1), :] = top + jnp.log(total)
        return carry

    lax.fori_loop(0, kv_width // LANES, attend, 0)


def whole_spec():
    return pl.BlockSpec(memory_space=pltpu.VMEM)


def attention_forward(bias, input_all, hidden_in, gain, w_query, w_kv, tables, tables_own):
    tokens, width = input_all.shape
    rows = hidden_in.shape[0]
    kv_width = w_kv.shape[1] // 2
    return pl.pallas_call(
        attention_forward_kernel,
        in_specs=[pl.BlockSpec(memory_space=pltpu.SMEM)] + [whole_spec()] * 9,
        out_specs=[whole_spec()] * 6,
        out_shape=[
            jax.ShapeDtypeStruct((tokens, width), jnp.bfloat16),
            jax.ShapeDtypeStruct((rows, w_query.shape[1]), jnp.bfloat16),
            jax.ShapeDtypeStruct((tokens, kv_width), jnp.bfloat16),
            jax.ShapeDtypeStruct((tokens, kv_width), jnp.bfloat16),
            jax.ShapeDtypeStruct((rows, w_query.shape[1]), jnp.bfloat16),
            jax.ShapeDtypeStruct((KV_HEADS, 2 * rows), jnp.float32),
        ],
        scratch_shapes=[pltpu.VMEM((tokens, 2 * rows), jnp.float32)],
        compiler_params=pltpu.CompilerParams(vmem_limit_bytes=VMEM_BYTES),
        cost_estimate=SMALL_COST,
        name="attention_forward",
    )(bias, input_all, hidden_in, gain, w_query, w_kv, *tables, *tables_own)


def attention_backward_kernel(
    bias_ref, query_ref, key_ref, value_ref, norm_ref, grad_ref, cos_ref, sin_ref, cos_own_ref, sin_own_ref,
    dquery_ref, dkv_ref, probs, dprobs, dkeys, dvalues
):
    tokens, kv_width = key_ref.shape
    key_rows = tokens // bias_ref.shape[0]

    def pull(pair, carry):
        lanes = lane_block(pair)
        turned_keys = key_ref[:, lanes].astype(jnp.float32).T.astype(jnp.bfloat16)
        for parity in range(2):
            group = 2 * pair + parity
            stacked = stack_heads(query_ref[:, lane_block(group)], parity)
            stacked_grad = stack_heads(grad_ref[:, lane_block(group)], parity)
            log_norm = norm_ref[pl.ds(group, 1), :]
            total = None
            for at in range(bias_ref.shape[0]):
                rows = pl.ds(at * key_rows, key_rows)
                part = dot_nt(key_ref[rows, lanes], stacked) + bias_ref[at]
                prob = jnp.exp(part - log_norm)
                d_prob = dot_nt(value_ref[rows, lanes], stacked_grad)
                probs[rows, :] = prob
                dprobs[rows, :] = d_prob
                d_value = dot_nn(prob.astype(jnp.bfloat16), stacked_grad)
                dvalues[rows, :] = d_value if parity == 0 else dvalues[rows, :] + d_value
                weighted = jnp.sum(prob * d_prob, axis=0, keepdims=True)
                total = weighted if total is None else total + weighted
            d_query = None
            for at in range(bias_ref.shape[0]):
                rows = pl.ds(at * key_rows, key_rows)
                d_score = (probs[rows, :] * (dprobs[rows, :] - total)).astype(jnp.bfloat16)
                d_key = dot_nn(d_score, stacked)
                dkeys[rows, :] = d_key if parity == 0 else dkeys[rows, :] + d_key
                part = dot_nn(turned_keys[:, at * key_rows : (at + 1) * key_rows], d_score)
                d_query = part if d_query is None else d_query + part
            part = unstack_heads(d_query.T, parity) * attn_mult
            turned = part * cos_own_ref[...] - swap_halves(part) * sin_own_ref[...]
            dquery_ref[:, lane_block(group)] = turned.astype(jnp.bfloat16)
        part = dkeys[...]
        turned = part * cos_ref[...] - swap_halves(part) * sin_ref[...]
        dkv_ref[:, lanes] = turned.astype(jnp.bfloat16)
        dkv_ref[:, lane_block(pair + kv_width // LANES)] = dvalues[...].astype(jnp.bfloat16)
        return carry

    lax.fori_loop(0, kv_width // LANES, pull, 0)


def attention_backward(bias, query, key, value, log_norm, grad, tables, tables_own):
    tokens, kv_width = key.shape
    rows, width = query.shape
    return pl.pallas_call(
        attention_backward_kernel,
        in_specs=[pl.BlockSpec(memory_space=pltpu.SMEM)] + [whole_spec()] * 9,
        out_specs=[whole_spec()] * 2,
        out_shape=[
            jax.ShapeDtypeStruct((rows, width), jnp.bfloat16),
            jax.ShapeDtypeStruct((tokens, 2 * kv_width), jnp.bfloat16),
        ],
        scratch_shapes=[
            pltpu.VMEM((tokens, 2 * rows), jnp.float32),
            pltpu.VMEM((tokens, 2 * rows), jnp.float32),
            pltpu.VMEM((tokens, LANES), jnp.float32),
            pltpu.VMEM((tokens, LANES), jnp.float32),
        ],
        compiler_params=pltpu.CompilerParams(vmem_limit_bytes=VMEM_BYTES),
        cost_estimate=SMALL_COST,
        name="attention_backward",
    )(bias, query, key, value, log_norm, grad, *tables, *tables_own)


def exchange(block, bit):
    count = lax.axis_size("rep")
    return lax.ppermute(block, "rep", [(at, at ^ bit) for at in range(count)])


def side_of(bit):
    return (lax.axis_index("rep") // bit) % 2


def after(value, *others):
    return lax.optimization_barrier((value, *others))[0]


def slices_of(parts, start, size, axis):
    return [lax.dynamic_slice_in_dim(part, start, size, axis) for part in parts]


def add_parts(parts):
    total = parts[0].astype(jnp.float32)
    for part in parts[1:]:
        total = total + part.astype(jnp.float32)
    return total.astype(jnp.bfloat16)


def halve(parts, bit, axis, offset=0, length=None):
    length = parts[0].shape[axis] if length is None else length
    half = length // 2
    side = side_of(bit)
    sent = slices_of(parts, offset + (1 - side) * half, half, axis)
    sent = sent[0] if len(sent) == 1 else add_parts(sent)
    kept = slices_of(parts, offset + side * half, half, axis)
    return sent, kept + [exchange(sent, bit)]


def double(block, bit, axis):
    size = block.shape[axis]
    side = side_of(bit)
    held = lax.concatenate([block, block], axis)
    return lax.dynamic_update_slice_in_dim(held, exchange(block, bit), (1 - side) * size, axis)


def rep_bits():
    count = lax.axis_size("rep")
    return [1 << at for at in range(count.bit_length() - 1)]


def body(
    hidden_in,
    valid_mask,
    teacher,
    routes,
    attn_norm,
    w_query,
    w_key,
    w_value,
    w_output,
    ffn_norm,
    router,
    w_in,
    w_out,
):
    row_count, model_width = hidden_in.shape
    shard_count = lax.axis_size("shard")
    seq_tokens = row_count * shard_count
    all_tokens = seq_tokens * lax.axis_size("rep")
    shard_at = lax.axis_index("shard")
    tables = rope_tables(jnp.arange(seq_tokens, dtype=jnp.int32))
    tables_own = tuple(
        lax.dynamic_slice_in_dim(table, shard_at * row_count, row_count, 0) for table in tables
    )
    key_blocks = jnp.arange(seq_tokens // BLOCK, dtype=jnp.int32)
    bias = jnp.where(key_blocks <= shard_at * row_count // BLOCK, 0.0, very_low)
    bits = rep_bits()
    near, far = bits[0], bits[1:]

    def gather(block):
        return lax.all_gather(block, "shard", axis=0, tiled=True)

    def scatter(block):
        return lax.psum_scatter(block, "shard", scatter_dimension=0, tiled=True)

    kv_width = w_key.shape[1]
    query_width = w_query.shape[1]
    half_width = w_output.shape[1] // 2
    own_rows = w_query.shape[0]
    piece_rows = own_rows // lax.axis_size("rep")

    def piece_of(block, order):
        index = 0
        for at, bit in enumerate(order):
            index = index + side_of(bit) * (1 << at)
        return lax.dynamic_slice_in_dim(block, index * piece_rows, piece_rows, 0)

    order_first, order_second = far + [near], far[::-1] + [near]
    w_kv = jnp.concatenate([w_key, w_value], 1)
    input_all = gather(hidden_in)
    pieces = lax.all_gather(
        jnp.concatenate([piece_of(w_query, order_first), piece_of(w_kv, order_second)], 1),
        "shard",
        axis=0,
    )
    query_full = pieces[..., :query_width]
    kv_full = pieces[..., query_width:]
    for bit_first, bit_second in zip(order_first, order_second):
        query_full = double(query_full, bit_first, 1)
        kv_full = double(kv_full, bit_second, 1)
    query_full = query_full.reshape(own_rows * shard_count, query_width)
    kv_full = kv_full.reshape(own_rows * shard_count, 2 * kv_width)
    near_rows = own_rows // 2
    output_half = lax.dynamic_slice_in_dim(w_output, side_of(near) * near_rows, near_rows, 0)
    output_half = lax.all_gather(after(output_half, input_all), "shard", axis=0)
    expert_count = router.shape[1]
    valid_float = valid_mask.astype(jnp.float32)
    small_parts = [
        jnp.concatenate([attn_norm[:, None], ffn_norm[:, None], router], 1).reshape(1, -1),
        routes.astype(jnp.bfloat16).reshape(1, -1),
        jnp.sum(valid_float).astype(jnp.bfloat16).reshape(1, 1),
    ]
    small_all = gather(jnp.concatenate(small_parts, 1))
    small_size, routes_size = small_parts[0].size, small_parts[1].size
    small_full = small_all[:, :small_size].reshape(-1, 2 + expert_count)
    routes_all = small_all[:, small_size : small_size + routes_size]
    valid_count = jnp.broadcast_to(jnp.sum(small_all[:, -1].astype(jnp.float32)), (8, LANES))
    for bit in bits:
        valid_count = valid_count + exchange(valid_count, bit)
    valid_count = valid_count[0, 0]
    gain_attn, gain_ffn = small_full[:, 0], small_full[:, 1]
    router_full = small_full[:, 2:]
    gain_attn = gain_attn.astype(jnp.float32)
    input_float = hidden_in.astype(jnp.float32)
    scale_attn = rms_scale(input_float)
    all_float = input_all.astype(jnp.float32)
    normed_all, query_rows, keys_all, values_all, attended, log_norm = attention_forward(
        bias, input_all, hidden_in, gain_attn[None], query_full, kv_full, tables, tables_own
    )
    normed_attn = lax.dynamic_slice_in_dim(normed_all, shard_at * row_count, row_count, 0)
    output_half, attended = lax.optimization_barrier((output_half, attended))
    output_full = double(output_half, near, 1).reshape(own_rows * shard_count, -1)
    branch = dot_nn(attended, output_full)
    middle = input_float + resid_mult * branch
    scale_ffn = rms_scale(middle)
    normed_ffn = (middle * scale_ffn * gain_ffn).astype(jnp.bfloat16)
    own_experts = w_in.shape[0]
    expert_ids = jnp.arange(expert_count, dtype=jnp.bfloat16)
    chunk_rows = row_count // CHUNKS
    spans = [slice(at * chunk_rows, (at + 1) * chunk_rows) for at in range(CHUNKS)]
    tokens_in = [gather(normed_ffn[span]) for span in spans]
    routes_all = routes_all.reshape(shard_count, row_count, -1)
    gates, forward = [], []
    for span, tokens in zip(spans, tokens_in):
        logits = dot_nn(tokens, router_full)
        routes_part = routes_all[:, span].reshape(shard_count * chunk_rows, -1)
        chosen = jnp.any(routes_part[..., None] == expert_ids, 1)
        masked = jnp.where(chosen, logits, very_low)
        raised = jnp.where(chosen, jnp.exp(masked - jnp.max(masked, -1, keepdims=True)), 0.0)
        gates_part = raised / jnp.sum(raised, -1, keepdims=True)
        gates_own = lax.dynamic_slice_in_dim(gates_part, shard_at * own_experts, own_experts, 1)
        gates_own = jnp.pad(gates_own, ((0, 0), (0, LANES - own_experts)))
        gates.append(lax.dynamic_slice_in_dim(gates_part, shard_at * chunk_rows, chunk_rows, 0))
        forward.append((gates_own, *experts_forward(tokens, gates_own, w_in, w_out)))
    gates = jnp.concatenate(gates, 0)
    results, d_results, d_mix_out, d_mix_in, own_loss = [], [], [], [], 0.0
    for span, (_, mix_part, _, _) in zip(spans, forward):
        mixture = scatter(mix_part)
        if d_mix_out:
            mixture = after(mixture, d_mix_out[-1])
        mixture = mixture.astype(jnp.float32)
        result_part = middle[span] + resid_mult * mixture
        deviation = result_part - teacher[span].astype(jnp.float32)
        masked = valid_float[span, None] * deviation
        d_result = masked * (all_tokens / (2.0 * valid_count))
        results.append(result_part.astype(jnp.bfloat16))
        d_results.append(d_result)
        d_mix_out.append((resid_mult * d_result).astype(jnp.bfloat16))
        d_mix_in.append(gather(d_mix_out[-1]))
        own_loss = own_loss + jnp.sum(masked * deviation)
    d_result = jnp.concatenate(d_results, 0)
    d_rows, d_gates, backward = [], [], []
    for d_mix, (gates_own, _, gate_up, hidden_gated), tokens in zip(d_mix_in, forward, tokens_in):
        d_rows_part, d_gate_up, d_gates_part = experts_backward(
            d_mix, gates_own, gate_up, w_in, w_out
        )
        d_rows.append(scatter(d_rows_part))
        d_gates.append(d_gates_part[:, :own_experts].reshape(shard_count, chunk_rows, own_experts))
        backward.append((tokens, d_mix, d_gate_up, hidden_gated))
    d_rows_in = d_rows
    d_rows = jnp.concatenate(d_rows, 0).astype(jnp.float32)
    d_gates = jnp.concatenate(d_gates, 1).reshape(shard_count * row_count, own_experts)
    d_gates = lax.all_to_all(d_gates, "shard", split_axis=0, concat_axis=1, tiled=True)
    kept_experts = own_experts // 2
    grad_rows = model_width + w_out.shape[1]
    flat_rows = kept_experts * grad_rows
    side = side_of(near)
    order = jnp.arange(kept_experts, dtype=jnp.int32)
    order_sent = order + (1 - side) * kept_experts
    order_kept = order + side * kept_experts
    flat = (grad_rows, w_in.shape[2])
    sent = [experts_grads(order_sent[at : at + 1], backward).reshape(flat) for at in range(kept_experts)]
    other = [exchange(part, near) for part in sent]
    kept = experts_grads(after(order_kept, *sent, d_rows_in[0]), backward).reshape(flat_rows, -1)
    if kept_experts > 1:
        kept_first, kept_second = kept[: flat_rows // 2], kept[flat_rows // 2 :]
        other_first = jnp.concatenate(other[: kept_experts // 2], 0)
        other_second = jnp.concatenate(other[kept_experts // 2 :], 0)
    else:
        kept_first, kept_second = kept[: flat_rows // 2], kept[flat_rows // 2 :]
        other_first, other_second = other[0][: flat_rows // 2], other[0][flat_rows // 2 :]
    moe_sent_first, moe_first = halve([kept_first, other_first], far[0], 0)
    moe_sent_second, moe_second = halve([kept_second, other_second], far[-1], 0)
    d_rows = after(d_rows, moe_sent_first, moe_sent_second)
    d_logits = (gates * (d_gates - jnp.sum(gates * d_gates, -1, keepdims=True))).astype(
        jnp.bfloat16
    )
    d_normed_ffn = d_rows + dot_nt(d_logits, router_full)
    grad_router = dot_tn(normed_ffn, d_logits)
    d_norm_mid, grad_gain_ffn = norm_back(d_normed_ffn, middle, scale_ffn, gain_ffn)
    d_middle = d_result + d_norm_mid
    d_branch = (resid_mult * d_middle).astype(jnp.bfloat16)
    d_attended = dot_nt(d_branch, output_full).astype(
        jnp.bfloat16
    )
    query_grad_rows, kv_grad_all = attention_backward(
        bias, query_rows, keys_all, values_all, log_norm, d_attended, tables, tables_own
    )
    query_grad_rows, kv_grad_all = lax.optimization_barrier(
        (query_grad_rows, kv_grad_all, moe_first[-1], moe_second[-1])
    )[:2]
    d_normed_kv = dot_nt(kv_grad_all, kv_full)
    d_normed_query = dot_nt(query_grad_rows, query_full)
    grad_gain_attn = jnp.sum(d_normed_kv * all_float * rms_scale(all_float), 0) + jnp.sum(
        d_normed_query * input_float * scale_attn, 0
    )
    kv_scattered = scatter(d_normed_kv.astype(jnp.bfloat16))
    grad_small = jnp.concatenate(
        [
            grad_gain_attn[:, None],
            grad_gain_ffn[:, None],
            grad_router,
            jnp.zeros((model_width, LANES - 2 - expert_count), jnp.float32),
        ],
        1,
    )

    first, second = attention_grads(
        normed_attn, query_grad_rows, normed_all, kv_grad_all, attended, d_branch, grad_small
    )
    d_normed_query = after(d_normed_query, first, second)
    d_normed_attn = kv_scattered.astype(jnp.float32) + d_normed_query
    d_norm_in, _ = norm_back(d_normed_attn, input_float, scale_attn, gain_attn)
    d_input = d_middle + d_norm_in
    for bit_first, bit_second in zip(far[1:], far[::-1][1:]):
        _, moe_first = halve(moe_first, bit_first, 0)
        _, moe_second = halve(moe_second, bit_second, 0)
    first, second = lax.optimization_barrier((first, second, moe_first[-1], moe_second[-1]))[:2]
    moe_first, moe_second = add_parts(moe_first), add_parts(moe_second)
    first = [first.reshape(shard_count, own_rows, -1)]
    second = [second.reshape(shard_count, own_rows, -1)]
    _, first = halve(first, near, 1)
    _, second = halve(second, near, 1)
    for bit_first, bit_second in zip(far[:0:-1], far[:-1]):
        moe_first = double(moe_first, bit_first, 0)
        moe_second = double(moe_second, bit_second, 0)
    for bit_first, bit_second in zip(far, far[::-1]):
        _, first = halve(first, bit_first, 1)
        _, second = halve(second, bit_second, 1)
    moe_first = after(moe_first, first[-1], second[-1])
    moe_second = after(moe_second, first[-1], second[-1])
    moe_first = double(moe_first, far[0], 0)
    moe_second = double(moe_second, far[-1], 0)
    split_at = first[0].shape[2]
    joined = jnp.concatenate([add_parts(first), add_parts(second)], 2)
    joined = lax.psum_scatter(joined, "shard", scatter_dimension=0)
    first, second = joined[:, :split_at], joined[:, split_at:]
    for bit_first, bit_second in zip(far[::-1] + [near], far + [near]):
        first = double(first, bit_first, 0)
        second = double(second, bit_second, 0)
    first, second = first.astype(jnp.float32), second.astype(jnp.float32)
    sum_query = first[:, :query_width]
    sum_key = second[:, :kv_width]
    sum_value = second[:, kv_width : 2 * kv_width]
    sum_output = jnp.concatenate(
        [first[:, query_width : query_width + half_width], second[:, 2 * kv_width :]], 1
    )
    sum_small = first[:, query_width + half_width :]
    if kept_experts % 2 == 0:
        pieces = [moe_first, moe_second]
    else:
        pieces = [lax.concatenate([moe_first, moe_second], 0)]
    pieces = [piece.reshape(-1, grad_rows, piece.shape[1]) for piece in pieces]
    others = [exchange(piece, near) for piece in pieces]
    held = []
    for start, group in ((side, pieces), (1 - side, others)):
        base = start * kept_experts
        for piece in group:
            held = widen(jnp.reshape(base, (1,)), piece, model_width, own_experts, held)
            base = base + piece.shape[0]
    sum_in, sum_out = held
    loss_sum = jnp.broadcast_to(own_loss, (8, LANES))
    for bit in bits:
        loss_sum = loss_sum + exchange(loss_sum, bit)
    step = 1
    while step < shard_count:
        pairs = [(at, at ^ step) for at in range(shard_count)]
        loss_sum = loss_sum + lax.ppermute(loss_sum, "shard", pairs)
        step = 2 * step
    loss = loss_sum[0, 0] / (model_width * valid_count)
    return (
        jnp.concatenate(results, 0),
        loss,
        d_input,
        sum_small[:, 0],
        sum_query,
        sum_key,
        sum_value,
        sum_output,
        sum_small[:, 1],
        sum_small[:, 2 : 2 + expert_count],
        sum_in,
        sum_out,
    )


def solution(mesh):
    in_specs = (
        P(("rep", "shard"), None),
        P(("rep", "shard")),
        P(("rep", "shard"), None),
        P(("rep", "shard"), None),
        P("shard"),
        P("shard", None),
        P("shard", None),
        P("shard", None),
        P("shard", None),
        P("shard"),
        P("shard", None),
        P("shard", None, None),
        P("shard", None, None),
    )
    out_specs = (
        P(("rep", "shard"), None),
        P(),
        P(("rep", "shard"), None),
        P("shard"),
        P("shard", None),
        P("shard", None),
        P("shard", None),
        P("shard", None),
        P("shard"),
        P("shard", None),
        P("shard", None, None),
        P("shard", None, None),
    )
    return jax.shard_map(body, mesh=mesh, in_specs=in_specs, out_specs=out_specs, check_vma=False)
```

```python
import functools

import jax
import jax.numpy as jnp
from jax import lax
from jax.experimental import pallas as pl
from jax.experimental.pallas import tpu as pltpu
from jax.sharding import PartitionSpec as P

HEADS = 16
KV_HEADS = 8
HEAD_DIM = 64
TOP = 8
BLOCK = 256
CHUNKS = 2
SMALL_COST = pl.CostEstimate(flops=1000000, bytes_accessed=100000, transcendentals=0)


norm_eps = 1e-06
resid_mult = 0.22
attn_mult = 0.015625
rope_base = 10000.0
very_low = -1e30


def rope_tables(positions):
    half_dim = HEAD_DIM // 2
    frequency = rope_base ** (-jnp.arange(half_dim, dtype=jnp.float32) / half_dim)
    angles = positions.astype(jnp.float32)[:, None] * frequency[None, :]
    cosine, sine = jnp.cos(angles), jnp.sin(angles)
    return (
        jnp.concatenate([cosine] * 4, 1),
        jnp.concatenate([-sine, sine, -sine, sine], 1),
    )


def rms_scale(values):
    return lax.rsqrt(jnp.mean(values * values, axis=-1, keepdims=True) + norm_eps)


def norm_back(d_normed, values, scale_vals, gain_vec):
    scaled_grad = d_normed * gain_vec
    d_gain = jnp.sum(d_normed * values * scale_vals, 0)
    d_values = scale_vals * (
        scaled_grad
        - values * scale_vals * scale_vals * jnp.mean(scaled_grad * values, axis=-1, keepdims=True)
    )
    return (d_values, d_gain)


LANES = 128
ROW_STEP = 256
EXPERT_STEP = 512


def row_chunks(count):
    step = min(count, EXPERT_STEP)
    return [pl.ds(at, step) for at in range(0, count, step)]


def pick_lane(values, lane):
    lanes = lax.broadcasted_iota(jnp.int32, values.shape, 1)
    return jnp.sum(jnp.where(lanes == lane, values, 0.0), axis=1, keepdims=True)


def dot_nn(left, right):
    return jnp.dot(left, right, preferred_element_type=jnp.float32)


def dot_nt(left, right):
    return lax.dot_general(left, right, (((1,), (1,)), ((), ())), preferred_element_type=jnp.float32)


def dot_tn(left, right):
    return lax.dot_general(left, right, (((0,), (0,)), ((), ())), preferred_element_type=jnp.float32)


def experts_forward_kernel(x_ref, gate_ref, in_ref, out_ref, mix_ref, gate_up_ref, hidden_ref, total):
    expert = pl.program_id(0)
    units = out_ref.shape[1]

    @pl.when(expert == 0)
    def _():
        total[...] = jnp.zeros_like(total)

    for rows in row_chunks(x_ref.shape[0]):
        gate_up = dot_nn(x_ref[rows, :], in_ref[0])
        gate_up_ref[0, rows, :] = gate_up
        gate_vals = gate_up[:, :units]
        silu_gate = gate_vals / (1.0 + jnp.exp(-gate_vals))
        weight = pick_lane(gate_ref[rows, :], expert)
        hidden = (silu_gate * gate_up[:, units:] * weight).astype(jnp.bfloat16)
        hidden_ref[0, rows, :] = hidden
        total[rows, :] += dot_nn(hidden, out_ref[0])

    @pl.when(expert == pl.num_programs(0) - 1)
    def _():
        mix_ref[...] = total[...].astype(mix_ref.dtype)


def experts_forward(tokens, gates_own, w_in, w_out):
    count, width = tokens.shape
    experts, units = w_out.shape[0], w_out.shape[1]
    return pl.pallas_call(
        experts_forward_kernel,
        grid=(experts,),
        in_specs=[
            pl.BlockSpec((count, width), lambda e: (0, 0)),
            pl.BlockSpec((count, LANES), lambda e: (0, 0)),
            pl.BlockSpec((1, width, 2 * units), lambda e: (e, 0, 0)),
            pl.BlockSpec((1, units, width), lambda e: (e, 0, 0)),
        ],
        out_specs=[
            pl.BlockSpec((count, width), lambda e: (0, 0)),
            pl.BlockSpec((1, count, 2 * units), lambda e: (e, 0, 0)),
            pl.BlockSpec((1, count, units), lambda e: (e, 0, 0)),
        ],
        out_shape=[
            jax.ShapeDtypeStruct((count, width), jnp.bfloat16),
            jax.ShapeDtypeStruct((experts, count, 2 * units), jnp.float32),
            jax.ShapeDtypeStruct((experts, count, units), jnp.bfloat16),
        ],
        scratch_shapes=[pltpu.VMEM((count, width), jnp.float32)],
        compiler_params=pltpu.CompilerParams(vmem_limit_bytes=VMEM_BYTES),
        cost_estimate=SMALL_COST,
        name="experts_forward",
    )(tokens, gates_own, w_in, w_out)


def experts_backward_kernel(
    dmix_ref, gate_ref, gate_up_ref, in_ref, out_ref, drows_ref, dgate_up_ref, dgates_ref, total
):
    expert = pl.program_id(0)
    units = out_ref.shape[1]
    lanes = lax.broadcasted_iota(jnp.int32, (1, LANES), 1)

    @pl.when(expert == 0)
    def _():
        total[...] = jnp.zeros_like(total)
        dgates_ref[...] = jnp.zeros_like(dgates_ref)

    for rows in row_chunks(dmix_ref.shape[0]):
        pulled = dot_nt(dmix_ref[rows, :], out_ref[0])
        gate_vals = gate_up_ref[0, rows, :units]
        up_vals = gate_up_ref[0, rows, units:]
        sigmoid = 1.0 / (1.0 + jnp.exp(-gate_vals))
        silu_gate = gate_vals * sigmoid
        weight = pick_lane(gate_ref[rows, :], expert)
        d_up = pulled * silu_gate
        own = jnp.sum(d_up * up_vals, axis=1, keepdims=True)
        own = jnp.where(lanes == expert, own, 0.0)
        d_up = d_up * weight
        d_gate = (pulled * weight) * up_vals * (sigmoid + silu_gate * (1.0 - sigmoid))
        dgate_up_ref[0, rows, :units] = d_gate.astype(jnp.bfloat16)
        dgate_up_ref[0, rows, units:] = d_up.astype(jnp.bfloat16)
        total[rows, :] += dot_nt(dgate_up_ref[0, rows, :], in_ref[0])
        dgates_ref[rows, :] += own

    @pl.when(expert == pl.num_programs(0) - 1)
    def _():
        drows_ref[...] = total[...].astype(drows_ref.dtype)


def experts_backward(d_mix, gates_own, gate_up, w_in, w_out):
    count, width = d_mix.shape
    experts, units = w_out.shape[0], w_out.shape[1]
    return pl.pallas_call(
        experts_backward_kernel,
        grid=(experts,),
        in_specs=[
            pl.BlockSpec((count, width), lambda e: (0, 0)),
            pl.BlockSpec((count, LANES), lambda e: (0, 0)),
            pl.BlockSpec((1, count, 2 * units), lambda e: (e, 0, 0)),
            pl.BlockSpec((1, width, 2 * units), lambda e: (e, 0, 0)),
            pl.BlockSpec((1, units, width), lambda e: (e, 0, 0)),
        ],
        out_specs=[
            pl.BlockSpec((count, width), lambda e: (0, 0)),
            pl.BlockSpec((1, count, 2 * units), lambda e: (e, 0, 0)),
            pl.BlockSpec((count, LANES), lambda e: (0, 0)),
        ],
        out_shape=[
            jax.ShapeDtypeStruct((count, width), jnp.bfloat16),
            jax.ShapeDtypeStruct((experts, count, 2 * units), jnp.bfloat16),
            jax.ShapeDtypeStruct((count, LANES), jnp.float32),
        ],
        scratch_shapes=[pltpu.VMEM((count, width), jnp.float32)],
        compiler_params=pltpu.CompilerParams(vmem_limit_bytes=VMEM_BYTES),
        cost_estimate=SMALL_COST,
        name="experts_backward",
    )(d_mix, gates_own, gate_up, w_in, w_out)


def experts_grads_kernel(outputs, units, order_ref, *refs):
    grads_refs, refs = refs[-outputs:], refs[:-outputs]
    count = len(refs) // 4
    width = refs[0].shape[1]
    grad_in, grad_out = None, None
    for at in range(count):
        x_ref, dmix_ref, dgate_up_ref, hidden_ref = refs[4 * at : 4 * at + 4]
        part_in = dot_tn(x_ref[...], dgate_up_ref[0])
        part_out = dot_tn(hidden_ref[0], dmix_ref[...])
        grad_in = part_in if grad_in is None else grad_in + part_in
        grad_out = part_out if grad_out is None else grad_out + part_out
    grad_in, grad_out = grad_in.astype(jnp.bfloat16), grad_out.astype(jnp.bfloat16)
    tall, short = width // units, grad_out.shape[0] // units

    def put(ref):
        for at in range(units):
            start = at * (tall + short)
            ref[start : start + tall, :] = grad_in[at * tall : (at + 1) * tall]
            ref[start + tall : start + tall + short, :] = grad_out[at * short : (at + 1) * short]

    if outputs == 1:
        put(grads_refs[0].at[0])
        return
    for at in range(outputs):
        pl.when(pl.program_id(0) == at)(functools.partial(put, grads_refs[at]))


def experts_grads(order, chunks, apart, row_units):
    count, width = chunks[0][0].shape
    units = chunks[0][3].shape[2]
    experts = order.shape[0]
    specs = [
        pl.BlockSpec((count, width), lambda e, order: (0, 0)),
        pl.BlockSpec((count, width), lambda e, order: (0, 0)),
        pl.BlockSpec((1, count, 2 * units), lambda e, order: (order[e], 0, 0)),
        pl.BlockSpec((1, count, units), lambda e, order: (order[e], 0, 0)),
    ]
    rows, columns = width + units, 2 * units
    if apart and experts > 1:
        outputs = experts
        out_specs = [pl.BlockSpec((rows, columns), lambda e, order: (0, 0))] * experts
        out_shape = [jax.ShapeDtypeStruct((rows, columns), jnp.bfloat16)] * experts
    else:
        outputs = 1
        out_specs = [pl.BlockSpec((1, rows, columns), lambda e, order: (e, 0, 0))]
        out_shape = [jax.ShapeDtypeStruct((experts, rows, columns), jnp.bfloat16)]
    grads = pl.pallas_call(
        functools.partial(experts_grads_kernel, outputs, row_units),
        grid_spec=pltpu.PrefetchScalarGridSpec(
            num_scalar_prefetch=1,
            grid=(experts,),
            in_specs=specs * len(chunks),
            out_specs=out_specs,
        ),
        out_shape=out_shape,
        compiler_params=pltpu.CompilerParams(vmem_limit_bytes=VMEM_BYTES),
        cost_estimate=SMALL_COST,
        name="experts_grads",
    )(order, *[part for chunk in chunks for part in chunk])
    return [part.reshape(-1, columns) for part in grads]


def widen_kernel(spot_ref, piece_ref, *refs):
    gin_ref, gout_ref = refs[-2:]
    tall = gin_ref.shape[1]
    gin_ref[0] = piece_ref[:tall, :].astype(jnp.float32)
    gout_ref[0] = piece_ref[tall:, :].astype(jnp.float32)


def widen(spot, piece, shapes, units, held):
    rows, columns = shapes[0][1] + shapes[1][1], piece.shape[1]
    unit = rows // units
    return pl.pallas_call(
        widen_kernel,
        grid_spec=pltpu.PrefetchScalarGridSpec(
            num_scalar_prefetch=1,
            grid=(piece.shape[0] // unit,),
            in_specs=[pl.BlockSpec((unit, columns), lambda at, spot: (at, 0))]
            + [pl.BlockSpec(memory_space=pl.ANY)] * len(held),
            out_specs=[
                pl.BlockSpec(
                    (1, shape[1] // units, columns), lambda at, spot: (spot[0], spot[1] + at, 0)
                )
                for shape in shapes
            ],
        ),
        out_shape=[jax.ShapeDtypeStruct(shape, jnp.float32) for shape in shapes],
        input_output_aliases={2 + at: at for at in range(len(held))},
        compiler_params=pltpu.CompilerParams(vmem_limit_bytes=VMEM_BYTES),
        cost_estimate=SMALL_COST,
        name="widen",
    )(spot, piece, *held)


def finish_kernel(spots, widths, piece_ref, query_ref, key_ref, value_ref, output_ref, small_ref):
    query_width, half, kv_width = widths
    rows = piece_ref.shape[1]
    for at, (first, second) in enumerate(spots):
        first_at = slice(first * rows, (first + 1) * rows)
        second_at = slice(second * rows, (second + 1) * rows)
        block = piece_ref[at].astype(jnp.float32)
        query_ref[first_at, :] = block[:, :query_width]
        start = query_width + half
        output_ref[first_at, :half] = block[:, query_width:start]
        small_ref[first_at, :] = block[:, start : start + LANES]
        start = start + LANES
        key_ref[second_at, :] = block[:, start : start + kv_width]
        value_ref[second_at, :] = block[:, start + kv_width : start + 2 * kv_width]
        output_ref[second_at, half:] = block[:, start + 2 * kv_width :]


def finish(pieces, spots, widths):
    count, rows, _ = pieces.shape
    query_width, half, kv_width = widths
    return pl.pallas_call(
        functools.partial(finish_kernel, spots, widths),
        in_specs=[whole_spec()],
        out_specs=[whole_spec()] * 5,
        out_shape=[
            jax.ShapeDtypeStruct((count * rows, columns), jnp.float32)
            for columns in (query_width, kv_width, kv_width, 2 * half, LANES)
        ],
        compiler_params=pltpu.CompilerParams(vmem_limit_bytes=VMEM_BYTES),
        cost_estimate=SMALL_COST,
        name="finish",
    )(pieces)


def attention_grads_kernel(
    sets,
    side_ref, digits_ref, normed_ref, dquery_ref, all_ref, dkv_ref, attended_ref, dbranch_ref,
    gain_ref, router_ref,
    wq_ref, wkv_ref, input_ref, own_ref,
    dnormed_kv_ref, dnormed_query_ref, sent_first, kept_first, sent_second, kept_second,
    first_ref, second_ref
):
    query_width = dquery_ref.shape[1]
    half = dbranch_ref.shape[1] // 2
    kv_width = dkv_ref.shape[1]
    shards, rows = kept_first.shape[0], kept_first.shape[1]

    def gain_of(d_normed, block):
        values = block.astype(jnp.float32)
        scale = lax.rsqrt(jnp.mean(values * values, axis=-1, keepdims=True) + norm_eps)
        return jnp.sum(d_normed * values * scale, axis=0, keepdims=True)

    def put(ref, columns, value):
        ref[:, :, columns] = value.astype(jnp.bfloat16).reshape(shards, 2 * rows, -1)

    d_normed = dot_nt(dquery_ref[...], wq_ref[...])
    dnormed_query_ref[...] = d_normed
    gain = gain_of(d_normed, own_ref[...])
    for start in range(0, all_ref.shape[0], ROW_STEP):
        span = pl.ds(start, ROW_STEP)
        d_normed = dot_nt(dkv_ref[span, :], wkv_ref[...])
        dnormed_kv_ref[span, :] = d_normed.astype(jnp.bfloat16)
        gain = gain + gain_of(d_normed, input_ref[span, :])
    put(second_ref, slice(0, kv_width), dot_tn(all_ref[...], dkv_ref[...]))
    put(first_ref, slice(0, query_width), dot_tn(normed_ref[...], dquery_ref[...]))
    grad_output = dot_tn(attended_ref[...], dbranch_ref[...])
    put(first_ref, slice(query_width, query_width + half), grad_output[:, :half])
    put(second_ref, slice(kv_width, kv_width + half), grad_output[:, half:])
    experts, width = router_ref.shape
    row = lax.broadcasted_iota(jnp.int32, (LANES - experts, width), 0)
    spot = lax.broadcasted_iota(jnp.int32, row.shape, 1) % (2 * rows)
    rest = jnp.where(row == 0, gain, jnp.where(row == 1, gain_ref[...], 0.0))
    for at in range(digits_ref.shape[0]):
        for turn in range(sets):
            here = (row == 2 + at * sets + turn) & (spot == side_ref[1] - 2 * rows * turn)
            rest = jnp.where(here, digits_ref[at], rest)
    small = jnp.concatenate([router_ref[...], rest], 0).T
    put(first_ref, slice(query_width + half, first_ref.shape[2]), small)
    kept_at = pl.ds(pl.multiple_of(side_ref[0] * rows, rows), rows)
    sent_at = pl.ds(pl.multiple_of((1 - side_ref[0]) * rows, rows), rows)
    sent_first[...] = first_ref[:, sent_at, :]
    sent_second[...] = second_ref[:, sent_at, :]
    kept_first[...] = first_ref[:, kept_at, :]
    kept_second[...] = second_ref[:, kept_at, :]


def attention_grads(
    side, digits, sets, shards, normed, d_query, normed_all, d_kv, attended, d_branch, gain, router,
    w_query, w_kv, input_all, hidden_in
):
    width = normed.shape[1]
    half = d_branch.shape[1] // 2
    rows = width // shards // 2
    widths = (d_query.shape[1] + half + LANES, d_kv.shape[1] + half)
    return pl.pallas_call(
        functools.partial(attention_grads_kernel, sets),
        in_specs=[pl.BlockSpec(memory_space=pltpu.SMEM)] * 2 + [whole_spec()] * 12,
        out_specs=[whole_spec()] * 6,
        out_shape=[
            jax.ShapeDtypeStruct(input_all.shape, jnp.bfloat16),
            jax.ShapeDtypeStruct(hidden_in.shape, jnp.float32),
        ]
        + [
            jax.ShapeDtypeStruct((shards, rows, columns), jnp.bfloat16)
            for columns in (widths[0], widths[0], widths[1], widths[1])
        ],
        scratch_shapes=[
            pltpu.VMEM((shards, 2 * rows, columns), jnp.bfloat16) for columns in widths
        ],
        compiler_params=pltpu.CompilerParams(vmem_limit_bytes=VMEM_BYTES),
        cost_estimate=SMALL_COST,
        name="attention_grads",
    )(
        side, digits, normed, d_query, normed_all, d_kv, attended, d_branch, gain, router,
        w_query, w_kv, input_all, hidden_in,
    )


VMEM_BYTES = 60 * 1024 * 1024


def swap_halves(values):
    lanes = lax.broadcasted_iota(jnp.int32, values.shape, 1)
    ahead = pltpu.roll(values, LANES - HEAD_DIM // 2, 1)
    behind = pltpu.roll(values, HEAD_DIM // 2, 1)
    return jnp.where(lanes % HEAD_DIM < HEAD_DIM // 2, ahead, behind)


def stack_heads(block, parity):
    values = block.astype(jnp.float32)
    lanes = lax.broadcasted_iota(jnp.int32, values.shape, 1)
    low = jnp.where(lanes < HEAD_DIM, values, 0.0)
    high = values - low
    if parity == 0:
        high = pltpu.roll(high, HEAD_DIM, 1)
    else:
        low = pltpu.roll(low, HEAD_DIM, 1)
    return jnp.concatenate([low, high], 0).astype(jnp.bfloat16)


def unstack_heads(stacked, parity):
    rows = stacked.shape[0] // 2
    low, high = stacked[:rows], stacked[rows:]
    if parity == 0:
        high = pltpu.roll(high, HEAD_DIM, 1)
    else:
        low = pltpu.roll(low, HEAD_DIM, 1)
    lanes = lax.broadcasted_iota(jnp.int32, low.shape, 1)
    return jnp.where(lanes < HEAD_DIM, low, high)


def lane_block(at):
    return pl.ds(pl.multiple_of(at * LANES, LANES), LANES)


def attention_forward_kernel(
    bias_ref, side_ref, all_ref, own_ref, gain_ref, query_held, query_other, kv_held, kv_other,
    cos_ref, sin_ref, cos_own_ref, sin_own_ref,
    wq_parts, wkv_parts, normed_ref, normed_own_ref, query_ref, key_ref, value_ref, attended_ref, norm_ref, scores
):
    tokens, width = all_ref.shape
    kv_width = key_ref.shape[1]
    key_rows = tokens // bias_ref.shape[0]
    half_rows = query_held.shape[1]
    held_at = pl.ds(pl.multiple_of(side_ref[0] * half_rows, half_rows), half_rows)
    other_at = pl.ds(pl.multiple_of((1 - side_ref[0]) * half_rows, half_rows), half_rows)
    wq_parts[:, held_at, :] = query_held[...]
    wq_parts[:, other_at, :] = query_other[...]
    wkv_parts[:, held_at, :] = kv_held[...]
    wkv_parts[:, other_at, :] = kv_other[...]
    wq_ref = wq_parts.reshape(width, wq_parts.shape[2])
    wkv_ref = wkv_parts.reshape(width, wkv_parts.shape[2])

    def normed_rows(block):
        values = block.astype(jnp.float32)
        scale = lax.rsqrt(jnp.mean(values * values, axis=-1, keepdims=True) + norm_eps)
        return (values * scale * gain_ref[...]).astype(jnp.bfloat16)

    def project(at, carry):
        rows = pl.ds(pl.multiple_of(at * ROW_STEP, ROW_STEP), ROW_STEP)
        normed = normed_rows(all_ref[rows, :])
        normed_ref[rows, :] = normed
        linear = dot_nn(normed, wkv_ref[...])
        for col in range(0, kv_width, LANES):
            part = linear[:, col : col + LANES]
            turned = part * cos_ref[rows, :] + swap_halves(part) * sin_ref[rows, :]
            key_ref[rows, col : col + LANES] = turned.astype(jnp.bfloat16)
        value_ref[rows, :] = linear[:, kv_width:].astype(jnp.bfloat16)
        return carry

    lax.fori_loop(0, tokens // ROW_STEP, project, 0)
    normed_own = normed_rows(own_ref[...])
    normed_own_ref[...] = normed_own
    linear = dot_nn(normed_own, wq_ref[...])
    for col in range(0, wq_ref.shape[1], LANES):
        part = linear[:, col : col + LANES]
        turned = part * cos_own_ref[...] + swap_halves(part) * sin_own_ref[...]
        query_ref[:, col : col + LANES] = (turned.astype(jnp.bfloat16).astype(jnp.float32) * attn_mult).astype(jnp.bfloat16)

    def attend(pair, carry):
        lanes = lane_block(pair)
        turned_values = value_ref[:, lanes].astype(jnp.float32).T.astype(jnp.bfloat16)
        for parity in range(2):
            group = 2 * pair + parity
            stacked = stack_heads(query_ref[:, lane_block(group)], parity)
            top = None
            for at in range(bias_ref.shape[0]):
                rows = pl.ds(at * key_rows, key_rows)
                part = dot_nt(key_ref[rows, lanes], stacked) + bias_ref[at]
                scores[rows, :] = part
                high = jnp.max(part, axis=0, keepdims=True)
                top = high if top is None else jnp.maximum(top, high)
            total, gathered = None, None
            for at in range(bias_ref.shape[0]):
                rows = pl.ds(at * key_rows, key_rows)
                raised = jnp.exp(scores[rows, :] - top)
                part = jnp.sum(raised, axis=0, keepdims=True)
                mixed = dot_nn(
                    turned_values[:, at * key_rows : (at + 1) * key_rows], raised.astype(jnp.bfloat16)
                )
                total = part if total is None else total + part
                gathered = mixed if gathered is None else gathered + mixed
            gathered = (gathered / total).T
            attended_ref[:, lane_block(group)] = unstack_heads(gathered, parity).astype(jnp.bfloat16)
            norm_ref[pl.ds(group, 1), :] = top + jnp.log(total)
        return carry

    lax.fori_loop(0, kv_width // LANES, attend, 0)


def whole_spec():
    return pl.BlockSpec(memory_space=pltpu.VMEM)


def attention_forward(bias, side, input_all, hidden_in, gain, query_pair, kv_pair, tables, tables_own):
    tokens, width = input_all.shape
    rows = hidden_in.shape[0]
    shards, half_rows, query_width = query_pair[0].shape
    kv_width = kv_pair[0].shape[2] // 2
    return pl.pallas_call(
        attention_forward_kernel,
        in_specs=[pl.BlockSpec(memory_space=pltpu.SMEM)] * 2 + [whole_spec()] * 11,
        out_specs=[whole_spec()] * 9,
        out_shape=[
            jax.ShapeDtypeStruct((shards, 2 * half_rows, query_width), jnp.bfloat16),
            jax.ShapeDtypeStruct((shards, 2 * half_rows, 2 * kv_width), jnp.bfloat16),
            jax.ShapeDtypeStruct((tokens, width), jnp.bfloat16),
            jax.ShapeDtypeStruct((rows, width), jnp.bfloat16),
            jax.ShapeDtypeStruct((rows, query_width), jnp.bfloat16),
            jax.ShapeDtypeStruct((tokens, kv_width), jnp.bfloat16),
            jax.ShapeDtypeStruct((tokens, kv_width), jnp.bfloat16),
            jax.ShapeDtypeStruct((rows, query_width), jnp.bfloat16),
            jax.ShapeDtypeStruct((KV_HEADS, 2 * rows), jnp.float32),
        ],
        scratch_shapes=[pltpu.VMEM((tokens, 2 * rows), jnp.float32)],
        compiler_params=pltpu.CompilerParams(vmem_limit_bytes=VMEM_BYTES),
        cost_estimate=SMALL_COST,
        name="attention_forward",
    )(bias, side, input_all, hidden_in, gain, *query_pair, *kv_pair, *tables, *tables_own)


def attention_backward_kernel(
    bias_ref, query_ref, key_ref, value_ref, norm_ref, grad_ref, cos_ref, sin_ref, cos_own_ref, sin_own_ref,
    dquery_ref, dkv_ref, probs, dprobs, dkeys, dvalues
):
    tokens, kv_width = key_ref.shape
    key_rows = tokens // bias_ref.shape[0]

    def pull(pair, carry):
        lanes = lane_block(pair)
        turned_keys = key_ref[:, lanes].astype(jnp.float32).T.astype(jnp.bfloat16)
        for parity in range(2):
            group = 2 * pair + parity
            stacked = stack_heads(query_ref[:, lane_block(group)], parity)
            stacked_grad = stack_heads(grad_ref[:, lane_block(group)], parity)
            log_norm = norm_ref[pl.ds(group, 1), :]
            total = None
            for at in range(bias_ref.shape[0]):
                rows = pl.ds(at * key_rows, key_rows)
                part = dot_nt(key_ref[rows, lanes], stacked) + bias_ref[at]
                prob = jnp.exp(part - log_norm)
                d_prob = dot_nt(value_ref[rows, lanes], stacked_grad)
                probs[rows, :] = prob
                dprobs[rows, :] = d_prob
                d_value = dot_nn(prob.astype(jnp.bfloat16), stacked_grad)
                dvalues[rows, :] = d_value if parity == 0 else dvalues[rows, :] + d_value
                weighted = jnp.sum(prob * d_prob, axis=0, keepdims=True)
                total = weighted if total is None else total + weighted
            d_query = None
            for at in range(bias_ref.shape[0]):
                rows = pl.ds(at * key_rows, key_rows)
                d_score = (probs[rows, :] * (dprobs[rows, :] - total)).astype(jnp.bfloat16)
                d_key = dot_nn(d_score, stacked)
                dkeys[rows, :] = d_key if parity == 0 else dkeys[rows, :] + d_key
                part = dot_nn(turned_keys[:, at * key_rows : (at + 1) * key_rows], d_score)
                d_query = part if d_query is None else d_query + part
            part = unstack_heads(d_query.T, parity) * attn_mult
            turned = part * cos_own_ref[...] - swap_halves(part) * sin_own_ref[...]
            dquery_ref[:, lane_block(group)] = turned.astype(jnp.bfloat16)
        part = dkeys[...]
        turned = part * cos_ref[...] - swap_halves(part) * sin_ref[...]
        dkv_ref[:, lanes] = turned.astype(jnp.bfloat16)
        dkv_ref[:, lane_block(pair + kv_width // LANES)] = dvalues[...].astype(jnp.bfloat16)
        return carry

    lax.fori_loop(0, kv_width // LANES, pull, 0)


def attention_backward(bias, query, key, value, log_norm, grad, tables, tables_own):
    tokens, kv_width = key.shape
    rows, width = query.shape
    return pl.pallas_call(
        attention_backward_kernel,
        in_specs=[pl.BlockSpec(memory_space=pltpu.SMEM)] + [whole_spec()] * 9,
        out_specs=[whole_spec()] * 2,
        out_shape=[
            jax.ShapeDtypeStruct((rows, width), jnp.bfloat16),
            jax.ShapeDtypeStruct((tokens, 2 * kv_width), jnp.bfloat16),
        ],
        scratch_shapes=[
            pltpu.VMEM((tokens, 2 * rows), jnp.float32),
            pltpu.VMEM((tokens, 2 * rows), jnp.float32),
            pltpu.VMEM((tokens, LANES), jnp.float32),
            pltpu.VMEM((tokens, LANES), jnp.float32),
        ],
        compiler_params=pltpu.CompilerParams(vmem_limit_bytes=VMEM_BYTES),
        cost_estimate=SMALL_COST,
        name="attention_backward",
    )(bias, query, key, value, log_norm, grad, *tables, *tables_own)


def exchange(block, bit):
    count = lax.axis_size("rep")
    return lax.ppermute(block, "rep", [(at, at ^ bit) for at in range(count)])


def side_of(bit):
    return (lax.axis_index("rep") // bit) % 2


def after(value, *others):
    return lax.optimization_barrier((value, *others))[0]


def slices_of(parts, start, size, axis):
    return [
        lax.dynamic_slice_in_dim(part, base + start, size, axis)
        for part, base in ((part if isinstance(part, tuple) else (part, 0)) for part in parts)
    ]


def add_parts(parts):
    total = parts[0].astype(jnp.float32)
    for part in parts[1:]:
        total = total + part.astype(jnp.float32)
    return total.astype(jnp.bfloat16)


def halve(parts, bit, axis, length=None):
    length = parts[0].shape[axis] if length is None else length
    half = length // 2
    side = side_of(bit)
    sent = slices_of(parts, (1 - side) * half, half, axis)
    sent = sent[0] if len(sent) == 1 else add_parts(sent)
    kept = slices_of(parts, side * half, half, axis)
    return sent, kept + [exchange(sent, bit)]


def double(block, bit, axis):
    size = block.shape[axis]
    side = side_of(bit)
    held = lax.concatenate([block, block], axis)
    return lax.dynamic_update_slice_in_dim(held, exchange(block, bit), (1 - side) * size, axis)


def rep_bits():
    count = lax.axis_size("rep")
    return [1 << at for at in range(count.bit_length() - 1)]


def body(
    hidden_in,
    valid_mask,
    teacher,
    routes,
    attn_norm,
    w_query,
    w_key,
    w_value,
    w_output,
    ffn_norm,
    router,
    w_in,
    w_out,
):
    row_count, model_width = hidden_in.shape
    shard_count = lax.axis_size("shard")
    seq_tokens = row_count * shard_count
    all_tokens = seq_tokens * lax.axis_size("rep")
    shard_at = lax.axis_index("shard")
    tables = rope_tables(jnp.arange(seq_tokens, dtype=jnp.int32))
    tables_own = tuple(
        lax.dynamic_slice_in_dim(table, shard_at * row_count, row_count, 0) for table in tables
    )
    key_blocks = jnp.arange(seq_tokens // BLOCK, dtype=jnp.int32)
    bias = jnp.where(key_blocks <= shard_at * row_count // BLOCK, 0.0, very_low)
    bits = rep_bits()
    near, far = bits[0], bits[1:]

    def gather(block):
        return lax.all_gather(block, "shard", axis=0, tiled=True)

    def scatter(block):
        return lax.psum_scatter(block, "shard", scatter_dimension=0, tiled=True)

    kv_width = w_key.shape[1]
    query_width = w_query.shape[1]
    half_width = w_output.shape[1] // 2
    own_rows = w_query.shape[0]
    piece_rows = own_rows // lax.axis_size("rep")

    def piece_of(block, order):
        index = 0
        for at, bit in enumerate(order):
            index = index + side_of(bit) * (1 << at)
        return lax.dynamic_slice_in_dim(block, index * piece_rows, piece_rows, 0)

    order_first, order_second = far + [near], far[::-1] + [near]
    w_kv = jnp.concatenate([w_key, w_value], 1)
    input_all = gather(hidden_in)
    valid_float = valid_mask.astype(jnp.float32)
    expert_count = router.shape[1]
    small_parts = [
        jnp.concatenate([attn_norm, ffn_norm, router.reshape(-1)]).reshape(1, -1),
        routes.astype(jnp.bfloat16).reshape(1, -1),
        jnp.sum(valid_float).astype(jnp.bfloat16).reshape(1, 1),
    ]
    small_size, routes_size = small_parts[0].size, small_parts[1].size
    pieces = lax.all_gather(
        jnp.concatenate([piece_of(w_query, order_first), piece_of(w_kv, order_second)], 1),
        "shard",
        axis=0,
    )
    query_full = pieces[..., :query_width]
    kv_full = pieces[..., query_width:]
    for bit_first, bit_second in zip(order_first[:-1], order_second[:-1]):
        query_full = double(query_full, bit_first, 1)
        kv_full = double(kv_full, bit_second, 1)
    small_parts = after(jnp.concatenate(small_parts, 1), query_full, kv_full, *tables, *tables_own)
    small_all = gather(small_parts)
    query_pair = query_full, exchange(query_full, near)
    kv_pair = kv_full, exchange(kv_full, near)
    near_rows = own_rows // 2
    output_half = lax.dynamic_slice_in_dim(w_output, side_of(near) * near_rows, near_rows, 0)
    output_half = lax.all_gather(after(output_half, query_pair[0], kv_pair[0]), "shard", axis=0)
    gain_attn = small_all[:, :own_rows].reshape(-1).astype(jnp.float32)
    gain_ffn = small_all[:, own_rows : 2 * own_rows].reshape(-1)
    router_full = small_all[:, 2 * own_rows : small_size].reshape(-1, expert_count)
    routes_all = small_all[:, small_size : small_size + routes_size]
    valid_count = jnp.broadcast_to(jnp.sum(small_all[:, small_size + routes_size].astype(jnp.float32)), (8, LANES))
    for bit in bits:
        valid_count = valid_count + exchange(valid_count, bit)
    valid_count = valid_count[0, 0]
    input_float = hidden_in.astype(jnp.float32)
    scale_attn = rms_scale(input_float)
    (
        query_full, kv_full, normed_all, normed_attn, query_rows, keys_all, values_all, attended, log_norm
    ) = attention_forward(
        bias, jnp.reshape(side_of(near), (1,)), input_all, hidden_in, gain_attn[None],
        query_pair, kv_pair, tables, tables_own,
    )
    query_full = query_full.reshape(model_width, query_width)
    kv_full = kv_full.reshape(model_width, 2 * kv_width)
    output_half, attended = lax.optimization_barrier((output_half, attended))
    output_full = double(output_half, near, 1).reshape(own_rows * shard_count, -1)
    branch = dot_nn(attended, output_full)
    middle = input_float + resid_mult * branch
    scale_ffn = rms_scale(middle)
    normed_ffn = (middle * scale_ffn * gain_ffn).astype(jnp.bfloat16)
    own_experts = w_in.shape[0]
    expert_ids = jnp.arange(expert_count, dtype=jnp.bfloat16)
    chunk_rows = row_count // CHUNKS
    spans = [slice(at * chunk_rows, (at + 1) * chunk_rows) for at in range(CHUNKS)]
    tokens_in = [gather(normed_ffn[span]) for span in spans]
    routes_all = routes_all.reshape(shard_count, row_count, -1)
    gates, forward = [], []
    for span, tokens in zip(spans, tokens_in):
        logits = dot_nn(tokens, router_full)
        routes_part = routes_all[:, span].reshape(shard_count * chunk_rows, -1)
        chosen = jnp.any(routes_part[..., None] == expert_ids, 1)
        masked = jnp.where(chosen, logits, very_low)
        raised = jnp.where(chosen, jnp.exp(masked - jnp.max(masked, -1, keepdims=True)), 0.0)
        gates_part = raised / jnp.sum(raised, -1, keepdims=True)
        gates_own = lax.dynamic_slice_in_dim(gates_part, shard_at * own_experts, own_experts, 1)
        gates_own = jnp.pad(gates_own, ((0, 0), (0, LANES - own_experts)))
        gates.append(lax.dynamic_slice_in_dim(gates_part, shard_at * chunk_rows, chunk_rows, 0))
        if not forward:
            gates_own = after(gates_own, valid_count)
        forward.append((gates_own, *experts_forward(tokens, gates_own, w_in, w_out)))
    gates = jnp.concatenate(gates, 0)
    results, d_results, d_mix_out, d_mix_in, own_loss = [], [], [], [], 0.0
    for span, (_, mix_part, _, _) in zip(spans, forward):
        mixture = scatter(mix_part)
        if d_mix_out:
            mixture = after(mixture, d_mix_out[-1])
        mixture = mixture.astype(jnp.float32)
        result_part = middle[span] + resid_mult * mixture
        deviation = result_part - teacher[span].astype(jnp.float32)
        masked = valid_float[span, None] * deviation
        d_result = masked * (all_tokens / (2.0 * valid_count))
        results.append(result_part.astype(jnp.bfloat16))
        d_results.append(d_result)
        d_mix_out.append((resid_mult * d_result).astype(jnp.bfloat16))
        d_mix_in.append(gather(d_mix_out[-1]))
        own_loss = own_loss + jnp.sum(masked * deviation)
    d_result = jnp.concatenate(d_results, 0)
    kept_experts = own_experts // 2
    grad_rows = model_width + w_out.shape[1]
    flat_rows = kept_experts * grad_rows
    row_units = 2 * grad_rows // (flat_rows >> len(far))
    side = side_of(near)
    digits, rest = [], own_loss
    for _ in range(3):
        digits.append(lax.reduce_precision(rest, 8, 7))
        rest = rest - digits[-1]
    device = lax.axis_index("rep") * shard_count + shard_at
    sets = -(-lax.axis_size("rep") * shard_count // own_rows)
    place, digits = jnp.stack([side, device]), jnp.stack(digits)
    columns = w_in.shape[2]
    shapes = (own_experts, model_width, columns), (own_experts, grad_rows - model_width, columns)
    half_units = row_units * flat_rows // grad_rows // 4
    second_at = (1, 0) if kept_experts > 1 else (0, 2 * half_units)
    targets = {}
    for path, bit, (expert, unit) in ((0, far[0], (0, 0)), (1, far[-1], second_at)):
        for across in range(2):
            half = side_of(bit) if across == 0 else 1 - side_of(bit)
            for core in range(2):
                owner = side if core == 0 else 1 - side
                targets[path, across, core] = jnp.stack(
                    [owner * kept_experts + expert, unit + half * half_units]
                )
    d_rows, d_gates, backward = [], [], []
    for d_mix, (gates_own, _, gate_up, hidden_gated), tokens in zip(d_mix_in, forward, tokens_in):
        if not backward:
            gates_own = after(gates_own, place, digits, *targets.values())
        d_rows_part, d_gate_up, d_gates_part = experts_backward(
            d_mix, gates_own, gate_up, w_in, w_out
        )
        d_rows.append(scatter(d_rows_part))
        d_gates.append(d_gates_part)
        backward.append((tokens, d_mix, d_gate_up, hidden_gated))
    first_rows = d_rows[0]
    d_rows = jnp.concatenate(d_rows, 0).astype(jnp.float32)
    order = jnp.arange(kept_experts, dtype=jnp.int32)
    order_sent = order + (1 - side) * kept_experts
    order_kept = order + side * kept_experts
    sent = experts_grads(order_sent, backward, True, row_units)
    other = [exchange(part, near) for part in sent]
    kept = experts_grads(after(order_kept, *sent, first_rows), backward, False, row_units)[0]
    half_rows = flat_rows // 2
    if kept_experts > 1:
        other_first = jnp.concatenate(other[: kept_experts // 2], 0)
        other_second = jnp.concatenate(other[kept_experts // 2 :], 0)
        spots = ((kept, 0), (other_first, 0)), ((kept, half_rows), (other_second, 0))
    else:
        spots = ((kept, 0), (other[0], 0)), ((kept, half_rows), (other[0], half_rows))
    moe_sent_first, moe_first = halve(spots[0], far[0], 0, half_rows)
    moe_sent_second, moe_second = halve(spots[1], far[-1], 0, half_rows)
    d_gates = [after(part, moe_sent_first, moe_sent_second) for part in d_gates]
    d_gates = [
        part[:, :own_experts].reshape(shard_count, chunk_rows, own_experts) for part in d_gates
    ]
    d_gates = jnp.concatenate(d_gates, 1).reshape(shard_count * row_count, own_experts)
    d_gates = lax.all_to_all(d_gates, "shard", split_axis=0, concat_axis=1, tiled=True)
    d_rows = after(d_rows, moe_sent_first, moe_sent_second)
    d_logits = (gates * (d_gates - jnp.sum(gates * d_gates, -1, keepdims=True))).astype(
        jnp.bfloat16
    )
    d_normed_ffn = d_rows + dot_nt(d_logits, router_full)
    grad_router = dot_tn(d_logits, normed_ffn)
    d_norm_mid, grad_gain_ffn = norm_back(d_normed_ffn, middle, scale_ffn, gain_ffn)
    d_middle = d_result + d_norm_mid
    d_branch = (resid_mult * d_middle).astype(jnp.bfloat16)
    d_attended = dot_nt(d_branch, output_full).astype(
        jnp.bfloat16
    )
    query_grad_rows, kv_grad_all = attention_backward(
        bias, query_rows, keys_all, values_all, log_norm, d_attended, tables, tables_own
    )
    query_grad_rows, kv_grad_all, moe_first[-1], moe_second[-1] = lax.optimization_barrier(
        (query_grad_rows, kv_grad_all, moe_first[-1], moe_second[-1])
    )
    d_normed_kv, d_normed_query, sent_first, kept_first, sent_second, kept_second = attention_grads(
        place, digits, sets, shard_count, normed_attn, query_grad_rows,
        normed_all, kv_grad_all, attended, d_branch, grad_gain_ffn[None], grad_router,
        query_full, kv_full, input_all, hidden_in
    )
    used = expert_count + 2
    kv_scattered = scatter(d_normed_kv)
    d_normed_query = after(d_normed_query, sent_first, sent_second)
    d_normed_attn = kv_scattered.astype(jnp.float32) + d_normed_query
    d_norm_in, _ = norm_back(d_normed_attn, input_float, scale_attn, gain_attn)
    d_input = d_middle + d_norm_in
    for bit_first, bit_second in zip(far[1:], far[::-1][1:]):
        _, moe_first = halve(moe_first, bit_first, 0)
        _, moe_second = halve(moe_second, bit_second, 0)
    sent_first, sent_second, moe_first[-1], moe_second[-1] = lax.optimization_barrier(
        (sent_first, sent_second, moe_first[-1], moe_second[-1])
    )
    moe_first, moe_second = add_parts(moe_first), add_parts(moe_second)
    sent_first, sent_second = lax.optimization_barrier(
        (sent_first, sent_second, moe_first, moe_second)
    )[:2]
    first = [kept_first, exchange(sent_first, near)]
    second = [kept_second, exchange(sent_second, near)]
    for bit_first, bit_second in zip(far[:0:-1], far[:-1]):
        moe_first = double(moe_first, bit_first, 0)
        moe_second = double(moe_second, bit_second, 0)
    for bit_first, bit_second in zip(far, far[::-1]):
        _, first = halve(first, bit_first, 1)
        _, second = halve(second, bit_second, 1)
        if bit_first == far[0]:
            first[-1] = after(first[-1], moe_first, moe_second)
            second[-1] = after(second[-1], moe_first, moe_second)
    first[-1] = after(first[-1], kv_scattered)
    moe_first = after(moe_first, first[-1], second[-1])
    moe_second = after(moe_second, first[-1], second[-1])
    own_first, own_second = moe_first, moe_second
    far_first, far_second = exchange(own_first, far[0]), exchange(own_second, far[-1])
    near_own = exchange(own_first, near), exchange(own_second, near)
    split_at = first[0].shape[2]
    joined = jnp.concatenate([add_parts(first), add_parts(second)], 2)
    joined = lax.psum_scatter(joined, "shard", scatter_dimension=0)
    def put(held, piece, *where):
        return widen(targets[where], piece, shapes, row_units, held)

    held = []
    held = put(held, own_first, 0, 0, 0)
    held = put(held, own_second, 1, 0, 0)
    *held, joined, d_input = lax.optimization_barrier((*held, joined, d_input))
    gathered = lax.all_gather(joined, "rep", axis=0)
    held = put(held, near_own[0], 0, 0, 1)
    held = put(held, near_own[1], 1, 0, 1)
    *held, far_first, far_second = lax.optimization_barrier((*held, far_first, far_second))
    near_far = exchange(far_first, near), exchange(far_second, near)
    held = put(held, far_first, 0, 1, 0)
    held = put(held, far_second, 1, 1, 0)
    held = put(held, near_far[0], 0, 1, 1)
    held = put(held, near_far[1], 1, 1, 1)
    sum_in, sum_out = held
    def row_of(at, order):
        return sum(((at // bit) % 2) << (len(order) - 1 - turn) for turn, bit in enumerate(order))

    pairs = tuple(
        (row_of(at, [near] + far), row_of(at, [near] + far[::-1])) for at in range(lax.axis_size("rep"))
    )
    sum_query, sum_key, sum_value, sum_output, sum_small = finish(
        gathered, pairs, (query_width, half_width, kv_width)
    )
    loss = jnp.sum(sum_small[:, used : used + 3 * sets]) / (model_width * valid_count)
    return (
        jnp.concatenate(results, 0),
        loss,
        d_input,
        sum_small[:, expert_count],
        sum_query,
        sum_key,
        sum_value,
        sum_output,
        sum_small[:, expert_count + 1],
        sum_small[:, :expert_count],
        sum_in,
        sum_out,
    )


def solution(mesh):
    in_specs = (
        P(("rep", "shard"), None),
        P(("rep", "shard")),
        P(("rep", "shard"), None),
        P(("rep", "shard"), None),
        P("shard"),
        P("shard", None),
        P("shard", None),
        P("shard", None),
        P("shard", None),
        P("shard"),
        P("shard", None),
        P("shard", None, None),
        P("shard", None, None),
    )
    out_specs = (
        P(("rep", "shard"), None),
        P(),
        P(("rep", "shard"), None),
        P("shard"),
        P("shard", None),
        P("shard", None),
        P("shard", None),
        P("shard", None),
        P("shard"),
        P("shard", None),
        P("shard", None, None),
        P("shard", None, None),
    )
    return jax.shard_map(body, mesh=mesh, in_specs=in_specs, out_specs=out_specs, check_vma=False)
```

```python
import functools

import jax
import jax.numpy as jnp
from jax import lax
from jax.experimental import pallas as pl
from jax.experimental.pallas import tpu as pltpu
from jax.sharding import PartitionSpec as P

HEADS = 16
KV_HEADS = 8
HEAD_DIM = 64
TOP = 8
BLOCK = 256
CHUNKS = 2
SMALL_COST = pl.CostEstimate(flops=1000000, bytes_accessed=100000, transcendentals=0)


norm_eps = 1e-06
resid_mult = 0.22
attn_mult = 0.015625
rope_base = 10000.0
very_low = -1e30


def rope_tables(positions):
    half_dim = HEAD_DIM // 2
    frequency = rope_base ** (-jnp.arange(half_dim, dtype=jnp.float32) / half_dim)
    angles = positions.astype(jnp.float32)[:, None] * frequency[None, :]
    cosine, sine = jnp.cos(angles), jnp.sin(angles)
    return (
        jnp.concatenate([cosine] * 4, 1),
        jnp.concatenate([-sine, sine, -sine, sine], 1),
    )


def rms_scale(values):
    return lax.rsqrt(jnp.mean(values * values, axis=-1, keepdims=True) + norm_eps)


def norm_back(d_normed, values, scale_vals, gain_vec):
    scaled_grad = d_normed * gain_vec
    d_gain = jnp.sum(d_normed * values * scale_vals, 0)
    d_values = scale_vals * (
        scaled_grad
        - values * scale_vals * scale_vals * jnp.mean(scaled_grad * values, axis=-1, keepdims=True)
    )
    return (d_values, d_gain)


LANES = 128
ROW_STEP = 256
EXPERT_STEP = 512


def row_chunks(count):
    step = min(count, EXPERT_STEP)
    return [pl.ds(at, step) for at in range(0, count, step)]


def pick_lane(values, lane):
    lanes = lax.broadcasted_iota(jnp.int32, values.shape, 1)
    return jnp.sum(jnp.where(lanes == lane, values, 0.0), axis=1, keepdims=True)


def dot_nn(left, right):
    return jnp.dot(left, right, preferred_element_type=jnp.float32)


def dot_nt(left, right):
    return lax.dot_general(left, right, (((1,), (1,)), ((), ())), preferred_element_type=jnp.float32)


def dot_tn(left, right):
    return lax.dot_general(left, right, (((0,), (0,)), ((), ())), preferred_element_type=jnp.float32)


def experts_forward_kernel(x_ref, gate_ref, in_ref, out_ref, mix_ref, gate_up_ref, hidden_ref, total):
    expert = pl.program_id(0)
    units = out_ref.shape[1]

    @pl.when(expert == 0)
    def _():
        total[...] = jnp.zeros_like(total)

    for rows in row_chunks(x_ref.shape[0]):
        gate_up = dot_nn(x_ref[rows, :], in_ref[0])
        gate_up_ref[0, rows, :] = gate_up
        gate_vals = gate_up[:, :units]
        silu_gate = gate_vals / (1.0 + jnp.exp(-gate_vals))
        weight = pick_lane(gate_ref[rows, :], expert)
        hidden = (silu_gate * gate_up[:, units:] * weight).astype(jnp.bfloat16)
        hidden_ref[0, rows, :] = hidden
        total[rows, :] += dot_nn(hidden, out_ref[0])

    @pl.when(expert == pl.num_programs(0) - 1)
    def _():
        mix_ref[...] = total[...].astype(mix_ref.dtype)


def experts_forward(tokens, gates_own, w_in, w_out):
    count, width = tokens.shape
    experts, units = w_out.shape[0], w_out.shape[1]
    return pl.pallas_call(
        experts_forward_kernel,
        grid=(experts,),
        in_specs=[
            pl.BlockSpec((count, width), lambda e: (0, 0)),
            pl.BlockSpec((count, LANES), lambda e: (0, 0)),
            pl.BlockSpec((1, width, 2 * units), lambda e: (e, 0, 0)),
            pl.BlockSpec((1, units, width), lambda e: (e, 0, 0)),
        ],
        out_specs=[
            pl.BlockSpec((count, width), lambda e: (0, 0)),
            pl.BlockSpec((1, count, 2 * units), lambda e: (e, 0, 0)),
            pl.BlockSpec((1, count, units), lambda e: (e, 0, 0)),
        ],
        out_shape=[
            jax.ShapeDtypeStruct((count, width), jnp.bfloat16),
            jax.ShapeDtypeStruct((experts, count, 2 * units), jnp.float32),
            jax.ShapeDtypeStruct((experts, count, units), jnp.bfloat16),
        ],
        scratch_shapes=[pltpu.VMEM((count, width), jnp.float32)],
        compiler_params=pltpu.CompilerParams(vmem_limit_bytes=VMEM_BYTES),
        cost_estimate=SMALL_COST,
        name="experts_forward",
    )(tokens, gates_own, w_in, w_out)


def experts_backward_kernel(
    dmix_ref, gate_ref, gate_up_ref, in_ref, out_ref, drows_ref, dgate_up_ref, dgates_ref, total
):
    expert = pl.program_id(0)
    units = out_ref.shape[1]
    lanes = lax.broadcasted_iota(jnp.int32, (1, LANES), 1)

    @pl.when(expert == 0)
    def _():
        total[...] = jnp.zeros_like(total)
        dgates_ref[...] = jnp.zeros_like(dgates_ref)

    for rows in row_chunks(dmix_ref.shape[0]):
        pulled = dot_nt(dmix_ref[rows, :], out_ref[0])
        gate_vals = gate_up_ref[0, rows, :units]
        up_vals = gate_up_ref[0, rows, units:]
        sigmoid = 1.0 / (1.0 + jnp.exp(-gate_vals))
        silu_gate = gate_vals * sigmoid
        weight = pick_lane(gate_ref[rows, :], expert)
        d_up = pulled * silu_gate
        own = jnp.sum(d_up * up_vals, axis=1, keepdims=True)
        own = jnp.where(lanes == expert, own, 0.0)
        d_up = d_up * weight
        d_gate = (pulled * weight) * up_vals * (sigmoid + silu_gate * (1.0 - sigmoid))
        dgate_up_ref[0, rows, :units] = d_gate.astype(jnp.bfloat16)
        dgate_up_ref[0, rows, units:] = d_up.astype(jnp.bfloat16)
        total[rows, :] += dot_nt(dgate_up_ref[0, rows, :], in_ref[0])
        dgates_ref[rows, :] += own

    @pl.when(expert == pl.num_programs(0) - 1)
    def _():
        drows_ref[...] = total[...].astype(drows_ref.dtype)


def experts_backward(d_mix, gates_own, gate_up, w_in, w_out):
    count, width = d_mix.shape
    experts, units = w_out.shape[0], w_out.shape[1]
    return pl.pallas_call(
        experts_backward_kernel,
        grid=(experts,),
        in_specs=[
            pl.BlockSpec((count, width), lambda e: (0, 0)),
            pl.BlockSpec((count, LANES), lambda e: (0, 0)),
            pl.BlockSpec((1, count, 2 * units), lambda e: (e, 0, 0)),
            pl.BlockSpec((1, width, 2 * units), lambda e: (e, 0, 0)),
            pl.BlockSpec((1, units, width), lambda e: (e, 0, 0)),
        ],
        out_specs=[
            pl.BlockSpec((count, width), lambda e: (0, 0)),
            pl.BlockSpec((1, count, 2 * units), lambda e: (e, 0, 0)),
            pl.BlockSpec((count, LANES), lambda e: (0, 0)),
        ],
        out_shape=[
            jax.ShapeDtypeStruct((count, width), jnp.bfloat16),
            jax.ShapeDtypeStruct((experts, count, 2 * units), jnp.bfloat16),
            jax.ShapeDtypeStruct((count, LANES), jnp.float32),
        ],
        scratch_shapes=[pltpu.VMEM((count, width), jnp.float32)],
        compiler_params=pltpu.CompilerParams(vmem_limit_bytes=VMEM_BYTES),
        cost_estimate=SMALL_COST,
        name="experts_backward",
    )(d_mix, gates_own, gate_up, w_in, w_out)


def experts_grads_kernel(outputs, units, based, order_ref, *refs):
    grads_refs, refs = refs[-outputs:], refs[:-outputs]
    base_ref, refs = (refs[0], refs[1:]) if based else (None, refs)
    count = len(refs) // 4
    width = refs[0].shape[1]
    grad_in, grad_out = None, None
    for at in range(count):
        x_ref, dmix_ref, dgate_up_ref, hidden_ref = refs[4 * at : 4 * at + 4]
        part_in = dot_tn(x_ref[...], dgate_up_ref[0])
        part_out = dot_tn(hidden_ref[0], dmix_ref[...])
        grad_in = part_in if grad_in is None else grad_in + part_in
        grad_out = part_out if grad_out is None else grad_out + part_out
    tall, short = width // units, grad_out.shape[0] // units

    def put(ref):
        for at in range(units):
            start = at * (tall + short)
            for first, size, value in (
                (start, tall, grad_in[at * tall : (at + 1) * tall]),
                (start + tall, short, grad_out[at * short : (at + 1) * short]),
            ):
                span = slice(first, first + size)
                if based:
                    value = value + base_ref[0, span, :].astype(jnp.float32)
                ref[span, :] = value.astype(jnp.bfloat16)

    if outputs == 1:
        put(grads_refs[0].at[0])
        return
    for at in range(outputs):
        pl.when(pl.program_id(0) == at)(functools.partial(put, grads_refs[at]))


def experts_grads(order, chunks, apart, row_units, base=None, base_at=0):
    count, width = chunks[0][0].shape
    units = chunks[0][3].shape[2]
    experts = order.shape[0]
    specs = [
        pl.BlockSpec((count, width), lambda e, order: (0, 0)),
        pl.BlockSpec((count, width), lambda e, order: (0, 0)),
        pl.BlockSpec((1, count, 2 * units), lambda e, order: (order[e], 0, 0)),
        pl.BlockSpec((1, count, units), lambda e, order: (order[e], 0, 0)),
    ]
    rows, columns = width + units, 2 * units
    base_specs = []
    if base is not None:
        base_specs = [pl.BlockSpec((1, rows, columns), lambda e, order: (base_at + e, 0, 0))]
    if apart and experts > 1:
        outputs = experts
        out_specs = [pl.BlockSpec((rows, columns), lambda e, order: (0, 0))] * experts
        out_shape = [jax.ShapeDtypeStruct((rows, columns), jnp.bfloat16)] * experts
    else:
        outputs = 1
        out_specs = [pl.BlockSpec((1, rows, columns), lambda e, order: (e, 0, 0))]
        out_shape = [jax.ShapeDtypeStruct((experts, rows, columns), jnp.bfloat16)]
    grads = pl.pallas_call(
        functools.partial(experts_grads_kernel, outputs, row_units, base is not None),
        grid_spec=pltpu.PrefetchScalarGridSpec(
            num_scalar_prefetch=1,
            grid=(experts,),
            in_specs=base_specs + specs * len(chunks),
            out_specs=out_specs,
        ),
        out_shape=out_shape,
        compiler_params=pltpu.CompilerParams(vmem_limit_bytes=VMEM_BYTES),
        cost_estimate=SMALL_COST,
        name="experts_grads",
    )(order, *([] if base is None else [base]), *[part for chunk in chunks for part in chunk])
    return grads


def widen_kernel(steps, spot_ref, first_ref, second_ref, *refs):
    gin_ref, gout_ref = refs[-2:]
    tall = gin_ref.shape[1]

    def put(piece_ref):
        gin_ref[0] = piece_ref[:tall, :].astype(jnp.float32)
        gout_ref[0] = piece_ref[tall:, :].astype(jnp.float32)

    at = pl.program_id(0)
    pl.when(at < steps)(functools.partial(put, first_ref))
    pl.when(at >= steps)(functools.partial(put, second_ref))


def widen(spot, first, second, shapes, units, held):
    rows, columns = shapes[0][1] + shapes[1][1], first.shape[1]
    unit = rows // units
    steps = first.shape[0] // unit

    def place(at, spot):
        late = at >= steps
        expert = jnp.where(late, spot[2], spot[0])
        return (expert, jnp.where(late, spot[3] + at - steps, spot[1] + at), 0)

    return pl.pallas_call(
        functools.partial(widen_kernel, steps),
        grid_spec=pltpu.PrefetchScalarGridSpec(
            num_scalar_prefetch=1,
            grid=(2 * steps,),
            in_specs=[
                pl.BlockSpec((unit, columns), lambda at, spot: (jnp.minimum(at, steps - 1), 0)),
                pl.BlockSpec((unit, columns), lambda at, spot: (jnp.maximum(at - steps, 0), 0)),
            ]
            + [pl.BlockSpec(memory_space=pl.ANY)] * len(held),
            out_specs=[
                pl.BlockSpec((1, shape[1] // units, columns), place) for shape in shapes
            ],
        ),
        out_shape=[jax.ShapeDtypeStruct(shape, jnp.float32) for shape in shapes],
        input_output_aliases={3 + at: at for at in range(len(held))},
        compiler_params=pltpu.CompilerParams(vmem_limit_bytes=20 * MIB),
        cost_estimate=SMALL_COST,
        name="widen",
    )(spot, first, second, *held)


def finish_kernel(
    spots, widths, digits, piece_ref, query_ref, key_ref, value_ref, output_ref, router_ref, gain_ref,
    loss_ref, small_ref
):
    query_width, half, kv_width = widths
    experts = router_ref.shape[1]
    rows = piece_ref.shape[1]
    for at, (first, second) in enumerate(spots):
        first_at = slice(first * rows, (first + 1) * rows)
        second_at = slice(second * rows, (second + 1) * rows)
        block = piece_ref[at].astype(jnp.float32)
        query_ref[first_at, :] = block[:, :query_width]
        start = query_width + half
        output_ref[first_at, :half] = block[:, query_width:start]
        small_ref[first_at, :] = block[:, start : start + LANES]
        start = start + LANES
        key_ref[second_at, :] = block[:, start : start + kv_width]
        value_ref[second_at, :] = block[:, start + kv_width : start + 2 * kv_width]
        output_ref[second_at, half:] = block[:, start + 2 * kv_width :]
    router_ref[...] = small_ref[:, :experts]
    turned = small_ref[...].T
    gain_ref[...] = turned[experts : experts + 8]
    row = lax.broadcasted_iota(jnp.int32, turned.shape, 0) - experts - 2
    loss = jnp.sum(jnp.where((row >= 0) & (row < digits), turned, 0.0))
    loss_ref[...] = jnp.full(loss_ref.shape, loss, jnp.float32)


def finish(pieces, spots, widths, digits, experts):
    count, rows, _ = pieces.shape
    query_width, half, kv_width = widths
    return pl.pallas_call(
        functools.partial(finish_kernel, spots, widths, digits),
        in_specs=[whole_spec()],
        out_specs=[whole_spec()] * 7,
        out_shape=[
            jax.ShapeDtypeStruct((count * rows, columns), jnp.float32)
            for columns in (query_width, kv_width, kv_width, 2 * half, experts)
        ]
        + [jax.ShapeDtypeStruct((8, columns), jnp.float32) for columns in (count * rows, LANES)],
        scratch_shapes=[pltpu.VMEM((count * rows, LANES), jnp.float32)],
        compiler_params=pltpu.CompilerParams(vmem_limit_bytes=20 * MIB),
        cost_estimate=SMALL_COST,
        name="finish",
    )(pieces)


def attention_grads_kernel(
    sets,
    side_ref, digits_ref, normed_ref, dquery_ref, all_ref, dkv_ref, attended_ref, dbranch_ref,
    gain_ref, router_ref,
    wq_ref, wkv_ref, input_ref, own_ref,
    dnormed_kv_ref, dnormed_query_ref, sent_first, kept_first, sent_second, kept_second,
    first_ref, second_ref
):
    query_width = dquery_ref.shape[1]
    half = dbranch_ref.shape[1] // 2
    kv_width = dkv_ref.shape[1]
    shards, rows = kept_first.shape[0], kept_first.shape[1]

    def gain_of(d_normed, block):
        values = block.astype(jnp.float32)
        scale = lax.rsqrt(jnp.mean(values * values, axis=-1, keepdims=True) + norm_eps)
        return jnp.sum(d_normed * values * scale, axis=0, keepdims=True)

    def put(ref, columns, value):
        ref[:, :, columns] = value.astype(jnp.bfloat16).reshape(shards, 2 * rows, -1)

    d_normed = dot_nt(dquery_ref[...], wq_ref[...])
    dnormed_query_ref[...] = d_normed
    gain = gain_of(d_normed, own_ref[...])
    for start in range(0, all_ref.shape[0], ROW_STEP):
        span = pl.ds(start, ROW_STEP)
        d_normed = dot_nt(dkv_ref[span, :], wkv_ref[...])
        dnormed_kv_ref[span, :] = d_normed.astype(jnp.bfloat16)
        gain = gain + gain_of(d_normed, input_ref[span, :])
    put(second_ref, slice(0, kv_width), dot_tn(all_ref[...], dkv_ref[...]))
    put(first_ref, slice(0, query_width), dot_tn(normed_ref[...], dquery_ref[...]))
    grad_output = dot_tn(attended_ref[...], dbranch_ref[...])
    put(first_ref, slice(query_width, query_width + half), grad_output[:, :half])
    put(second_ref, slice(kv_width, kv_width + half), grad_output[:, half:])
    experts, width = router_ref.shape
    row = lax.broadcasted_iota(jnp.int32, (LANES - experts, width), 0)
    spot = lax.broadcasted_iota(jnp.int32, row.shape, 1) % (2 * rows)
    rest = jnp.where(row == 0, gain, jnp.where(row == 1, gain_ref[...], 0.0))
    for at in range(digits_ref.shape[0]):
        for turn in range(sets):
            here = (row == 2 + at * sets + turn) & (spot == side_ref[1] - 2 * rows * turn)
            rest = jnp.where(here, digits_ref[at], rest)
    small = jnp.concatenate([router_ref[...], rest], 0).T
    put(first_ref, slice(query_width + half, first_ref.shape[2]), small)
    kept_at = pl.ds(pl.multiple_of(side_ref[0] * rows, rows), rows)
    sent_at = pl.ds(pl.multiple_of((1 - side_ref[0]) * rows, rows), rows)
    sent_first[...] = first_ref[:, sent_at, :]
    sent_second[...] = second_ref[:, sent_at, :]
    kept_first[...] = first_ref[:, kept_at, :]
    kept_second[...] = second_ref[:, kept_at, :]


def attention_grads(
    side, digits, sets, shards, normed, d_query, normed_all, d_kv, attended, d_branch, gain, router,
    w_query, w_kv, input_all, hidden_in
):
    width = normed.shape[1]
    half = d_branch.shape[1] // 2
    rows = width // shards // 2
    widths = (d_query.shape[1] + half + LANES, d_kv.shape[1] + half)
    return pl.pallas_call(
        functools.partial(attention_grads_kernel, sets),
        in_specs=[pl.BlockSpec(memory_space=pltpu.SMEM)] * 2 + [whole_spec()] * 12,
        out_specs=[whole_spec()] * 6,
        out_shape=[
            jax.ShapeDtypeStruct(input_all.shape, jnp.bfloat16),
            jax.ShapeDtypeStruct(hidden_in.shape, jnp.float32),
        ]
        + [
            jax.ShapeDtypeStruct((shards, rows, columns), jnp.bfloat16)
            for columns in (widths[0], widths[0], widths[1], widths[1])
        ],
        scratch_shapes=[
            pltpu.VMEM((shards, 2 * rows, columns), jnp.bfloat16) for columns in widths
        ],
        compiler_params=pltpu.CompilerParams(vmem_limit_bytes=46 * MIB),
        cost_estimate=SMALL_COST,
        name="attention_grads",
    )(
        side, digits, normed, d_query, normed_all, d_kv, attended, d_branch, gain, router,
        w_query, w_kv, input_all, hidden_in,
    )


MIB = 1024 * 1024
VMEM_BYTES = 60 * MIB


def swap_halves(values):
    lanes = lax.broadcasted_iota(jnp.int32, values.shape, 1)
    ahead = pltpu.roll(values, LANES - HEAD_DIM // 2, 1)
    behind = pltpu.roll(values, HEAD_DIM // 2, 1)
    return jnp.where(lanes % HEAD_DIM < HEAD_DIM // 2, ahead, behind)


def stack_heads(block, parity):
    values = block.astype(jnp.float32)
    lanes = lax.broadcasted_iota(jnp.int32, values.shape, 1)
    low = jnp.where(lanes < HEAD_DIM, values, 0.0)
    high = values - low
    if parity == 0:
        high = pltpu.roll(high, HEAD_DIM, 1)
    else:
        low = pltpu.roll(low, HEAD_DIM, 1)
    return jnp.concatenate([low, high], 0).astype(jnp.bfloat16)


def unstack_heads(stacked, parity):
    rows = stacked.shape[0] // 2
    low, high = stacked[:rows], stacked[rows:]
    if parity == 0:
        high = pltpu.roll(high, HEAD_DIM, 1)
    else:
        low = pltpu.roll(low, HEAD_DIM, 1)
    lanes = lax.broadcasted_iota(jnp.int32, low.shape, 1)
    return jnp.where(lanes < HEAD_DIM, low, high)


def lane_block(at):
    return pl.ds(pl.multiple_of(at * LANES, LANES), LANES)


def attention_forward_kernel(
    bias_ref, side_ref, all_ref, own_ref, gain_ref, query_held, query_other, kv_held, kv_other,
    cos_ref, sin_ref, cos_own_ref, sin_own_ref,
    wq_parts, wkv_parts, normed_ref, normed_own_ref, query_ref, key_ref, value_ref, attended_ref, norm_ref, scores
):
    tokens, width = all_ref.shape
    kv_width = key_ref.shape[1]
    key_rows = tokens // bias_ref.shape[0]
    half_rows = query_held.shape[1]
    held_at = pl.ds(pl.multiple_of(side_ref[0] * half_rows, half_rows), half_rows)
    other_at = pl.ds(pl.multiple_of((1 - side_ref[0]) * half_rows, half_rows), half_rows)
    wq_parts[:, held_at, :] = query_held[...]
    wq_parts[:, other_at, :] = query_other[...]
    wkv_parts[:, held_at, :] = kv_held[...]
    wkv_parts[:, other_at, :] = kv_other[...]
    wq_ref = wq_parts.reshape(width, wq_parts.shape[2])
    wkv_ref = wkv_parts.reshape(width, wkv_parts.shape[2])

    def normed_rows(block):
        values = block.astype(jnp.float32)
        scale = lax.rsqrt(jnp.mean(values * values, axis=-1, keepdims=True) + norm_eps)
        return (values * scale * gain_ref[...]).astype(jnp.bfloat16)

    def project(at, carry):
        rows = pl.ds(pl.multiple_of(at * ROW_STEP, ROW_STEP), ROW_STEP)
        normed = normed_rows(all_ref[rows, :])
        normed_ref[rows, :] = normed
        linear = dot_nn(normed, wkv_ref[...])
        for col in range(0, kv_width, LANES):
            part = linear[:, col : col + LANES]
            turned = part * cos_ref[rows, :] + swap_halves(part) * sin_ref[rows, :]
            key_ref[rows, col : col + LANES] = turned.astype(jnp.bfloat16)
        value_ref[rows, :] = linear[:, kv_width:].astype(jnp.bfloat16)
        return carry

    lax.fori_loop(0, tokens // ROW_STEP, project, 0)
    normed_own = normed_rows(own_ref[...])
    normed_own_ref[...] = normed_own
    linear = dot_nn(normed_own, wq_ref[...])
    for col in range(0, wq_ref.shape[1], LANES):
        part = linear[:, col : col + LANES]
        turned = part * cos_own_ref[...] + swap_halves(part) * sin_own_ref[...]
        query_ref[:, col : col + LANES] = (turned.astype(jnp.bfloat16).astype(jnp.float32) * attn_mult).astype(jnp.bfloat16)

    def attend(pair, carry):
        lanes = lane_block(pair)
        turned_values = value_ref[:, lanes].astype(jnp.float32).T.astype(jnp.bfloat16)
        for parity in range(2):
            group = 2 * pair + parity
            stacked = stack_heads(query_ref[:, lane_block(group)], parity)
            top = None
            for at in range(bias_ref.shape[0]):
                rows = pl.ds(at * key_rows, key_rows)
                part = dot_nt(key_ref[rows, lanes], stacked) + bias_ref[at]
                scores[rows, :] = part
                high = jnp.max(part, axis=0, keepdims=True)
                top = high if top is None else jnp.maximum(top, high)
            total, gathered = None, None
            for at in range(bias_ref.shape[0]):
                rows = pl.ds(at * key_rows, key_rows)
                raised = jnp.exp(scores[rows, :] - top)
                part = jnp.sum(raised, axis=0, keepdims=True)
                mixed = dot_nn(
                    turned_values[:, at * key_rows : (at + 1) * key_rows], raised.astype(jnp.bfloat16)
                )
                total = part if total is None else total + part
                gathered = mixed if gathered is None else gathered + mixed
            gathered = (gathered / total).T
            attended_ref[:, lane_block(group)] = unstack_heads(gathered, parity).astype(jnp.bfloat16)
            norm_ref[pl.ds(group, 1), :] = top + jnp.log(total)
        return carry

    lax.fori_loop(0, kv_width // LANES, attend, 0)


def whole_spec():
    return pl.BlockSpec(memory_space=pltpu.VMEM)


def attention_forward(bias, side, input_all, hidden_in, gain, query_pair, kv_pair, tables, tables_own):
    tokens, width = input_all.shape
    rows = hidden_in.shape[0]
    shards, half_rows, query_width = query_pair[0].shape
    kv_width = kv_pair[0].shape[2] // 2
    return pl.pallas_call(
        attention_forward_kernel,
        in_specs=[pl.BlockSpec(memory_space=pltpu.SMEM)] * 2 + [whole_spec()] * 11,
        out_specs=[whole_spec()] * 9,
        out_shape=[
            jax.ShapeDtypeStruct((shards, 2 * half_rows, query_width), jnp.bfloat16),
            jax.ShapeDtypeStruct((shards, 2 * half_rows, 2 * kv_width), jnp.bfloat16),
            jax.ShapeDtypeStruct((tokens, width), jnp.bfloat16),
            jax.ShapeDtypeStruct((rows, width), jnp.bfloat16),
            jax.ShapeDtypeStruct((rows, query_width), jnp.bfloat16),
            jax.ShapeDtypeStruct((tokens, kv_width), jnp.bfloat16),
            jax.ShapeDtypeStruct((tokens, kv_width), jnp.bfloat16),
            jax.ShapeDtypeStruct((rows, query_width), jnp.bfloat16),
            jax.ShapeDtypeStruct((KV_HEADS, 2 * rows), jnp.float32),
        ],
        scratch_shapes=[pltpu.VMEM((tokens, 2 * rows), jnp.float32)],
        compiler_params=pltpu.CompilerParams(vmem_limit_bytes=VMEM_BYTES),
        cost_estimate=SMALL_COST,
        name="attention_forward",
    )(bias, side, input_all, hidden_in, gain, *query_pair, *kv_pair, *tables, *tables_own)


def attention_backward_kernel(
    bias_ref, query_ref, key_ref, value_ref, norm_ref, grad_ref, cos_ref, sin_ref, cos_own_ref, sin_own_ref,
    dquery_ref, dkv_ref, probs, dprobs, dkeys, dvalues
):
    tokens, kv_width = key_ref.shape
    key_rows = tokens // bias_ref.shape[0]

    def pull(pair, carry):
        lanes = lane_block(pair)
        turned_keys = key_ref[:, lanes].astype(jnp.float32).T.astype(jnp.bfloat16)
        for parity in range(2):
            group = 2 * pair + parity
            stacked = stack_heads(query_ref[:, lane_block(group)], parity)
            stacked_grad = stack_heads(grad_ref[:, lane_block(group)], parity)
            log_norm = norm_ref[pl.ds(group, 1), :]
            total = None
            for at in range(bias_ref.shape[0]):
                rows = pl.ds(at * key_rows, key_rows)
                part = dot_nt(key_ref[rows, lanes], stacked) + bias_ref[at]
                prob = jnp.exp(part - log_norm)
                d_prob = dot_nt(value_ref[rows, lanes], stacked_grad)
                probs[rows, :] = prob
                dprobs[rows, :] = d_prob
                d_value = dot_nn(prob.astype(jnp.bfloat16), stacked_grad)
                dvalues[rows, :] = d_value if parity == 0 else dvalues[rows, :] + d_value
                weighted = jnp.sum(prob * d_prob, axis=0, keepdims=True)
                total = weighted if total is None else total + weighted
            d_query = None
            for at in range(bias_ref.shape[0]):
                rows = pl.ds(at * key_rows, key_rows)
                d_score = (probs[rows, :] * (dprobs[rows, :] - total)).astype(jnp.bfloat16)
                d_key = dot_nn(d_score, stacked)
                dkeys[rows, :] = d_key if parity == 0 else dkeys[rows, :] + d_key
                part = dot_nn(turned_keys[:, at * key_rows : (at + 1) * key_rows], d_score)
                d_query = part if d_query is None else d_query + part
            part = unstack_heads(d_query.T, parity) * attn_mult
            turned = part * cos_own_ref[...] - swap_halves(part) * sin_own_ref[...]
            dquery_ref[:, lane_block(group)] = turned.astype(jnp.bfloat16)
        part = dkeys[...]
        turned = part * cos_ref[...] - swap_halves(part) * sin_ref[...]
        dkv_ref[:, lanes] = turned.astype(jnp.bfloat16)
        dkv_ref[:, lane_block(pair + kv_width // LANES)] = dvalues[...].astype(jnp.bfloat16)
        return carry

    lax.fori_loop(0, kv_width // LANES, pull, 0)


def attention_backward(bias, query, key, value, log_norm, grad, tables, tables_own):
    tokens, kv_width = key.shape
    rows, width = query.shape
    return pl.pallas_call(
        attention_backward_kernel,
        in_specs=[pl.BlockSpec(memory_space=pltpu.SMEM)] + [whole_spec()] * 9,
        out_specs=[whole_spec()] * 2,
        out_shape=[
            jax.ShapeDtypeStruct((rows, width), jnp.bfloat16),
            jax.ShapeDtypeStruct((tokens, 2 * kv_width), jnp.bfloat16),
        ],
        scratch_shapes=[
            pltpu.VMEM((tokens, 2 * rows), jnp.float32),
            pltpu.VMEM((tokens, 2 * rows), jnp.float32),
            pltpu.VMEM((tokens, LANES), jnp.float32),
            pltpu.VMEM((tokens, LANES), jnp.float32),
        ],
        compiler_params=pltpu.CompilerParams(vmem_limit_bytes=22 * MIB),
        cost_estimate=SMALL_COST,
        name="attention_backward",
    )(bias, query, key, value, log_norm, grad, *tables, *tables_own)


def exchange(block, bit):
    count = lax.axis_size("rep")
    return lax.ppermute(block, "rep", [(at, at ^ bit) for at in range(count)])


def side_of(bit):
    return (lax.axis_index("rep") // bit) % 2


def after(value, *others):
    return lax.optimization_barrier((value, *others))[0]


def slices_of(parts, start, size, axis):
    return [
        lax.dynamic_slice_in_dim(part, base + start, size, axis)
        for part, base in ((part if isinstance(part, tuple) else (part, 0)) for part in parts)
    ]


def add_parts(parts):
    total = parts[0].astype(jnp.float32)
    for part in parts[1:]:
        total = total + part.astype(jnp.float32)
    return total.astype(jnp.bfloat16)


def halve(parts, bit, axis, length=None):
    length = parts[0].shape[axis] if length is None else length
    half = length // 2
    side = side_of(bit)
    sent = slices_of(parts, (1 - side) * half, half, axis)
    sent = sent[0] if len(sent) == 1 else add_parts(sent)
    kept = slices_of(parts, side * half, half, axis)
    return sent, kept + [exchange(sent, bit)]


def double(block, bit, axis):
    size = block.shape[axis]
    side = side_of(bit)
    held = lax.concatenate([block, block], axis)
    return lax.dynamic_update_slice_in_dim(held, exchange(block, bit), (1 - side) * size, axis)


def rep_bits():
    count = lax.axis_size("rep")
    return [1 << at for at in range(count.bit_length() - 1)]


def body(
    hidden_in,
    valid_mask,
    teacher,
    routes,
    attn_norm,
    w_query,
    w_key,
    w_value,
    w_output,
    ffn_norm,
    router,
    w_in,
    w_out,
):
    row_count, model_width = hidden_in.shape
    shard_count = lax.axis_size("shard")
    seq_tokens = row_count * shard_count
    all_tokens = seq_tokens * lax.axis_size("rep")
    shard_at = lax.axis_index("shard")
    tables = rope_tables(jnp.arange(seq_tokens, dtype=jnp.int32))
    tables_own = tuple(
        lax.dynamic_slice_in_dim(table, shard_at * row_count, row_count, 0) for table in tables
    )
    key_blocks = jnp.arange(seq_tokens // BLOCK, dtype=jnp.int32)
    bias = jnp.where(key_blocks <= shard_at * row_count // BLOCK, 0.0, very_low)
    bits = rep_bits()
    near, far = bits[0], bits[1:]

    def gather(block):
        return lax.all_gather(block, "shard", axis=0, tiled=True)

    def scatter(block):
        return lax.psum_scatter(block, "shard", scatter_dimension=0, tiled=True)

    kv_width = w_key.shape[1]
    query_width = w_query.shape[1]
    half_width = w_output.shape[1] // 2
    own_rows = w_query.shape[0]
    piece_rows = own_rows // lax.axis_size("rep")

    def piece_of(block, order):
        index = 0
        for at, bit in enumerate(order):
            index = index + side_of(bit) * (1 << at)
        return lax.dynamic_slice_in_dim(block, index * piece_rows, piece_rows, 0)

    order_first, order_second = far + [near], far[::-1] + [near]
    w_kv = jnp.concatenate([w_key, w_value], 1)
    input_all = gather(hidden_in)
    valid_float = valid_mask.astype(jnp.float32)
    expert_count = router.shape[1]
    small_parts = [
        jnp.concatenate([attn_norm, ffn_norm, router.reshape(-1)]).reshape(1, -1),
        routes.astype(jnp.bfloat16).reshape(1, -1),
        jnp.sum(valid_float).astype(jnp.bfloat16).reshape(1, 1),
    ]
    small_size, routes_size = small_parts[0].size, small_parts[1].size
    pieces = lax.all_gather(
        jnp.concatenate([piece_of(w_query, order_first), piece_of(w_kv, order_second)], 1),
        "shard",
        axis=0,
    )
    query_full = pieces[..., :query_width]
    kv_full = pieces[..., query_width:]
    for bit_first, bit_second in zip(order_first[:-1], order_second[:-1]):
        query_full = double(query_full, bit_first, 1)
        kv_full = double(kv_full, bit_second, 1)
    small_parts = after(jnp.concatenate(small_parts, 1), query_full, kv_full, *tables, *tables_own)
    small_all = gather(small_parts)
    query_pair = query_full, exchange(query_full, near)
    kv_pair = kv_full, exchange(kv_full, near)
    near_rows = own_rows // 2
    output_half = lax.dynamic_slice_in_dim(w_output, side_of(near) * near_rows, near_rows, 0)
    output_half = lax.all_gather(after(output_half, query_pair[0], kv_pair[0]), "shard", axis=0)
    gain_attn = small_all[:, :own_rows].reshape(-1).astype(jnp.float32)
    gain_ffn = small_all[:, own_rows : 2 * own_rows].reshape(-1)
    router_full = small_all[:, 2 * own_rows : small_size].reshape(-1, expert_count)
    routes_all = small_all[:, small_size : small_size + routes_size]
    valid_count = jnp.broadcast_to(jnp.sum(small_all[:, small_size + routes_size].astype(jnp.float32)), (8, LANES))
    for bit in bits:
        valid_count = valid_count + exchange(valid_count, bit)
    valid_count = valid_count[0, 0]
    input_float = hidden_in.astype(jnp.float32)
    scale_attn = rms_scale(input_float)
    (
        query_full, kv_full, normed_all, normed_attn, query_rows, keys_all, values_all, attended, log_norm
    ) = attention_forward(
        bias, jnp.reshape(side_of(near), (1,)), input_all, hidden_in, gain_attn[None],
        query_pair, kv_pair, tables, tables_own,
    )
    query_full = query_full.reshape(model_width, query_width)
    kv_full = kv_full.reshape(model_width, 2 * kv_width)
    output_half, attended = lax.optimization_barrier((output_half, attended))
    output_full = double(output_half, near, 1).reshape(own_rows * shard_count, -1)
    branch = dot_nn(attended, output_full)
    middle = input_float + resid_mult * branch
    scale_ffn = rms_scale(middle)
    normed_ffn = (middle * scale_ffn * gain_ffn).astype(jnp.bfloat16)
    own_experts = w_in.shape[0]
    expert_ids = jnp.arange(expert_count, dtype=jnp.bfloat16)
    chunk_rows = row_count // CHUNKS
    spans = [slice(at * chunk_rows, (at + 1) * chunk_rows) for at in range(CHUNKS)]
    tokens_in = [gather(normed_ffn[span]) for span in spans]
    routes_all = routes_all.reshape(shard_count, row_count, -1)
    gates, forward = [], []
    for span, tokens in zip(spans, tokens_in):
        logits = dot_nn(tokens, router_full)
        routes_part = routes_all[:, span].reshape(shard_count * chunk_rows, -1)
        chosen = jnp.any(routes_part[..., None] == expert_ids, 1)
        masked = jnp.where(chosen, logits, very_low)
        raised = jnp.where(chosen, jnp.exp(masked - jnp.max(masked, -1, keepdims=True)), 0.0)
        gates_part = raised / jnp.sum(raised, -1, keepdims=True)
        gates_own = lax.dynamic_slice_in_dim(gates_part, shard_at * own_experts, own_experts, 1)
        gates_own = jnp.pad(gates_own, ((0, 0), (0, LANES - own_experts)))
        gates.append(lax.dynamic_slice_in_dim(gates_part, shard_at * chunk_rows, chunk_rows, 0))
        if not forward:
            gates_own = after(gates_own, valid_count)
        forward.append((gates_own, *experts_forward(tokens, gates_own, w_in, w_out)))
    gates = jnp.concatenate(gates, 0)
    results, d_results, d_mix_out, d_mix_in, own_loss = [], [], [], [], 0.0
    for span, (_, mix_part, _, _) in zip(spans, forward):
        mixture = scatter(mix_part)
        if d_mix_out:
            mixture = after(mixture, d_mix_out[-1])
        mixture = mixture.astype(jnp.float32)
        result_part = middle[span] + resid_mult * mixture
        deviation = result_part - teacher[span].astype(jnp.float32)
        masked = valid_float[span, None] * deviation
        d_result = masked * (all_tokens / (2.0 * valid_count))
        results.append(result_part.astype(jnp.bfloat16))
        d_results.append(d_result)
        d_mix_out.append((resid_mult * d_result).astype(jnp.bfloat16))
        d_mix_in.append(gather(d_mix_out[-1]))
        own_loss = own_loss + jnp.sum(masked * deviation)
    d_result = jnp.concatenate(d_results, 0)
    kept_experts = own_experts // 2
    grad_rows = model_width + w_out.shape[1]
    flat_rows = kept_experts * grad_rows
    row_units = 2 * grad_rows // (flat_rows >> len(far))
    side = side_of(near)
    digits, rest = [], own_loss
    for _ in range(3):
        digits.append(lax.reduce_precision(rest, 8, 7))
        rest = rest - digits[-1]
    device = lax.axis_index("rep") * shard_count + shard_at
    sets = -(-lax.axis_size("rep") * shard_count // own_rows)
    place, digits = jnp.stack([side, device]), jnp.stack(digits)
    columns = w_in.shape[2]
    shapes = (own_experts, model_width, columns), (own_experts, grad_rows - model_width, columns)
    half_units = row_units * flat_rows // grad_rows // 4
    second_at = (1, 0) if kept_experts > 1 else (0, 2 * half_units)
    targets = {}
    for across in range(2):
        for core in range(2):
            spot = []
            for bit, (expert, unit) in ((far[0], (0, 0)), (far[-1], second_at)):
                half = side_of(bit) if across == 0 else 1 - side_of(bit)
                owner = side if core == 0 else 1 - side
                spot += [owner * kept_experts + expert, unit + half * half_units]
            targets[across, core] = jnp.stack(spot)
    order = jnp.arange(kept_experts, dtype=jnp.int32)
    order_sent = order + (1 - side) * kept_experts
    order_kept = order + side * kept_experts
    d_rows, d_gates, backward = [], [], []
    for d_mix, (gates_own, _, gate_up, hidden_gated), tokens in zip(d_mix_in, forward, tokens_in):
        if not backward:
            gates_own = after(gates_own, place, digits, *targets.values())
        if len(backward) == CHUNKS - 1:
            order_all = jnp.concatenate([order_sent, order_kept])
            partial_grads = experts_grads(order_all, backward, False, row_units)[0]
            gates_own = after(gates_own, partial_grads)
        d_rows_part, d_gate_up, d_gates_part = experts_backward(
            d_mix, gates_own, gate_up, w_in, w_out
        )
        d_rows.append(scatter(d_rows_part))
        d_gates.append(d_gates_part)
        backward.append((tokens, d_mix, d_gate_up, hidden_gated))
    first_rows = d_rows[0]
    d_rows = jnp.concatenate(d_rows, 0).astype(jnp.float32)
    sent = experts_grads(order_sent, backward[-1:], True, row_units, partial_grads, 0)
    sent = [part.reshape(-1, columns) for part in sent]
    other = [exchange(part, near) for part in sent]
    kept = experts_grads(
        after(order_kept, *sent), backward[-1:], False, row_units, partial_grads, kept_experts
    )
    kept = after(kept[0].reshape(-1, columns), first_rows)
    half_rows = flat_rows // 2
    if kept_experts > 1:
        other_first = jnp.concatenate(other[: kept_experts // 2], 0)
        other_second = jnp.concatenate(other[kept_experts // 2 :], 0)
        spots = ((kept, 0), (other_first, 0)), ((kept, half_rows), (other_second, 0))
    else:
        spots = ((kept, 0), (other[0], 0)), ((kept, half_rows), (other[0], half_rows))
    moe_sent_first, moe_first = halve(spots[0], far[0], 0, half_rows)
    moe_sent_second, moe_second = halve(spots[1], far[-1], 0, half_rows)
    d_gates = [after(part, moe_sent_first, moe_sent_second) for part in d_gates]
    d_gates = [
        part[:, :own_experts].reshape(shard_count, chunk_rows, own_experts) for part in d_gates
    ]
    d_gates = jnp.concatenate(d_gates, 1).reshape(shard_count * row_count, own_experts)
    d_gates = lax.all_to_all(d_gates, "shard", split_axis=0, concat_axis=1, tiled=True)
    d_rows = after(d_rows, moe_sent_first, moe_sent_second)
    d_logits = (gates * (d_gates - jnp.sum(gates * d_gates, -1, keepdims=True))).astype(
        jnp.bfloat16
    )
    d_normed_ffn = d_rows + dot_nt(d_logits, router_full)
    grad_router = dot_tn(d_logits, normed_ffn)
    d_norm_mid, grad_gain_ffn = norm_back(d_normed_ffn, middle, scale_ffn, gain_ffn)
    d_middle = d_result + d_norm_mid
    d_branch = (resid_mult * d_middle).astype(jnp.bfloat16)
    d_attended = dot_nt(d_branch, output_full).astype(
        jnp.bfloat16
    )
    query_grad_rows, kv_grad_all = attention_backward(
        bias, query_rows, keys_all, values_all, log_norm, d_attended, tables, tables_own
    )
    query_grad_rows, kv_grad_all, moe_first[-1], moe_second[-1] = lax.optimization_barrier(
        (query_grad_rows, kv_grad_all, moe_first[-1], moe_second[-1])
    )
    d_normed_kv, d_normed_query, sent_first, kept_first, sent_second, kept_second = attention_grads(
        place, digits, sets, shard_count, normed_attn, query_grad_rows,
        normed_all, kv_grad_all, attended, d_branch, grad_gain_ffn[None], grad_router,
        query_full, kv_full, input_all, hidden_in
    )
    kv_scattered = scatter(d_normed_kv)
    d_normed_query = after(d_normed_query, sent_first, sent_second)
    d_normed_attn = kv_scattered.astype(jnp.float32) + d_normed_query
    d_norm_in, _ = norm_back(d_normed_attn, input_float, scale_attn, gain_attn)
    d_input = d_middle + d_norm_in
    for bit_first, bit_second in zip(far[1:], far[::-1][1:]):
        _, moe_first = halve(moe_first, bit_first, 0)
        _, moe_second = halve(moe_second, bit_second, 0)
    sent_first, sent_second, moe_first[-1], moe_second[-1] = lax.optimization_barrier(
        (sent_first, sent_second, moe_first[-1], moe_second[-1])
    )
    moe_first, moe_second = add_parts(moe_first), add_parts(moe_second)
    sent_first, sent_second = lax.optimization_barrier(
        (sent_first, sent_second, moe_first, moe_second)
    )[:2]
    first = [kept_first, exchange(sent_first, near)]
    second = [kept_second, exchange(sent_second, near)]
    for bit_first, bit_second in zip(far[:0:-1], far[:-1]):
        moe_first = double(moe_first, bit_first, 0)
        moe_second = double(moe_second, bit_second, 0)
    for bit_first, bit_second in zip(far, far[::-1]):
        _, first = halve(first, bit_first, 1)
        _, second = halve(second, bit_second, 1)
        if bit_first == far[0]:
            first[-1] = after(first[-1], moe_first, moe_second)
            second[-1] = after(second[-1], moe_first, moe_second)
    first[-1] = after(first[-1], kv_scattered)
    moe_first = after(moe_first, first[-1], second[-1])
    moe_second = after(moe_second, first[-1], second[-1])
    own_first, own_second = moe_first, moe_second
    far_first, far_second = exchange(own_first, far[0]), exchange(own_second, far[-1])
    near_own = exchange(own_first, near), exchange(own_second, near)
    split_at = first[0].shape[2]
    joined = jnp.concatenate([add_parts(first), add_parts(second)], 2)
    joined = lax.psum_scatter(joined, "shard", scatter_dimension=0)
    def put(held, pieces, *where):
        return widen(targets[where], *pieces, shapes, row_units, held)

    held = put([], (own_first, own_second), 0, 0)
    held = put(held, near_own, 0, 1)
    *held, joined, d_input = lax.optimization_barrier((*held, joined, d_input))
    gathered = lax.all_gather(joined, "rep", axis=0)
    *held, far_first, far_second = lax.optimization_barrier((*held, far_first, far_second))
    near_far = exchange(far_first, near), exchange(far_second, near)
    held = put(held, (far_first, far_second), 1, 0)
    held = put(held, near_far, 1, 1)
    sum_in, sum_out = held

    def row_of(at, order):
        return sum(((at // bit) % 2) << (len(order) - 1 - turn) for turn, bit in enumerate(order))

    pairs = tuple(
        (row_of(at, [near] + far), row_of(at, [near] + far[::-1])) for at in range(lax.axis_size("rep"))
    )
    sum_query, sum_key, sum_value, sum_output, sum_router, sum_gains, loss = finish(
        gathered, pairs, (query_width, half_width, kv_width), 3 * sets, expert_count
    )
    loss = loss[0, 0] / (model_width * valid_count)
    return (
        jnp.concatenate(results, 0),
        loss,
        d_input,
        sum_gains[0],
        sum_query,
        sum_key,
        sum_value,
        sum_output,
        sum_gains[1],
        sum_router,
        sum_in,
        sum_out,
    )


def solution(mesh):
    in_specs = (
        P(("rep", "shard"), None),
        P(("rep", "shard")),
        P(("rep", "shard"), None),
        P(("rep", "shard"), None),
        P("shard"),
        P("shard", None),
        P("shard", None),
        P("shard", None),
        P("shard", None),
        P("shard"),
        P("shard", None),
        P("shard", None, None),
        P("shard", None, None),
    )
    out_specs = (
        P(("rep", "shard"), None),
        P(),
        P(("rep", "shard"), None),
        P("shard"),
        P("shard", None),
        P("shard", None),
        P("shard", None),
        P("shard", None),
        P("shard"),
        P("shard", None),
        P("shard", None, None),
        P("shard", None, None),
    )
    return jax.shard_map(body, mesh=mesh, in_specs=in_specs, out_specs=out_specs, check_vma=False)
```

```python
import functools

import jax
import jax.numpy as jnp
from jax import lax
from jax.experimental import pallas as pl
from jax.experimental.pallas import tpu as pltpu
from jax.sharding import PartitionSpec as P

HEADS = 16
KV_HEADS = 8
HEAD_DIM = 64
TOP = 8
BLOCK = 256
CHUNKS = 2
SMALL_COST = pl.CostEstimate(flops=1000000, bytes_accessed=100000, transcendentals=0)


norm_eps = 1e-06
resid_mult = 0.22
attn_mult = 0.015625
rope_base = 10000.0
very_low = -1e30


def rope_tables(positions):
    half_dim = HEAD_DIM // 2
    frequency = rope_base ** (-jnp.arange(half_dim, dtype=jnp.float32) / half_dim)
    angles = positions.astype(jnp.float32)[:, None] * frequency[None, :]
    cosine, sine = jnp.cos(angles), jnp.sin(angles)
    return (
        jnp.concatenate([cosine] * 4, 1),
        jnp.concatenate([-sine, sine, -sine, sine], 1),
    )


def rms_scale(values):
    return lax.rsqrt(jnp.mean(values * values, axis=-1, keepdims=True) + norm_eps)


def norm_back(d_normed, values, scale_vals, gain_vec):
    scaled_grad = d_normed * gain_vec
    d_gain = jnp.sum(d_normed * values * scale_vals, 0)
    d_values = scale_vals * (
        scaled_grad
        - values * scale_vals * scale_vals * jnp.mean(scaled_grad * values, axis=-1, keepdims=True)
    )
    return (d_values, d_gain)


LANES = 128
ROW_STEP = 256
EXPERT_STEP = 512


def row_chunks(count):
    step = min(count, EXPERT_STEP)
    return [pl.ds(at, step) for at in range(0, count, step)]


def pick_lane(values, lane):
    lanes = lax.broadcasted_iota(jnp.int32, values.shape, 1)
    return jnp.sum(jnp.where(lanes == lane, values, 0.0), axis=1, keepdims=True)


def dot_nn(left, right):
    return jnp.dot(left, right, preferred_element_type=jnp.float32)


def dot_nt(left, right):
    return lax.dot_general(left, right, (((1,), (1,)), ((), ())), preferred_element_type=jnp.float32)


def dot_tn(left, right):
    return lax.dot_general(left, right, (((0,), (0,)), ((), ())), preferred_element_type=jnp.float32)


def experts_forward_kernel(x_ref, gate_ref, in_ref, out_ref, mix_ref, gate_up_ref, hidden_ref, total):
    expert = pl.program_id(0)
    units = out_ref.shape[1]

    @pl.when(expert == 0)
    def _():
        total[...] = jnp.zeros_like(total)

    for rows in row_chunks(x_ref.shape[0]):
        gate_up = dot_nn(x_ref[rows, :], in_ref[0])
        gate_up_ref[0, rows, :] = gate_up
        gate_vals = gate_up[:, :units]
        silu_gate = gate_vals / (1.0 + jnp.exp(-gate_vals))
        weight = pick_lane(gate_ref[rows, :], expert)
        hidden = (silu_gate * gate_up[:, units:] * weight).astype(jnp.bfloat16)
        hidden_ref[0, rows, :] = hidden
        total[rows, :] += dot_nn(hidden, out_ref[0])

    @pl.when(expert == pl.num_programs(0) - 1)
    def _():
        mix_ref[...] = total[...].astype(mix_ref.dtype)


def experts_forward(tokens, gates_own, w_in, w_out):
    count, width = tokens.shape
    experts, units = w_out.shape[0], w_out.shape[1]
    return pl.pallas_call(
        experts_forward_kernel,
        grid=(experts,),
        in_specs=[
            pl.BlockSpec((count, width), lambda e: (0, 0)),
            pl.BlockSpec((count, LANES), lambda e: (0, 0)),
            pl.BlockSpec((1, width, 2 * units), lambda e: (e, 0, 0)),
            pl.BlockSpec((1, units, width), lambda e: (e, 0, 0)),
        ],
        out_specs=[
            pl.BlockSpec((count, width), lambda e: (0, 0)),
            pl.BlockSpec((1, count, 2 * units), lambda e: (e, 0, 0)),
            pl.BlockSpec((1, count, units), lambda e: (e, 0, 0)),
        ],
        out_shape=[
            jax.ShapeDtypeStruct((count, width), jnp.bfloat16),
            jax.ShapeDtypeStruct((experts, count, 2 * units), jnp.float32),
            jax.ShapeDtypeStruct((experts, count, units), jnp.bfloat16),
        ],
        scratch_shapes=[pltpu.VMEM((count, width), jnp.float32)],
        compiler_params=pltpu.CompilerParams(vmem_limit_bytes=VMEM_BYTES),
        cost_estimate=SMALL_COST,
        name="experts_forward",
    )(tokens, gates_own, w_in, w_out)


def experts_backward_kernel(
    dmix_ref, gate_ref, gate_up_ref, in_ref, out_ref, drows_ref, dgate_up_ref, dgates_ref, total
):
    expert = pl.program_id(0)
    units = out_ref.shape[1]
    lanes = lax.broadcasted_iota(jnp.int32, (1, LANES), 1)

    @pl.when(expert == 0)
    def _():
        total[...] = jnp.zeros_like(total)
        dgates_ref[...] = jnp.zeros_like(dgates_ref)

    for rows in row_chunks(dmix_ref.shape[0]):
        pulled = dot_nt(dmix_ref[rows, :], out_ref[0])
        gate_vals = gate_up_ref[0, rows, :units]
        up_vals = gate_up_ref[0, rows, units:]
        sigmoid = 1.0 / (1.0 + jnp.exp(-gate_vals))
        silu_gate = gate_vals * sigmoid
        weight = pick_lane(gate_ref[rows, :], expert)
        d_up = pulled * silu_gate
        own = jnp.sum(d_up * up_vals, axis=1, keepdims=True)
        own = jnp.where(lanes == expert, own, 0.0)
        d_up = d_up * weight
        d_gate = (pulled * weight) * up_vals * (sigmoid + silu_gate * (1.0 - sigmoid))
        dgate_up_ref[0, rows, :units] = d_gate.astype(jnp.bfloat16)
        dgate_up_ref[0, rows, units:] = d_up.astype(jnp.bfloat16)
        total[rows, :] += dot_nt(dgate_up_ref[0, rows, :], in_ref[0])
        dgates_ref[rows, :] += own

    @pl.when(expert == pl.num_programs(0) - 1)
    def _():
        drows_ref[...] = total[...].astype(drows_ref.dtype)


def experts_backward(d_mix, gates_own, gate_up, w_in, w_out):
    count, width = d_mix.shape
    experts, units = w_out.shape[0], w_out.shape[1]
    return pl.pallas_call(
        experts_backward_kernel,
        grid=(experts,),
        in_specs=[
            pl.BlockSpec((count, width), lambda e: (0, 0)),
            pl.BlockSpec((count, LANES), lambda e: (0, 0)),
            pl.BlockSpec((1, count, 2 * units), lambda e: (e, 0, 0)),
            pl.BlockSpec((1, width, 2 * units), lambda e: (e, 0, 0)),
            pl.BlockSpec((1, units, width), lambda e: (e, 0, 0)),
        ],
        out_specs=[
            pl.BlockSpec((count, width), lambda e: (0, 0)),
            pl.BlockSpec((1, count, 2 * units), lambda e: (e, 0, 0)),
            pl.BlockSpec((count, LANES), lambda e: (0, 0)),
        ],
        out_shape=[
            jax.ShapeDtypeStruct((count, width), jnp.bfloat16),
            jax.ShapeDtypeStruct((experts, count, 2 * units), jnp.bfloat16),
            jax.ShapeDtypeStruct((count, LANES), jnp.float32),
        ],
        scratch_shapes=[pltpu.VMEM((count, width), jnp.float32)],
        compiler_params=pltpu.CompilerParams(vmem_limit_bytes=VMEM_BYTES),
        cost_estimate=SMALL_COST,
        name="experts_backward",
    )(d_mix, gates_own, gate_up, w_in, w_out)


def experts_grads_kernel(outputs, units, based, order_ref, *refs):
    grads_refs, refs = refs[-outputs:], refs[:-outputs]
    base_ref, refs = (refs[0], refs[1:]) if based else (None, refs)
    count = len(refs) // 4
    width = refs[0].shape[1]
    grad_in, grad_out = None, None
    for at in range(count):
        x_ref, dmix_ref, dgate_up_ref, hidden_ref = refs[4 * at : 4 * at + 4]
        part_in = dot_tn(x_ref[...], dgate_up_ref[0])
        part_out = dot_tn(hidden_ref[0], dmix_ref[...])
        grad_in = part_in if grad_in is None else grad_in + part_in
        grad_out = part_out if grad_out is None else grad_out + part_out
    tall, short = width // units, grad_out.shape[0] // units

    def put(ref):
        for at in range(units):
            start = at * (tall + short)
            for first, size, value in (
                (start, tall, grad_in[at * tall : (at + 1) * tall]),
                (start + tall, short, grad_out[at * short : (at + 1) * short]),
            ):
                span = slice(first, first + size)
                if based:
                    value = value + base_ref[0, span, :].astype(jnp.float32)
                ref[span, :] = value.astype(jnp.bfloat16)

    if outputs == 1:
        put(grads_refs[0].at[0])
        return
    for at in range(outputs):
        pl.when(pl.program_id(0) == at)(functools.partial(put, grads_refs[at]))


def experts_grads(order, chunks, apart, row_units, base=None, base_at=0):
    count, width = chunks[0][0].shape
    units = chunks[0][3].shape[2]
    experts = order.shape[0]
    specs = [
        pl.BlockSpec((count, width), lambda e, order: (0, 0)),
        pl.BlockSpec((count, width), lambda e, order: (0, 0)),
        pl.BlockSpec((1, count, 2 * units), lambda e, order: (order[e], 0, 0)),
        pl.BlockSpec((1, count, units), lambda e, order: (order[e], 0, 0)),
    ]
    rows, columns = width + units, 2 * units
    base_specs = []
    if base is not None:
        base_specs = [pl.BlockSpec((1, rows, columns), lambda e, order: (base_at + e, 0, 0))]
    if apart and experts > 1:
        outputs = experts
        out_specs = [pl.BlockSpec((rows, columns), lambda e, order: (0, 0))] * experts
        out_shape = [jax.ShapeDtypeStruct((rows, columns), jnp.bfloat16)] * experts
    else:
        outputs = 1
        out_specs = [pl.BlockSpec((1, rows, columns), lambda e, order: (e, 0, 0))]
        out_shape = [jax.ShapeDtypeStruct((experts, rows, columns), jnp.bfloat16)]
    grads = pl.pallas_call(
        functools.partial(experts_grads_kernel, outputs, row_units, base is not None),
        grid_spec=pltpu.PrefetchScalarGridSpec(
            num_scalar_prefetch=1,
            grid=(experts,),
            in_specs=base_specs + specs * len(chunks),
            out_specs=out_specs,
        ),
        out_shape=out_shape,
        compiler_params=pltpu.CompilerParams(vmem_limit_bytes=VMEM_BYTES),
        cost_estimate=SMALL_COST,
        name="experts_grads",
    )(order, *([] if base is None else [base]), *[part for chunk in chunks for part in chunk])
    return grads


def widen_kernel(steps, spot_ref, first_ref, second_ref, *refs):
    gin_ref, gout_ref = refs[-2:]
    tall = gin_ref.shape[1]

    def put(piece_ref):
        gin_ref[0] = piece_ref[:tall, :].astype(jnp.float32)
        gout_ref[0] = piece_ref[tall:, :].astype(jnp.float32)

    at = pl.program_id(0)
    pl.when(at < steps)(functools.partial(put, first_ref))
    pl.when(at >= steps)(functools.partial(put, second_ref))


def widen(spot, first, second, shapes, units, held):
    rows, columns = shapes[0][1] + shapes[1][1], first.shape[1]
    unit = rows // units
    steps = first.shape[0] // unit

    def place(at, spot):
        late = at >= steps
        expert = jnp.where(late, spot[2], spot[0])
        return (expert, jnp.where(late, spot[3] + at - steps, spot[1] + at), 0)

    return pl.pallas_call(
        functools.partial(widen_kernel, steps),
        grid_spec=pltpu.PrefetchScalarGridSpec(
            num_scalar_prefetch=1,
            grid=(2 * steps,),
            in_specs=[
                pl.BlockSpec((unit, columns), lambda at, spot: (jnp.minimum(at, steps - 1), 0)),
                pl.BlockSpec((unit, columns), lambda at, spot: (jnp.maximum(at - steps, 0), 0)),
            ]
            + [pl.BlockSpec(memory_space=pl.ANY)] * len(held),
            out_specs=[
                pl.BlockSpec((1, shape[1] // units, columns), place) for shape in shapes
            ],
        ),
        out_shape=[jax.ShapeDtypeStruct(shape, jnp.float32) for shape in shapes],
        input_output_aliases={3 + at: at for at in range(len(held))},
        compiler_params=pltpu.CompilerParams(vmem_limit_bytes=20 * MIB),
        cost_estimate=SMALL_COST,
        name="widen",
    )(spot, first, second, *held)


def finish_kernel(
    spots, widths, digits, piece_ref, query_ref, key_ref, value_ref, output_ref, router_ref, gain_ref,
    loss_ref, small_ref
):
    query_width, half, kv_width = widths
    experts = router_ref.shape[1]
    rows = piece_ref.shape[1]
    for at, (first, second) in enumerate(spots):
        first_at = slice(first * rows, (first + 1) * rows)
        second_at = slice(second * rows, (second + 1) * rows)
        block = piece_ref[at].astype(jnp.float32)
        query_ref[first_at, :] = block[:, :query_width]
        start = query_width + half
        output_ref[first_at, :half] = block[:, query_width:start]
        small_ref[first_at, :] = block[:, start : start + LANES]
        start = start + LANES
        key_ref[second_at, :] = block[:, start : start + kv_width]
        value_ref[second_at, :] = block[:, start + kv_width : start + 2 * kv_width]
        output_ref[second_at, half:] = block[:, start + 2 * kv_width :]
    router_ref[...] = small_ref[:, :experts]
    turned = small_ref[...].T
    gain_ref[...] = turned[experts : experts + 8]
    row = lax.broadcasted_iota(jnp.int32, turned.shape, 0) - experts - 2
    loss = jnp.sum(jnp.where((row >= 0) & (row < digits), turned, 0.0))
    loss_ref[...] = jnp.full(loss_ref.shape, loss, jnp.float32)


def finish(pieces, spots, widths, digits, experts):
    count, rows, _ = pieces.shape
    query_width, half, kv_width = widths
    return pl.pallas_call(
        functools.partial(finish_kernel, spots, widths, digits),
        in_specs=[whole_spec()],
        out_specs=[whole_spec()] * 7,
        out_shape=[
            jax.ShapeDtypeStruct((count * rows, columns), jnp.float32)
            for columns in (query_width, kv_width, kv_width, 2 * half, experts)
        ]
        + [jax.ShapeDtypeStruct((8, columns), jnp.float32) for columns in (count * rows, LANES)],
        scratch_shapes=[pltpu.VMEM((count * rows, LANES), jnp.float32)],
        compiler_params=pltpu.CompilerParams(vmem_limit_bytes=20 * MIB),
        cost_estimate=SMALL_COST,
        name="finish",
    )(pieces)


def attention_grads_kernel(
    sets,
    side_ref, digits_ref, normed_ref, dquery_ref, all_ref, dkv_ref, attended_ref, dbranch_ref,
    gain_ref, router_ref,
    wq_ref, wkv_ref, input_ref, own_ref,
    dnormed_kv_ref, dnormed_query_ref, sent_first, kept_first, sent_second, kept_second,
    first_ref, second_ref
):
    query_width = dquery_ref.shape[1]
    half = dbranch_ref.shape[1] // 2
    kv_width = dkv_ref.shape[1]
    shards, rows = kept_first.shape[0], kept_first.shape[1]

    def gain_of(d_normed, block):
        values = block.astype(jnp.float32)
        scale = lax.rsqrt(jnp.mean(values * values, axis=-1, keepdims=True) + norm_eps)
        return jnp.sum(d_normed * values * scale, axis=0, keepdims=True)

    def put(ref, columns, value):
        ref[:, :, columns] = value.astype(jnp.bfloat16).reshape(shards, 2 * rows, -1)

    d_normed = dot_nt(dquery_ref[...], wq_ref[...])
    dnormed_query_ref[...] = d_normed
    gain = gain_of(d_normed, own_ref[...])
    for start in range(0, all_ref.shape[0], ROW_STEP):
        span = pl.ds(start, ROW_STEP)
        d_normed = dot_nt(dkv_ref[span, :], wkv_ref[...])
        dnormed_kv_ref[span, :] = d_normed.astype(jnp.bfloat16)
        gain = gain + gain_of(d_normed, input_ref[span, :])
    put(second_ref, slice(0, kv_width), dot_tn(all_ref[...], dkv_ref[...]))
    put(first_ref, slice(0, query_width), dot_tn(normed_ref[...], dquery_ref[...]))
    grad_output = dot_tn(attended_ref[...], dbranch_ref[...])
    put(first_ref, slice(query_width, query_width + half), grad_output[:, :half])
    put(second_ref, slice(kv_width, kv_width + half), grad_output[:, half:])
    experts, width = router_ref.shape
    row = lax.broadcasted_iota(jnp.int32, (LANES - experts, width), 0)
    spot = lax.broadcasted_iota(jnp.int32, row.shape, 1) % (2 * rows)
    rest = jnp.where(row == 0, gain, jnp.where(row == 1, gain_ref[...], 0.0))
    for at in range(digits_ref.shape[0]):
        for turn in range(sets):
            here = (row == 2 + at * sets + turn) & (spot == side_ref[1] - 2 * rows * turn)
            rest = jnp.where(here, digits_ref[at], rest)
    small = jnp.concatenate([router_ref[...], rest], 0).T
    put(first_ref, slice(query_width + half, first_ref.shape[2]), small)
    kept_at = pl.ds(pl.multiple_of(side_ref[0] * rows, rows), rows)
    sent_at = pl.ds(pl.multiple_of((1 - side_ref[0]) * rows, rows), rows)
    sent_first[...] = first_ref[:, sent_at, :]
    sent_second[...] = second_ref[:, sent_at, :]
    kept_first[...] = first_ref[:, kept_at, :]
    kept_second[...] = second_ref[:, kept_at, :]


def attention_grads(
    side, digits, sets, shards, normed, d_query, normed_all, d_kv, attended, d_branch, gain, router,
    w_query, w_kv, input_all, hidden_in
):
    width = normed.shape[1]
    half = d_branch.shape[1] // 2
    rows = width // shards // 2
    widths = (d_query.shape[1] + half + LANES, d_kv.shape[1] + half)
    return pl.pallas_call(
        functools.partial(attention_grads_kernel, sets),
        in_specs=[pl.BlockSpec(memory_space=pltpu.SMEM)] * 2 + [whole_spec()] * 12,
        out_specs=[whole_spec()] * 6,
        out_shape=[
            jax.ShapeDtypeStruct(input_all.shape, jnp.bfloat16),
            jax.ShapeDtypeStruct(hidden_in.shape, jnp.float32),
        ]
        + [
            jax.ShapeDtypeStruct((shards, rows, columns), jnp.bfloat16)
            for columns in (widths[0], widths[0], widths[1], widths[1])
        ],
        scratch_shapes=[
            pltpu.VMEM((shards, 2 * rows, columns), jnp.bfloat16) for columns in widths
        ],
        compiler_params=pltpu.CompilerParams(vmem_limit_bytes=46 * MIB),
        cost_estimate=SMALL_COST,
        name="attention_grads",
    )(
        side, digits, normed, d_query, normed_all, d_kv, attended, d_branch, gain, router,
        w_query, w_kv, input_all, hidden_in,
    )


MIB = 1024 * 1024
VMEM_BYTES = 60 * MIB


def swap_halves(values):
    lanes = lax.broadcasted_iota(jnp.int32, values.shape, 1)
    ahead = pltpu.roll(values, LANES - HEAD_DIM // 2, 1)
    behind = pltpu.roll(values, HEAD_DIM // 2, 1)
    return jnp.where(lanes % HEAD_DIM < HEAD_DIM // 2, ahead, behind)


def stack_heads(block, parity):
    values = block.astype(jnp.float32)
    lanes = lax.broadcasted_iota(jnp.int32, values.shape, 1)
    low = jnp.where(lanes < HEAD_DIM, values, 0.0)
    high = values - low
    if parity == 0:
        high = pltpu.roll(high, HEAD_DIM, 1)
    else:
        low = pltpu.roll(low, HEAD_DIM, 1)
    return jnp.concatenate([low, high], 0).astype(jnp.bfloat16)


def unstack_heads(stacked, parity):
    rows = stacked.shape[0] // 2
    low, high = stacked[:rows], stacked[rows:]
    if parity == 0:
        high = pltpu.roll(high, HEAD_DIM, 1)
    else:
        low = pltpu.roll(low, HEAD_DIM, 1)
    lanes = lax.broadcasted_iota(jnp.int32, low.shape, 1)
    return jnp.where(lanes < HEAD_DIM, low, high)


def lane_block(at):
    return pl.ds(pl.multiple_of(at * LANES, LANES), LANES)


def attention_forward_kernel(
    bias_ref, side_ref, input_ref, own_ref, gain_ref, query_held, query_other, kv_held, kv_other,
    cos_ref, sin_ref, cos_own_ref, sin_own_ref,
    wq_out, wkv_out, normed_out, key_out, value_out, normed_own_ref, query_ref, attended_ref, norm_ref,
    all_ref, wq_parts, wkv_parts, normed_ref, key_ref, value_ref, scores, row_sems, in_sems, out_sems
):
    tokens, width = all_ref.shape
    kv_width = key_ref.shape[1]
    key_rows = tokens // bias_ref.shape[0]
    half_rows = query_held.shape[1]
    held_at = pl.ds(pl.multiple_of(side_ref[0] * half_rows, half_rows), half_rows)
    other_at = pl.ds(pl.multiple_of((1 - side_ref[0]) * half_rows, half_rows), half_rows)
    row_copies = []
    for at in range(tokens // ROW_STEP):
        span = pl.ds(at * ROW_STEP, ROW_STEP)
        copy = pltpu.make_async_copy(input_ref.at[span, :], all_ref.at[span, :], row_sems.at[at])
        copy.start()
        row_copies.append(copy)
    weight_copies = []
    for at, (source, target) in enumerate(
        (
            (kv_held, wkv_parts.at[:, held_at, :]),
            (kv_other, wkv_parts.at[:, other_at, :]),
            (query_held, wq_parts.at[:, held_at, :]),
            (query_other, wq_parts.at[:, other_at, :]),
        )
    ):
        copy = pltpu.make_async_copy(source, target, in_sems.at[at])
        copy.start()
        weight_copies.append(copy)
    wq_ref = wq_parts.reshape(width, wq_parts.shape[2])
    wkv_ref = wkv_parts.reshape(width, wkv_parts.shape[2])

    def normed_rows(block):
        values = block.astype(jnp.float32)
        scale = lax.rsqrt(jnp.mean(values * values, axis=-1, keepdims=True) + norm_eps)
        return (values * scale * gain_ref[...]).astype(jnp.bfloat16)

    normed_own = normed_rows(own_ref[...])
    normed_own_ref[...] = normed_own
    for at, copy in enumerate(row_copies):
        copy.wait()
        span = pl.ds(at * ROW_STEP, ROW_STEP)
        normed_ref[span, :] = normed_rows(all_ref[span, :])
    out_copies = [pltpu.make_async_copy(normed_ref, normed_out, out_sems.at[0])]
    out_copies[0].start()
    for copy in weight_copies:
        copy.wait()
    for at, (source, target) in enumerate(((wq_parts, wq_out), (wkv_parts, wkv_out))):
        out_copies.append(pltpu.make_async_copy(source, target, out_sems.at[1 + at]))
        out_copies[-1].start()

    def project(at, carry):
        rows = pl.ds(pl.multiple_of(at * ROW_STEP, ROW_STEP), ROW_STEP)
        linear = dot_nn(normed_ref[rows, :], wkv_ref[...])
        for col in range(0, kv_width, LANES):
            part = linear[:, col : col + LANES]
            turned = part * cos_ref[rows, :] + swap_halves(part) * sin_ref[rows, :]
            key_ref[rows, col : col + LANES] = turned.astype(jnp.bfloat16)
        value_ref[rows, :] = linear[:, kv_width:].astype(jnp.bfloat16)
        return carry

    lax.fori_loop(0, tokens // ROW_STEP, project, 0)
    for at, (source, target) in enumerate(((key_ref, key_out), (value_ref, value_out))):
        out_copies.append(pltpu.make_async_copy(source, target, out_sems.at[3 + at]))
        out_copies[-1].start()
    linear = dot_nn(normed_own, wq_ref[...])
    for col in range(0, wq_ref.shape[1], LANES):
        part = linear[:, col : col + LANES]
        turned = part * cos_own_ref[...] + swap_halves(part) * sin_own_ref[...]
        query_ref[:, col : col + LANES] = (turned.astype(jnp.bfloat16).astype(jnp.float32) * attn_mult).astype(jnp.bfloat16)

    def attend(pair, carry):
        lanes = lane_block(pair)
        turned_values = value_ref[:, lanes].astype(jnp.float32).T.astype(jnp.bfloat16)
        for parity in range(2):
            group = 2 * pair + parity
            stacked = stack_heads(query_ref[:, lane_block(group)], parity)
            top = None
            for at in range(bias_ref.shape[0]):
                rows = pl.ds(at * key_rows, key_rows)
                part = dot_nt(key_ref[rows, lanes], stacked)
                scores[rows, :] = part
                high = jnp.max(part, axis=0, keepdims=True) + bias_ref[at]
                top = high if top is None else jnp.maximum(top, high)
            total, gathered = None, None
            for at in range(bias_ref.shape[0]):
                rows = pl.ds(at * key_rows, key_rows)
                raised = jnp.exp(scores[rows, :] - (top - bias_ref[at]))
                part = jnp.sum(raised, axis=0, keepdims=True)
                mixed = dot_nn(
                    turned_values[:, at * key_rows : (at + 1) * key_rows], raised.astype(jnp.bfloat16)
                )
                total = part if total is None else total + part
                gathered = mixed if gathered is None else gathered + mixed
            gathered = (gathered / total).T
            attended_ref[:, lane_block(group)] = unstack_heads(gathered, parity).astype(jnp.bfloat16)
            norm_ref[pl.ds(group, 1), :] = top + jnp.log(total)
        return carry

    lax.fori_loop(0, kv_width // LANES, attend, 0)
    for copy in out_copies:
        copy.wait()


def far_spec():
    return pl.BlockSpec(memory_space=pl.ANY)


def whole_spec():
    return pl.BlockSpec(memory_space=pltpu.VMEM)


def attention_forward(bias, side, input_all, hidden_in, gain, query_pair, kv_pair, tables, tables_own):
    tokens, width = input_all.shape
    rows = hidden_in.shape[0]
    shards, half_rows, query_width = query_pair[0].shape
    kv_width = kv_pair[0].shape[2] // 2
    return pl.pallas_call(
        attention_forward_kernel,
        in_specs=[pl.BlockSpec(memory_space=pltpu.SMEM)] * 2
        + [far_spec()]
        + [whole_spec()] * 2
        + [far_spec()] * 4
        + [whole_spec()] * 4,
        out_specs=[far_spec()] * 5 + [whole_spec()] * 4,
        out_shape=[
            jax.ShapeDtypeStruct((shards, 2 * half_rows, query_width), jnp.bfloat16),
            jax.ShapeDtypeStruct((shards, 2 * half_rows, 2 * kv_width), jnp.bfloat16),
            jax.ShapeDtypeStruct((tokens, width), jnp.bfloat16),
            jax.ShapeDtypeStruct((tokens, kv_width), jnp.bfloat16),
            jax.ShapeDtypeStruct((tokens, kv_width), jnp.bfloat16),
            jax.ShapeDtypeStruct((rows, width), jnp.bfloat16),
            jax.ShapeDtypeStruct((rows, query_width), jnp.bfloat16),
            jax.ShapeDtypeStruct((rows, query_width), jnp.bfloat16),
            jax.ShapeDtypeStruct((KV_HEADS, 2 * rows), jnp.float32),
        ],
        scratch_shapes=[
            pltpu.VMEM((tokens, width), jnp.bfloat16),
            pltpu.VMEM((shards, 2 * half_rows, query_width), jnp.bfloat16),
            pltpu.VMEM((shards, 2 * half_rows, 2 * kv_width), jnp.bfloat16),
            pltpu.VMEM((tokens, width), jnp.bfloat16),
            pltpu.VMEM((tokens, kv_width), jnp.bfloat16),
            pltpu.VMEM((tokens, kv_width), jnp.bfloat16),
            pltpu.VMEM((tokens, 2 * rows), jnp.float32),
            pltpu.SemaphoreType.DMA((tokens // ROW_STEP,)),
            pltpu.SemaphoreType.DMA((4,)),
            pltpu.SemaphoreType.DMA((5,)),
        ],
        compiler_params=pltpu.CompilerParams(vmem_limit_bytes=VMEM_BYTES),
        cost_estimate=SMALL_COST,
        name="attention_forward",
    )(bias, side, input_all, hidden_in, gain, *query_pair, *kv_pair, *tables, *tables_own)


def attention_backward_kernel(
    bias_ref, query_ref, key_ref, value_ref, norm_ref, grad_ref, cos_ref, sin_ref, cos_own_ref, sin_own_ref,
    dquery_ref, dkv_ref, probs, dprobs, dkeys, dvalues
):
    tokens, kv_width = key_ref.shape
    key_rows = tokens // bias_ref.shape[0]

    def pull(pair, carry):
        lanes = lane_block(pair)
        turned_keys = key_ref[:, lanes].astype(jnp.float32).T.astype(jnp.bfloat16)
        for parity in range(2):
            group = 2 * pair + parity
            stacked = stack_heads(query_ref[:, lane_block(group)], parity)
            stacked_grad = stack_heads(grad_ref[:, lane_block(group)], parity)
            log_norm = norm_ref[pl.ds(group, 1), :]
            total = None
            for at in range(bias_ref.shape[0]):
                rows = pl.ds(at * key_rows, key_rows)
                part = dot_nt(key_ref[rows, lanes], stacked)
                prob = jnp.exp(part - (log_norm - bias_ref[at]))
                d_prob = dot_nt(value_ref[rows, lanes], stacked_grad)
                probs[rows, :] = prob
                dprobs[rows, :] = d_prob
                d_value = dot_nn(prob.astype(jnp.bfloat16), stacked_grad)
                dvalues[rows, :] = d_value if parity == 0 else dvalues[rows, :] + d_value
                weighted = jnp.sum(prob * d_prob, axis=0, keepdims=True)
                total = weighted if total is None else total + weighted
            d_query = None
            for at in range(bias_ref.shape[0]):
                rows = pl.ds(at * key_rows, key_rows)
                d_score = (probs[rows, :] * (dprobs[rows, :] - total)).astype(jnp.bfloat16)
                d_key = dot_nn(d_score, stacked)
                dkeys[rows, :] = d_key if parity == 0 else dkeys[rows, :] + d_key
                part = dot_nn(turned_keys[:, at * key_rows : (at + 1) * key_rows], d_score)
                d_query = part if d_query is None else d_query + part
            part = unstack_heads(d_query.T, parity) * attn_mult
            turned = part * cos_own_ref[...] - swap_halves(part) * sin_own_ref[...]
            dquery_ref[:, lane_block(group)] = turned.astype(jnp.bfloat16)
        part = dkeys[...]
        turned = part * cos_ref[...] - swap_halves(part) * sin_ref[...]
        dkv_ref[:, lanes] = turned.astype(jnp.bfloat16)
        dkv_ref[:, lane_block(pair + kv_width // LANES)] = dvalues[...].astype(jnp.bfloat16)
        return carry

    lax.fori_loop(0, kv_width // LANES, pull, 0)


def attention_backward(bias, query, key, value, log_norm, grad, tables, tables_own):
    tokens, kv_width = key.shape
    rows, width = query.shape
    return pl.pallas_call(
        attention_backward_kernel,
        in_specs=[pl.BlockSpec(memory_space=pltpu.SMEM)] + [whole_spec()] * 9,
        out_specs=[whole_spec()] * 2,
        out_shape=[
            jax.ShapeDtypeStruct((rows, width), jnp.bfloat16),
            jax.ShapeDtypeStruct((tokens, 2 * kv_width), jnp.bfloat16),
        ],
        scratch_shapes=[
            pltpu.VMEM((tokens, 2 * rows), jnp.float32),
            pltpu.VMEM((tokens, 2 * rows), jnp.float32),
            pltpu.VMEM((tokens, LANES), jnp.float32),
            pltpu.VMEM((tokens, LANES), jnp.float32),
        ],
        compiler_params=pltpu.CompilerParams(vmem_limit_bytes=22 * MIB),
        cost_estimate=SMALL_COST,
        name="attention_backward",
    )(bias, query, key, value, log_norm, grad, *tables, *tables_own)


def exchange(block, bit):
    count = lax.axis_size("rep")
    return lax.ppermute(block, "rep", [(at, at ^ bit) for at in range(count)])


def side_of(bit):
    return (lax.axis_index("rep") // bit) % 2


def after(value, *others):
    return lax.optimization_barrier((value, *others))[0]


def slices_of(parts, start, size, axis):
    return [
        lax.dynamic_slice_in_dim(part, base + start, size, axis)
        for part, base in ((part if isinstance(part, tuple) else (part, 0)) for part in parts)
    ]


def add_parts(parts):
    total = parts[0].astype(jnp.float32)
    for part in parts[1:]:
        total = total + part.astype(jnp.float32)
    return total.astype(jnp.bfloat16)


def halve(parts, bit, axis, length=None):
    length = parts[0].shape[axis] if length is None else length
    half = length // 2
    side = side_of(bit)
    sent = slices_of(parts, (1 - side) * half, half, axis)
    sent = sent[0] if len(sent) == 1 else add_parts(sent)
    kept = slices_of(parts, side * half, half, axis)
    return sent, kept + [exchange(sent, bit)]


def double(block, bit, axis):
    size = block.shape[axis]
    side = side_of(bit)
    held = lax.concatenate([block, block], axis)
    return lax.dynamic_update_slice_in_dim(held, exchange(block, bit), (1 - side) * size, axis)


def rep_bits():
    count = lax.axis_size("rep")
    return [1 << at for at in range(count.bit_length() - 1)]


def body(
    hidden_in,
    valid_mask,
    teacher,
    routes,
    attn_norm,
    w_query,
    w_key,
    w_value,
    w_output,
    ffn_norm,
    router,
    w_in,
    w_out,
):
    row_count, model_width = hidden_in.shape
    shard_count = lax.axis_size("shard")
    seq_tokens = row_count * shard_count
    all_tokens = seq_tokens * lax.axis_size("rep")
    shard_at = lax.axis_index("shard")
    tables = rope_tables(jnp.arange(seq_tokens, dtype=jnp.int32))
    tables_own = tuple(
        lax.dynamic_slice_in_dim(table, shard_at * row_count, row_count, 0) for table in tables
    )
    key_blocks = jnp.arange(seq_tokens // BLOCK, dtype=jnp.int32)
    bias = jnp.where(key_blocks <= shard_at * row_count // BLOCK, 0.0, very_low)
    bits = rep_bits()
    near, far = bits[0], bits[1:]

    def gather(block):
        return lax.all_gather(block, "shard", axis=0, tiled=True)

    def scatter(block):
        return lax.psum_scatter(block, "shard", scatter_dimension=0, tiled=True)

    kv_width = w_key.shape[1]
    query_width = w_query.shape[1]
    half_width = w_output.shape[1] // 2
    own_rows = w_query.shape[0]
    piece_rows = own_rows // lax.axis_size("rep")

    def piece_of(block, order):
        index = 0
        for at, bit in enumerate(order):
            index = index + side_of(bit) * (1 << at)
        return lax.dynamic_slice_in_dim(block, index * piece_rows, piece_rows, 0)

    order_first, order_second = far + [near], far[::-1] + [near]
    w_kv = jnp.concatenate([w_key, w_value], 1)
    input_all = gather(hidden_in)
    valid_float = valid_mask.astype(jnp.float32)
    expert_count = router.shape[1]
    small_parts = [
        jnp.concatenate([attn_norm, ffn_norm, router.reshape(-1)]).reshape(1, -1),
        routes.astype(jnp.bfloat16).reshape(1, -1),
        jnp.sum(valid_float).astype(jnp.bfloat16).reshape(1, 1),
    ]
    small_size, routes_size = small_parts[0].size, small_parts[1].size
    pieces = lax.all_gather(
        jnp.concatenate([piece_of(w_query, order_first), piece_of(w_kv, order_second)], 1),
        "shard",
        axis=0,
    )
    query_full = pieces[..., :query_width]
    kv_full = pieces[..., query_width:]
    small_parts = jnp.concatenate(small_parts, 1)
    for at, (bit_first, bit_second) in enumerate(zip(order_first[:-1], order_second[:-1])):
        if at == len(far) - 1:
            small_parts = after(small_parts, query_full, kv_full)
        query_full = double(query_full, bit_first, 1)
        kv_full = double(kv_full, bit_second, 1)
    small_all = gather(small_parts)
    query_full, kv_full = after(query_full, small_all), after(kv_full, small_all)
    query_pair = query_full, exchange(query_full, near)
    kv_pair = kv_full, exchange(kv_full, near)
    near_rows = own_rows // 2
    output_half = lax.dynamic_slice_in_dim(w_output, side_of(near) * near_rows, near_rows, 0)
    output_half = lax.all_gather(after(output_half, query_pair[0], kv_pair[0]), "shard", axis=0)
    gain_attn = small_all[:, :own_rows].reshape(-1).astype(jnp.float32)
    gain_ffn = small_all[:, own_rows : 2 * own_rows].reshape(-1)
    router_full = small_all[:, 2 * own_rows : small_size].reshape(-1, expert_count)
    routes_all = small_all[:, small_size : small_size + routes_size]
    valid_count = jnp.broadcast_to(jnp.sum(small_all[:, small_size + routes_size].astype(jnp.float32)), (8, LANES))
    for bit in bits:
        valid_count = valid_count + exchange(valid_count, bit)
    valid_count = valid_count[0, 0]
    input_float = hidden_in.astype(jnp.float32)
    scale_attn = rms_scale(input_float)
    (
        query_full, kv_full, normed_all, keys_all, values_all, normed_attn, query_rows, attended, log_norm
    ) = attention_forward(
        bias, jnp.reshape(side_of(near), (1,)), input_all, hidden_in, gain_attn[None],
        query_pair, kv_pair, tables, tables_own,
    )
    query_full = query_full.reshape(model_width, query_width)
    kv_full = kv_full.reshape(model_width, 2 * kv_width)
    output_half, attended = lax.optimization_barrier((output_half, attended))
    output_full = double(output_half, near, 1).reshape(own_rows * shard_count, -1)
    branch = dot_nn(attended, output_full)
    middle = input_float + resid_mult * branch
    scale_ffn = rms_scale(middle)
    normed_ffn = (middle * scale_ffn * gain_ffn).astype(jnp.bfloat16)
    own_experts = w_in.shape[0]
    expert_ids = jnp.arange(expert_count, dtype=jnp.bfloat16)
    chunk_rows = row_count // CHUNKS
    spans = [slice(at * chunk_rows, (at + 1) * chunk_rows) for at in range(CHUNKS)]
    tokens_in = [gather(normed_ffn[span]) for span in spans]
    routes_all = routes_all.reshape(shard_count, row_count, -1)
    gates, forward = [], []
    for span, tokens in zip(spans, tokens_in):
        logits = dot_nn(tokens, router_full)
        routes_part = routes_all[:, span].reshape(shard_count * chunk_rows, -1)
        chosen = jnp.any(routes_part[..., None] == expert_ids, 1)
        masked = jnp.where(chosen, logits, very_low)
        raised = jnp.where(chosen, jnp.exp(masked - jnp.max(masked, -1, keepdims=True)), 0.0)
        gates_part = raised / jnp.sum(raised, -1, keepdims=True)
        gates_own = lax.dynamic_slice_in_dim(gates_part, shard_at * own_experts, own_experts, 1)
        gates_own = jnp.pad(gates_own, ((0, 0), (0, LANES - own_experts)))
        gates.append(lax.dynamic_slice_in_dim(gates_part, shard_at * chunk_rows, chunk_rows, 0))
        if not forward:
            gates_own = after(gates_own, valid_count)
        forward.append((gates_own, *experts_forward(tokens, gates_own, w_in, w_out)))
    gates = jnp.concatenate(gates, 0)
    results, d_results, d_mix_out, d_mix_in, own_loss = [], [], [], [], 0.0
    for span, (_, mix_part, _, _) in zip(spans, forward):
        mixture = scatter(mix_part)
        if d_mix_out:
            mixture = after(mixture, d_mix_out[-1])
        mixture = mixture.astype(jnp.float32)
        result_part = middle[span] + resid_mult * mixture
        deviation = result_part - teacher[span].astype(jnp.float32)
        masked = valid_float[span, None] * deviation
        d_result = masked * (all_tokens / (2.0 * valid_count))
        results.append(result_part.astype(jnp.bfloat16))
        d_results.append(d_result)
        d_mix_out.append((resid_mult * d_result).astype(jnp.bfloat16))
        d_mix_in.append(gather(d_mix_out[-1]))
        own_loss = own_loss + jnp.sum(masked * deviation)
    d_result = jnp.concatenate(d_results, 0)
    kept_experts = own_experts // 2
    grad_rows = model_width + w_out.shape[1]
    flat_rows = kept_experts * grad_rows
    row_units = 2 * grad_rows // (flat_rows >> len(far))
    side = side_of(near)
    digits, rest = [], own_loss
    for _ in range(3):
        digits.append(lax.reduce_precision(rest, 8, 7))
        rest = rest - digits[-1]
    device = lax.axis_index("rep") * shard_count + shard_at
    sets = -(-lax.axis_size("rep") * shard_count // own_rows)
    place, digits = jnp.stack([side, device]), jnp.stack(digits)
    columns = w_in.shape[2]
    shapes = (own_experts, model_width, columns), (own_experts, grad_rows - model_width, columns)
    half_units = row_units * flat_rows // grad_rows // 4
    second_at = (1, 0) if kept_experts > 1 else (0, 2 * half_units)
    targets = {}
    for across in range(2):
        for core in range(2):
            spot = []
            for bit, (expert, unit) in ((far[0], (0, 0)), (far[-1], second_at)):
                half = side_of(bit) if across == 0 else 1 - side_of(bit)
                owner = side if core == 0 else 1 - side
                spot += [owner * kept_experts + expert, unit + half * half_units]
            targets[across, core] = jnp.stack(spot)
    order = jnp.arange(kept_experts, dtype=jnp.int32)
    order_sent = order + (1 - side) * kept_experts
    order_kept = order + side * kept_experts
    d_rows, d_gates, backward = [], [], []
    for d_mix, (gates_own, _, gate_up, hidden_gated), tokens in zip(d_mix_in, forward, tokens_in):
        if not backward:
            gates_own = after(gates_own, place, digits, *targets.values())
        if len(backward) == CHUNKS - 1:
            order_all = jnp.concatenate([order_sent, order_kept])
            partial_grads = experts_grads(order_all, backward, False, row_units)[0]
            gates_own = after(gates_own, partial_grads)
        d_rows_part, d_gate_up, d_gates_part = experts_backward(
            d_mix, gates_own, gate_up, w_in, w_out
        )
        d_rows.append(scatter(d_rows_part))
        d_gates.append(d_gates_part)
        backward.append((tokens, d_mix, d_gate_up, hidden_gated))
    first_rows = d_rows[0]
    d_rows = jnp.concatenate(d_rows, 0).astype(jnp.float32)
    sent = experts_grads(order_sent, backward[-1:], True, row_units, partial_grads, 0)
    unit_rows = flat_rows // 2 >> len(far)
    sent = [part.reshape(-1, unit_rows, columns) for part in sent]
    other = [exchange(part, near) for part in sent]
    kept = experts_grads(
        after(order_kept, *sent), backward[-1:], False, row_units, partial_grads, kept_experts
    )
    kept = after(kept[0].reshape(-1, unit_rows, columns), first_rows)
    half_rows = flat_rows // 2 // unit_rows
    if kept_experts > 1:
        other_first = jnp.concatenate(other[: kept_experts // 2], 0)
        other_second = jnp.concatenate(other[kept_experts // 2 :], 0)
        spots = ((kept, 0), (other_first, 0)), ((kept, half_rows), (other_second, 0))
    else:
        spots = ((kept, 0), (other[0], 0)), ((kept, half_rows), (other[0], half_rows))
    moe_sent_first, moe_first = halve(spots[0], far[0], 0, half_rows)
    moe_sent_second, moe_second = halve(spots[1], far[-1], 0, half_rows)
    d_gates = [after(part, moe_sent_first, moe_sent_second) for part in d_gates]
    d_gates = [
        part[:, :own_experts].reshape(shard_count, chunk_rows, own_experts) for part in d_gates
    ]
    d_gates = jnp.concatenate(d_gates, 1).reshape(shard_count * row_count, own_experts)
    d_gates = lax.all_to_all(d_gates, "shard", split_axis=0, concat_axis=1, tiled=True)
    d_rows = after(d_rows, moe_sent_first, moe_sent_second)
    d_logits = (gates * (d_gates - jnp.sum(gates * d_gates, -1, keepdims=True))).astype(
        jnp.bfloat16
    )
    d_normed_ffn = d_rows + dot_nt(d_logits, router_full)
    grad_router = dot_tn(d_logits, normed_ffn)
    d_norm_mid, grad_gain_ffn = norm_back(d_normed_ffn, middle, scale_ffn, gain_ffn)
    d_middle = d_result + d_norm_mid
    d_branch = (resid_mult * d_middle).astype(jnp.bfloat16)
    d_attended = dot_nt(d_branch, output_full).astype(
        jnp.bfloat16
    )
    query_grad_rows, kv_grad_all = attention_backward(
        bias, query_rows, keys_all, values_all, log_norm, d_attended, tables, tables_own
    )
    query_grad_rows, kv_grad_all, moe_first[-1], moe_second[-1] = lax.optimization_barrier(
        (query_grad_rows, kv_grad_all, moe_first[-1], moe_second[-1])
    )
    d_normed_kv, d_normed_query, sent_first, kept_first, sent_second, kept_second = attention_grads(
        place, digits, sets, shard_count, normed_attn, query_grad_rows,
        normed_all, kv_grad_all, attended, d_branch, grad_gain_ffn[None], grad_router,
        query_full, kv_full, input_all, hidden_in
    )
    kv_scattered = scatter(d_normed_kv)
    d_normed_query = after(d_normed_query, sent_first, sent_second)
    d_normed_attn = kv_scattered.astype(jnp.float32) + d_normed_query
    d_norm_in, _ = norm_back(d_normed_attn, input_float, scale_attn, gain_attn)
    d_input = d_middle + d_norm_in
    for bit_first, bit_second in zip(far[1:], far[::-1][1:]):
        _, moe_first = halve(moe_first, bit_first, 0)
        _, moe_second = halve(moe_second, bit_second, 0)
    def by_piece(block):
        return block.reshape(shard_count, -1, piece_rows, block.shape[2])

    sent_first, sent_second, moe_first[-1], moe_second[-1] = lax.optimization_barrier(
        (sent_first, sent_second, moe_first[-1], moe_second[-1])
    )
    moe_first, moe_second = add_parts(moe_first), add_parts(moe_second)
    sent_first, sent_second = lax.optimization_barrier(
        (sent_first, sent_second, moe_first, moe_second)
    )[:2]
    first = [by_piece(kept_first), exchange(by_piece(sent_first), near)]
    second = [by_piece(kept_second), exchange(by_piece(sent_second), near)]
    for bit_first, bit_second in zip(far[:0:-1], far[:-1]):
        moe_first = double(moe_first, bit_first, 0)
        moe_second = double(moe_second, bit_second, 0)
    for bit_first, bit_second in zip(far, far[::-1]):
        _, first = halve(first, bit_first, 1)
        _, second = halve(second, bit_second, 1)
        if bit_first == far[0]:
            first[-1] = after(first[-1], moe_first, moe_second)
            second[-1] = after(second[-1], moe_first, moe_second)
    first[-1] = after(first[-1], kv_scattered)
    moe_first = after(moe_first, first[-1], second[-1])
    moe_second = after(moe_second, first[-1], second[-1])
    own_first, own_second = moe_first, moe_second
    far_first, far_second = exchange(own_first, far[0]), exchange(own_second, far[-1])
    near_own = exchange(own_first, near), exchange(own_second, near)
    joined = jnp.concatenate([add_parts(first), add_parts(second)], 3)
    joined = joined.reshape(shard_count, piece_rows, -1)
    joined = lax.psum_scatter(joined, "shard", scatter_dimension=0)
    def put(held, pieces, *where):
        pieces = [piece.reshape(-1, columns) for piece in pieces]
        return widen(targets[where], *pieces, shapes, row_units, held)

    held = put([], (own_first, own_second), 0, 0)
    held = put(held, near_own, 0, 1)
    *held, joined, d_input = lax.optimization_barrier((*held, joined, d_input))
    gathered = lax.all_gather(joined, "rep", axis=0)
    *held, far_first, far_second = lax.optimization_barrier((*held, far_first, far_second))
    near_far = exchange(far_first, near), exchange(far_second, near)
    held = put(held, (far_first, far_second), 1, 0)
    held = put(held, near_far, 1, 1)
    sum_in, sum_out = held

    def row_of(at, order):
        return sum(((at // bit) % 2) << (len(order) - 1 - turn) for turn, bit in enumerate(order))

    pairs = tuple(
        (row_of(at, [near] + far), row_of(at, [near] + far[::-1])) for at in range(lax.axis_size("rep"))
    )
    sum_query, sum_key, sum_value, sum_output, sum_router, sum_gains, loss = finish(
        gathered, pairs, (query_width, half_width, kv_width), 3 * sets, expert_count
    )
    loss = loss[0, 0] / (model_width * valid_count)
    return (
        jnp.concatenate(results, 0),
        loss,
        d_input,
        sum_gains[0],
        sum_query,
        sum_key,
        sum_value,
        sum_output,
        sum_gains[1],
        sum_router,
        sum_in,
        sum_out,
    )


def solution(mesh):
    in_specs = (
        P(("rep", "shard"), None),
        P(("rep", "shard")),
        P(("rep", "shard"), None),
        P(("rep", "shard"), None),
        P("shard"),
        P("shard", None),
        P("shard", None),
        P("shard", None),
        P("shard", None),
        P("shard"),
        P("shard", None),
        P("shard", None, None),
        P("shard", None, None),
    )
    out_specs = (
        P(("rep", "shard"), None),
        P(),
        P(("rep", "shard"), None),
        P("shard"),
        P("shard", None),
        P("shard", None),
        P("shard", None),
        P("shard", None),
        P("shard"),
        P("shard", None),
        P("shard", None, None),
        P("shard", None, None),
    )
    return jax.shard_map(body, mesh=mesh, in_specs=in_specs, out_specs=out_specs, check_vma=False)
```

```python
import functools

import jax
import jax.numpy as jnp
from jax import lax
from jax.experimental import pallas as pl
from jax.experimental.pallas import tpu as pltpu
from jax.sharding import PartitionSpec as P

HEADS = 16
KV_HEADS = 8
HEAD_DIM = 64
TOP = 8
BLOCK = 256
CHUNKS = 2
SMALL_COST = pl.CostEstimate(flops=1000000, bytes_accessed=100000, transcendentals=0)


norm_eps = 1e-06
resid_mult = 0.22
attn_mult = 0.015625
rope_base = 10000.0
very_low = -1e30


def rope_tables(positions):
    half_dim = HEAD_DIM // 2
    frequency = rope_base ** (-jnp.arange(half_dim, dtype=jnp.float32) / half_dim)
    angles = positions.astype(jnp.float32)[:, None] * frequency[None, :]
    cosine, sine = jnp.cos(angles), jnp.sin(angles)
    return (
        jnp.concatenate([cosine] * 4, 1),
        jnp.concatenate([-sine, sine, -sine, sine], 1),
    )


def rms_scale(values):
    return lax.rsqrt(jnp.mean(values * values, axis=-1, keepdims=True) + norm_eps)


def norm_back(d_normed, values, scale_vals, gain_vec):
    scaled_grad = d_normed * gain_vec
    d_gain = jnp.sum(d_normed * values * scale_vals, 0)
    d_values = scale_vals * (
        scaled_grad
        - values * scale_vals * scale_vals * jnp.mean(scaled_grad * values, axis=-1, keepdims=True)
    )
    return (d_values, d_gain)


LANES = 128
ROW_STEP = 256
EXPERT_STEP = 512


def row_chunks(count):
    step = min(count, EXPERT_STEP)
    return [pl.ds(at, step) for at in range(0, count, step)]


def pick_lane(values, lane):
    lanes = lax.broadcasted_iota(jnp.int32, values.shape, 1)
    return jnp.sum(jnp.where(lanes == lane, values, 0.0), axis=1, keepdims=True)


def dot_nn(left, right):
    return jnp.dot(left, right, preferred_element_type=jnp.float32)


def dot_nt(left, right):
    return lax.dot_general(left, right, (((1,), (1,)), ((), ())), preferred_element_type=jnp.float32)


def dot_tn(left, right):
    return lax.dot_general(left, right, (((0,), (0,)), ((), ())), preferred_element_type=jnp.float32)


def experts_forward_kernel(x_ref, gate_ref, in_ref, out_ref, mix_ref, gate_up_ref, hidden_ref, total):
    expert = pl.program_id(0)
    units = out_ref.shape[1]

    @pl.when(expert == 0)
    def _():
        total[...] = jnp.zeros_like(total)

    for rows in row_chunks(x_ref.shape[0]):
        gate_up = dot_nn(x_ref[rows, :], in_ref[0])
        gate_up_ref[0, rows, :] = gate_up
        gate_vals = gate_up[:, :units]
        silu_gate = gate_vals / (1.0 + jnp.exp(-gate_vals))
        weight = pick_lane(gate_ref[rows, :], expert)
        hidden = (silu_gate * gate_up[:, units:] * weight).astype(jnp.bfloat16)
        hidden_ref[0, rows, :] = hidden
        total[rows, :] += dot_nn(hidden, out_ref[0])

    @pl.when(expert == pl.num_programs(0) - 1)
    def _():
        mix_ref[...] = total[...].astype(mix_ref.dtype)


def experts_forward(tokens, gates_own, w_in, w_out):
    count, width = tokens.shape
    experts, units = w_out.shape[0], w_out.shape[1]
    return pl.pallas_call(
        experts_forward_kernel,
        grid=(experts,),
        in_specs=[
            pl.BlockSpec((count, width), lambda e: (0, 0)),
            pl.BlockSpec((count, LANES), lambda e: (0, 0)),
            pl.BlockSpec((1, width, 2 * units), lambda e: (e, 0, 0)),
            pl.BlockSpec((1, units, width), lambda e: (e, 0, 0)),
        ],
        out_specs=[
            pl.BlockSpec((count, width), lambda e: (0, 0)),
            pl.BlockSpec((1, count, 2 * units), lambda e: (e, 0, 0)),
            pl.BlockSpec((1, count, units), lambda e: (e, 0, 0)),
        ],
        out_shape=[
            jax.ShapeDtypeStruct((count, width), jnp.bfloat16),
            jax.ShapeDtypeStruct((experts, count, 2 * units), jnp.float32),
            jax.ShapeDtypeStruct((experts, count, units), jnp.bfloat16),
        ],
        scratch_shapes=[pltpu.VMEM((count, width), jnp.float32)],
        compiler_params=pltpu.CompilerParams(vmem_limit_bytes=VMEM_BYTES),
        cost_estimate=SMALL_COST,
        name="experts_forward",
    )(tokens, gates_own, w_in, w_out)


def experts_backward_kernel(
    dmix_ref, gate_ref, gate_up_ref, in_ref, out_ref, drows_ref, dgate_up_ref, dgates_ref, total
):
    expert = pl.program_id(0)
    units = out_ref.shape[1]
    lanes = lax.broadcasted_iota(jnp.int32, (1, LANES), 1)

    @pl.when(expert == 0)
    def _():
        total[...] = jnp.zeros_like(total)
        dgates_ref[...] = jnp.zeros_like(dgates_ref)

    for rows in row_chunks(dmix_ref.shape[0]):
        pulled = dot_nt(dmix_ref[rows, :], out_ref[0])
        gate_vals = gate_up_ref[0, rows, :units]
        up_vals = gate_up_ref[0, rows, units:]
        sigmoid = 1.0 / (1.0 + jnp.exp(-gate_vals))
        silu_gate = gate_vals * sigmoid
        weight = pick_lane(gate_ref[rows, :], expert)
        d_up = pulled * silu_gate
        own = jnp.sum(d_up * up_vals, axis=1, keepdims=True)
        own = jnp.where(lanes == expert, own, 0.0)
        d_up = d_up * weight
        d_gate = (pulled * weight) * up_vals * (sigmoid + silu_gate * (1.0 - sigmoid))
        dgate_up_ref[0, rows, :units] = d_gate.astype(jnp.bfloat16)
        dgate_up_ref[0, rows, units:] = d_up.astype(jnp.bfloat16)
        total[rows, :] += dot_nt(dgate_up_ref[0, rows, :], in_ref[0])
        dgates_ref[rows, :] += own

    @pl.when(expert == pl.num_programs(0) - 1)
    def _():
        drows_ref[...] = total[...].astype(drows_ref.dtype)


def experts_backward(d_mix, gates_own, gate_up, w_in, w_out):
    count, width = d_mix.shape
    experts, units = w_out.shape[0], w_out.shape[1]
    return pl.pallas_call(
        experts_backward_kernel,
        grid=(experts,),
        in_specs=[
            pl.BlockSpec((count, width), lambda e: (0, 0)),
            pl.BlockSpec((count, LANES), lambda e: (0, 0)),
            pl.BlockSpec((1, count, 2 * units), lambda e: (e, 0, 0)),
            pl.BlockSpec((1, width, 2 * units), lambda e: (e, 0, 0)),
            pl.BlockSpec((1, units, width), lambda e: (e, 0, 0)),
        ],
        out_specs=[
            pl.BlockSpec((count, width), lambda e: (0, 0)),
            pl.BlockSpec((1, count, 2 * units), lambda e: (e, 0, 0)),
            pl.BlockSpec((count, LANES), lambda e: (0, 0)),
        ],
        out_shape=[
            jax.ShapeDtypeStruct((count, width), jnp.bfloat16),
            jax.ShapeDtypeStruct((experts, count, 2 * units), jnp.bfloat16),
            jax.ShapeDtypeStruct((count, LANES), jnp.float32),
        ],
        scratch_shapes=[pltpu.VMEM((count, width), jnp.float32)],
        compiler_params=pltpu.CompilerParams(vmem_limit_bytes=VMEM_BYTES),
        cost_estimate=SMALL_COST,
        name="experts_backward",
    )(d_mix, gates_own, gate_up, w_in, w_out)


def experts_grads_kernel(outputs, units, based, order_ref, *refs):
    grads_refs, refs = refs[-outputs:], refs[:-outputs]
    base_ref, refs = (refs[0], refs[1:]) if based else (None, refs)
    count = len(refs) // 4
    width = refs[0].shape[1]
    grad_in, grad_out = None, None
    for at in range(count):
        x_ref, dmix_ref, dgate_up_ref, hidden_ref = refs[4 * at : 4 * at + 4]
        part_in = dot_tn(x_ref[...], dgate_up_ref[0])
        part_out = dot_tn(hidden_ref[0], dmix_ref[...])
        grad_in = part_in if grad_in is None else grad_in + part_in
        grad_out = part_out if grad_out is None else grad_out + part_out
    tall, short = width // units, grad_out.shape[0] // units

    def put(ref):
        for at in range(units):
            start = at * (tall + short)
            for first, size, value in (
                (start, tall, grad_in[at * tall : (at + 1) * tall]),
                (start + tall, short, grad_out[at * short : (at + 1) * short]),
            ):
                span = slice(first, first + size)
                if based:
                    value = value + base_ref[0, span, :].astype(jnp.float32)
                ref[span, :] = value.astype(jnp.bfloat16)

    if outputs == 1:
        put(grads_refs[0].at[0])
        return
    for at in range(outputs):
        pl.when(pl.program_id(0) == at)(functools.partial(put, grads_refs[at]))


def experts_grads(order, chunks, apart, row_units, base=None, base_at=0):
    count, width = chunks[0][0].shape
    units = chunks[0][3].shape[2]
    experts = order.shape[0]
    specs = [
        pl.BlockSpec((count, width), lambda e, order: (0, 0)),
        pl.BlockSpec((count, width), lambda e, order: (0, 0)),
        pl.BlockSpec((1, count, 2 * units), lambda e, order: (order[e], 0, 0)),
        pl.BlockSpec((1, count, units), lambda e, order: (order[e], 0, 0)),
    ]
    rows, columns = width + units, 2 * units
    base_specs = []
    if base is not None:
        base_specs = [pl.BlockSpec((1, rows, columns), lambda e, order: (base_at + e, 0, 0))]
    if apart and experts > 1:
        outputs = experts
        out_specs = [pl.BlockSpec((rows, columns), lambda e, order: (0, 0))] * experts
        out_shape = [jax.ShapeDtypeStruct((rows, columns), jnp.bfloat16)] * experts
    else:
        outputs = 1
        out_specs = [pl.BlockSpec((1, rows, columns), lambda e, order: (e, 0, 0))]
        out_shape = [jax.ShapeDtypeStruct((experts, rows, columns), jnp.bfloat16)]
    grads = pl.pallas_call(
        functools.partial(experts_grads_kernel, outputs, row_units, base is not None),
        grid_spec=pltpu.PrefetchScalarGridSpec(
            num_scalar_prefetch=1,
            grid=(experts,),
            in_specs=base_specs + specs * len(chunks),
            out_specs=out_specs,
        ),
        out_shape=out_shape,
        compiler_params=pltpu.CompilerParams(vmem_limit_bytes=VMEM_BYTES),
        cost_estimate=SMALL_COST,
        name="experts_grads",
    )(order, *([] if base is None else [base]), *[part for chunk in chunks for part in chunk])
    return grads


def widen_kernel(steps, spot_ref, first_ref, second_ref, *refs):
    gin_ref, gout_ref = refs[-2:]
    tall = gin_ref.shape[1]

    def put(piece_ref):
        gin_ref[0] = piece_ref[:tall, :].astype(jnp.float32)
        gout_ref[0] = piece_ref[tall:, :].astype(jnp.float32)

    at = pl.program_id(0)
    pl.when(at < steps)(functools.partial(put, first_ref))
    pl.when(at >= steps)(functools.partial(put, second_ref))


def widen(spot, first, second, shapes, units, held):
    rows, columns = shapes[0][1] + shapes[1][1], first.shape[1]
    unit = rows // units
    steps = first.shape[0] // unit

    def place(at, spot):
        late = at >= steps
        expert = jnp.where(late, spot[2], spot[0])
        return (expert, jnp.where(late, spot[3] + at - steps, spot[1] + at), 0)

    return pl.pallas_call(
        functools.partial(widen_kernel, steps),
        grid_spec=pltpu.PrefetchScalarGridSpec(
            num_scalar_prefetch=1,
            grid=(2 * steps,),
            in_specs=[
                pl.BlockSpec((unit, columns), lambda at, spot: (jnp.minimum(at, steps - 1), 0)),
                pl.BlockSpec((unit, columns), lambda at, spot: (jnp.maximum(at - steps, 0), 0)),
            ]
            + [pl.BlockSpec(memory_space=pl.ANY)] * len(held),
            out_specs=[
                pl.BlockSpec((1, shape[1] // units, columns), place) for shape in shapes
            ],
        ),
        out_shape=[jax.ShapeDtypeStruct(shape, jnp.float32) for shape in shapes],
        input_output_aliases={3 + at: at for at in range(len(held))},
        compiler_params=pltpu.CompilerParams(vmem_limit_bytes=20 * MIB),
        cost_estimate=SMALL_COST,
        name="widen",
    )(spot, first, second, *held)


def finish_kernel(
    spots, widths, digits, piece_ref, query_ref, key_ref, value_ref, output_ref, router_ref, gain_ref,
    loss_ref, small_ref
):
    query_width, half, kv_width = widths
    experts = router_ref.shape[1]
    rows = piece_ref.shape[1]
    for at, (first, second) in enumerate(spots):
        first_at = slice(first * rows, (first + 1) * rows)
        second_at = slice(second * rows, (second + 1) * rows)
        block = piece_ref[at].astype(jnp.float32)
        query_ref[first_at, :] = block[:, :query_width]
        start = query_width + half
        output_ref[first_at, :half] = block[:, query_width:start]
        small_ref[first_at, :] = block[:, start : start + LANES]
        start = start + LANES
        key_ref[second_at, :] = block[:, start : start + kv_width]
        value_ref[second_at, :] = block[:, start + kv_width : start + 2 * kv_width]
        output_ref[second_at, half:] = block[:, start + 2 * kv_width :]
    router_ref[...] = small_ref[:, :experts]
    turned = small_ref[...].T
    gain_ref[...] = turned[experts : experts + 8]
    row = lax.broadcasted_iota(jnp.int32, turned.shape, 0) - experts - 2
    loss = jnp.sum(jnp.where((row >= 0) & (row < digits), turned, 0.0))
    loss_ref[...] = jnp.full(loss_ref.shape, loss, jnp.float32)


def finish(pieces, spots, widths, digits, experts):
    count, rows, _ = pieces.shape
    query_width, half, kv_width = widths
    return pl.pallas_call(
        functools.partial(finish_kernel, spots, widths, digits),
        in_specs=[whole_spec()],
        out_specs=[whole_spec()] * 7,
        out_shape=[
            jax.ShapeDtypeStruct((count * rows, columns), jnp.float32)
            for columns in (query_width, kv_width, kv_width, 2 * half, experts)
        ]
        + [jax.ShapeDtypeStruct((8, columns), jnp.float32) for columns in (count * rows, LANES)],
        scratch_shapes=[pltpu.VMEM((count * rows, LANES), jnp.float32)],
        compiler_params=pltpu.CompilerParams(vmem_limit_bytes=20 * MIB),
        cost_estimate=SMALL_COST,
        name="finish",
    )(pieces)


def attention_grads_kernel(
    sets,
    side_ref, digits_ref, normed_ref, dquery_ref, all_ref, dkv_ref, attended_ref, dbranch_ref,
    gain_ref, router_ref,
    wq_ref, wkv_ref, input_ref, own_ref,
    dnormed_kv_ref, dnormed_query_ref, sent_first, kept_first, sent_second, kept_second,
    first_ref, second_ref
):
    query_width = dquery_ref.shape[1]
    half = dbranch_ref.shape[1] // 2
    kv_width = dkv_ref.shape[1]
    shards, rows = kept_first.shape[0], kept_first.shape[1]

    def gain_of(d_normed, block):
        values = block.astype(jnp.float32)
        scale = lax.rsqrt(jnp.mean(values * values, axis=-1, keepdims=True) + norm_eps)
        return jnp.sum(d_normed * values * scale, axis=0, keepdims=True)

    def put(ref, columns, value):
        ref[:, :, columns] = value.astype(jnp.bfloat16).reshape(shards, 2 * rows, -1)

    d_normed = dot_nt(dquery_ref[...], wq_ref[...])
    dnormed_query_ref[...] = d_normed
    gain = gain_of(d_normed, own_ref[...])
    for start in range(0, all_ref.shape[0], ROW_STEP):
        span = pl.ds(start, ROW_STEP)
        d_normed = dot_nt(dkv_ref[span, :], wkv_ref[...])
        dnormed_kv_ref[span, :] = d_normed.astype(jnp.bfloat16)
        gain = gain + gain_of(d_normed, input_ref[span, :])
    put(second_ref, slice(0, kv_width), dot_tn(all_ref[...], dkv_ref[...]))
    put(first_ref, slice(0, query_width), dot_tn(normed_ref[...], dquery_ref[...]))
    grad_output = dot_tn(attended_ref[...], dbranch_ref[...])
    put(first_ref, slice(query_width, query_width + half), grad_output[:, :half])
    put(second_ref, slice(kv_width, kv_width + half), grad_output[:, half:])
    experts, width = router_ref.shape
    row = lax.broadcasted_iota(jnp.int32, (LANES - experts, width), 0)
    spot = lax.broadcasted_iota(jnp.int32, row.shape, 1) % (2 * rows)
    rest = jnp.where(row == 0, gain, jnp.where(row == 1, gain_ref[...], 0.0))
    for at in range(digits_ref.shape[0]):
        for turn in range(sets):
            here = (row == 2 + at * sets + turn) & (spot == side_ref[1] - 2 * rows * turn)
            rest = jnp.where(here, digits_ref[at], rest)
    small = jnp.concatenate([router_ref[...], rest], 0).T
    put(first_ref, slice(query_width + half, first_ref.shape[2]), small)
    kept_at = pl.ds(pl.multiple_of(side_ref[0] * rows, rows), rows)
    sent_at = pl.ds(pl.multiple_of((1 - side_ref[0]) * rows, rows), rows)
    sent_first[...] = first_ref[:, sent_at, :]
    sent_second[...] = second_ref[:, sent_at, :]
    kept_first[...] = first_ref[:, kept_at, :]
    kept_second[...] = second_ref[:, kept_at, :]


def attention_grads(
    side, digits, sets, shards, normed, d_query, normed_all, d_kv, attended, d_branch, gain, router,
    w_query, w_kv, input_all, hidden_in
):
    width = normed.shape[1]
    half = d_branch.shape[1] // 2
    rows = width // shards // 2
    widths = (d_query.shape[1] + half + LANES, d_kv.shape[1] + half)
    return pl.pallas_call(
        functools.partial(attention_grads_kernel, sets),
        in_specs=[pl.BlockSpec(memory_space=pltpu.SMEM)] * 2 + [whole_spec()] * 12,
        out_specs=[whole_spec()] * 6,
        out_shape=[
            jax.ShapeDtypeStruct(input_all.shape, jnp.bfloat16),
            jax.ShapeDtypeStruct(hidden_in.shape, jnp.float32),
        ]
        + [
            jax.ShapeDtypeStruct((shards, rows, columns), jnp.bfloat16)
            for columns in (widths[0], widths[0], widths[1], widths[1])
        ],
        scratch_shapes=[
            pltpu.VMEM((shards, 2 * rows, columns), jnp.bfloat16) for columns in widths
        ],
        compiler_params=pltpu.CompilerParams(vmem_limit_bytes=60 * MIB),
        cost_estimate=SMALL_COST,
        name="attention_grads",
    )(
        side, digits, normed, d_query, normed_all, d_kv, attended, d_branch, gain, router,
        w_query, w_kv, input_all, hidden_in,
    )


MIB = 1024 * 1024
VMEM_BYTES = 60 * MIB


def swap_halves(values):
    lanes = lax.broadcasted_iota(jnp.int32, values.shape, 1)
    ahead = pltpu.roll(values, LANES - HEAD_DIM // 2, 1)
    behind = pltpu.roll(values, HEAD_DIM // 2, 1)
    return jnp.where(lanes % HEAD_DIM < HEAD_DIM // 2, ahead, behind)


def stack_heads(block, parity):
    values = block.astype(jnp.float32)
    lanes = lax.broadcasted_iota(jnp.int32, values.shape, 1)
    low = jnp.where(lanes < HEAD_DIM, values, 0.0)
    high = values - low
    if parity == 0:
        high = pltpu.roll(high, HEAD_DIM, 1)
    else:
        low = pltpu.roll(low, HEAD_DIM, 1)
    return jnp.concatenate([low, high], 0).astype(jnp.bfloat16)


def unstack_heads(stacked, parity):
    rows = stacked.shape[0] // 2
    low, high = stacked[:rows], stacked[rows:]
    if parity == 0:
        high = pltpu.roll(high, HEAD_DIM, 1)
    else:
        low = pltpu.roll(low, HEAD_DIM, 1)
    lanes = lax.broadcasted_iota(jnp.int32, low.shape, 1)
    return jnp.where(lanes < HEAD_DIM, low, high)


def lane_block(at):
    return pl.ds(pl.multiple_of(at * LANES, LANES), LANES)


def attention_forward_kernel(
    bias_ref, side_ref, input_ref, own_ref, gain_ref, query_held, query_other, kv_held, kv_other,
    cos_ref, sin_ref, cos_own_ref, sin_own_ref,
    wq_out, wkv_out, normed_out, key_out, value_out, normed_own_ref, query_ref, attended_ref, norm_ref,
    all_ref, wq_parts, wkv_parts, normed_ref, key_ref, value_ref, scores, row_sems, in_sems, out_sems
):
    tokens, width = all_ref.shape
    kv_width = key_ref.shape[1]
    key_rows = tokens // bias_ref.shape[0]
    half_rows = query_held.shape[1]
    held_at = pl.ds(pl.multiple_of(side_ref[0] * half_rows, half_rows), half_rows)
    other_at = pl.ds(pl.multiple_of((1 - side_ref[0]) * half_rows, half_rows), half_rows)
    row_copies = []
    for at in range(tokens // ROW_STEP):
        span = pl.ds(at * ROW_STEP, ROW_STEP)
        copy = pltpu.make_async_copy(input_ref.at[span, :], all_ref.at[span, :], row_sems.at[at])
        copy.start()
        row_copies.append(copy)
    weight_copies = []
    for at, (source, target) in enumerate(
        (
            (kv_held, wkv_parts.at[:, held_at, :]),
            (kv_other, wkv_parts.at[:, other_at, :]),
            (query_held, wq_parts.at[:, held_at, :]),
            (query_other, wq_parts.at[:, other_at, :]),
        )
    ):
        copy = pltpu.make_async_copy(source, target, in_sems.at[at])
        copy.start()
        weight_copies.append(copy)
    wq_ref = wq_parts.reshape(width, wq_parts.shape[2])
    wkv_ref = wkv_parts.reshape(width, wkv_parts.shape[2])

    def normed_rows(block):
        values = block.astype(jnp.float32)
        scale = lax.rsqrt(jnp.mean(values * values, axis=-1, keepdims=True) + norm_eps)
        return (values * scale * gain_ref[...]).astype(jnp.bfloat16)

    normed_own = normed_rows(own_ref[...])
    normed_own_ref[...] = normed_own
    for at, copy in enumerate(row_copies):
        copy.wait()
        span = pl.ds(at * ROW_STEP, ROW_STEP)
        normed_ref[span, :] = normed_rows(all_ref[span, :])
    out_copies = [pltpu.make_async_copy(normed_ref, normed_out, out_sems.at[0])]
    out_copies[0].start()
    for copy in weight_copies:
        copy.wait()
    for at, (source, target) in enumerate(((wq_parts, wq_out), (wkv_parts, wkv_out))):
        out_copies.append(pltpu.make_async_copy(source, target, out_sems.at[1 + at]))
        out_copies[-1].start()

    def project(at, carry):
        rows = pl.ds(pl.multiple_of(at * ROW_STEP, ROW_STEP), ROW_STEP)
        linear = dot_nn(normed_ref[rows, :], wkv_ref[...])
        for col in range(0, kv_width, LANES):
            part = linear[:, col : col + LANES]
            turned = part * cos_ref[rows, :] + swap_halves(part) * sin_ref[rows, :]
            key_ref[rows, col : col + LANES] = turned.astype(jnp.bfloat16)
        value_ref[rows, :] = linear[:, kv_width:].astype(jnp.bfloat16)
        return carry

    lax.fori_loop(0, tokens // ROW_STEP, project, 0)
    for at, (source, target) in enumerate(((key_ref, key_out), (value_ref, value_out))):
        out_copies.append(pltpu.make_async_copy(source, target, out_sems.at[3 + at]))
        out_copies[-1].start()
    linear = dot_nn(normed_own, wq_ref[...])
    for col in range(0, wq_ref.shape[1], LANES):
        part = linear[:, col : col + LANES]
        turned = part * cos_own_ref[...] + swap_halves(part) * sin_own_ref[...]
        query_ref[:, col : col + LANES] = (turned.astype(jnp.bfloat16).astype(jnp.float32) * attn_mult).astype(jnp.bfloat16)

    def attend(pair, carry):
        lanes = lane_block(pair)
        turned_values = value_ref[:, lanes].astype(jnp.float32).T.astype(jnp.bfloat16)
        for parity in range(2):
            group = 2 * pair + parity
            stacked = stack_heads(query_ref[:, lane_block(group)], parity)
            top = None
            for at in range(bias_ref.shape[0]):
                rows = pl.ds(at * key_rows, key_rows)
                part = dot_nt(key_ref[rows, lanes], stacked)
                scores[rows, :] = part
                high = jnp.max(part, axis=0, keepdims=True) + bias_ref[at]
                top = high if top is None else jnp.maximum(top, high)
            total, gathered = None, None
            for at in range(bias_ref.shape[0]):
                rows = pl.ds(at * key_rows, key_rows)
                raised = jnp.exp(scores[rows, :] - (top - bias_ref[at]))
                part = jnp.sum(raised, axis=0, keepdims=True)
                mixed = dot_nn(
                    turned_values[:, at * key_rows : (at + 1) * key_rows], raised.astype(jnp.bfloat16)
                )
                total = part if total is None else total + part
                gathered = mixed if gathered is None else gathered + mixed
            gathered = (gathered / total).T
            attended_ref[:, lane_block(group)] = unstack_heads(gathered, parity).astype(jnp.bfloat16)
            norm_ref[pl.ds(group, 1), :] = top + jnp.log(total)
        return carry

    lax.fori_loop(0, kv_width // LANES, attend, 0)
    for copy in out_copies:
        copy.wait()


def far_spec():
    return pl.BlockSpec(memory_space=pl.ANY)


def whole_spec():
    return pl.BlockSpec(memory_space=pltpu.VMEM)


def attention_forward(bias, side, input_all, hidden_in, gain, query_pair, kv_pair, tables, tables_own):
    tokens, width = input_all.shape
    rows = hidden_in.shape[0]
    shards, half_rows, query_width = query_pair[0].shape
    kv_width = kv_pair[0].shape[2] // 2
    return pl.pallas_call(
        attention_forward_kernel,
        in_specs=[pl.BlockSpec(memory_space=pltpu.SMEM)] * 2
        + [far_spec()]
        + [whole_spec()] * 2
        + [far_spec()] * 4
        + [whole_spec()] * 4,
        out_specs=[far_spec()] * 5 + [whole_spec()] * 4,
        out_shape=[
            jax.ShapeDtypeStruct((shards, 2 * half_rows, query_width), jnp.bfloat16),
            jax.ShapeDtypeStruct((shards, 2 * half_rows, 2 * kv_width), jnp.bfloat16),
            jax.ShapeDtypeStruct((tokens, width), jnp.bfloat16),
            jax.ShapeDtypeStruct((tokens, kv_width), jnp.bfloat16),
            jax.ShapeDtypeStruct((tokens, kv_width), jnp.bfloat16),
            jax.ShapeDtypeStruct((rows, width), jnp.bfloat16),
            jax.ShapeDtypeStruct((rows, query_width), jnp.bfloat16),
            jax.ShapeDtypeStruct((rows, query_width), jnp.bfloat16),
            jax.ShapeDtypeStruct((KV_HEADS, 2 * rows), jnp.float32),
        ],
        scratch_shapes=[
            pltpu.VMEM((tokens, width), jnp.bfloat16),
            pltpu.VMEM((shards, 2 * half_rows, query_width), jnp.bfloat16),
            pltpu.VMEM((shards, 2 * half_rows, 2 * kv_width), jnp.bfloat16),
            pltpu.VMEM((tokens, width), jnp.bfloat16),
            pltpu.VMEM((tokens, kv_width), jnp.bfloat16),
            pltpu.VMEM((tokens, kv_width), jnp.bfloat16),
            pltpu.VMEM((tokens, 2 * rows), jnp.float32),
            pltpu.SemaphoreType.DMA((tokens // ROW_STEP,)),
            pltpu.SemaphoreType.DMA((4,)),
            pltpu.SemaphoreType.DMA((5,)),
        ],
        compiler_params=pltpu.CompilerParams(vmem_limit_bytes=VMEM_BYTES),
        cost_estimate=SMALL_COST,
        name="attention_forward",
    )(bias, side, input_all, hidden_in, gain, *query_pair, *kv_pair, *tables, *tables_own)


def attention_backward_kernel(
    bias_ref, query_ref, key_ref, value_ref, norm_ref, grad_ref, cos_ref, sin_ref, cos_own_ref, sin_own_ref,
    dquery_ref, dkv_ref, probs, dprobs, dkeys, dvalues
):
    tokens, kv_width = key_ref.shape
    key_rows = tokens // bias_ref.shape[0]

    def pull(pair, carry):
        lanes = lane_block(pair)
        turned_keys = key_ref[:, lanes].astype(jnp.float32).T.astype(jnp.bfloat16)
        for parity in range(2):
            group = 2 * pair + parity
            stacked = stack_heads(query_ref[:, lane_block(group)], parity)
            stacked_grad = stack_heads(grad_ref[:, lane_block(group)], parity)
            log_norm = norm_ref[pl.ds(group, 1), :]
            total = None
            for at in range(bias_ref.shape[0]):
                rows = pl.ds(at * key_rows, key_rows)
                part = dot_nt(key_ref[rows, lanes], stacked)
                prob = jnp.exp(part - (log_norm - bias_ref[at]))
                d_prob = dot_nt(value_ref[rows, lanes], stacked_grad)
                probs[rows, :] = prob
                dprobs[rows, :] = d_prob
                d_value = dot_nn(prob.astype(jnp.bfloat16), stacked_grad)
                dvalues[rows, :] = d_value if parity == 0 else dvalues[rows, :] + d_value
                weighted = jnp.sum(prob * d_prob, axis=0, keepdims=True)
                total = weighted if total is None else total + weighted
            d_query = None
            for at in range(bias_ref.shape[0]):
                rows = pl.ds(at * key_rows, key_rows)
                d_score = (probs[rows, :] * (dprobs[rows, :] - total)).astype(jnp.bfloat16)
                d_key = dot_nn(d_score, stacked)
                dkeys[rows, :] = d_key if parity == 0 else dkeys[rows, :] + d_key
                part = dot_nn(turned_keys[:, at * key_rows : (at + 1) * key_rows], d_score)
                d_query = part if d_query is None else d_query + part
            part = unstack_heads(d_query.T, parity) * attn_mult
            turned = part * cos_own_ref[...] - swap_halves(part) * sin_own_ref[...]
            dquery_ref[:, lane_block(group)] = turned.astype(jnp.bfloat16)
        part = dkeys[...]
        turned = part * cos_ref[...] - swap_halves(part) * sin_ref[...]
        dkv_ref[:, lanes] = turned.astype(jnp.bfloat16)
        dkv_ref[:, lane_block(pair + kv_width // LANES)] = dvalues[...].astype(jnp.bfloat16)
        return carry

    lax.fori_loop(0, kv_width // LANES, pull, 0)


def attention_backward(bias, query, key, value, log_norm, grad, tables, tables_own):
    tokens, kv_width = key.shape
    rows, width = query.shape
    return pl.pallas_call(
        attention_backward_kernel,
        in_specs=[pl.BlockSpec(memory_space=pltpu.SMEM)] + [whole_spec()] * 9,
        out_specs=[whole_spec()] * 2,
        out_shape=[
            jax.ShapeDtypeStruct((rows, width), jnp.bfloat16),
            jax.ShapeDtypeStruct((tokens, 2 * kv_width), jnp.bfloat16),
        ],
        scratch_shapes=[
            pltpu.VMEM((tokens, 2 * rows), jnp.float32),
            pltpu.VMEM((tokens, 2 * rows), jnp.float32),
            pltpu.VMEM((tokens, LANES), jnp.float32),
            pltpu.VMEM((tokens, LANES), jnp.float32),
        ],
        compiler_params=pltpu.CompilerParams(vmem_limit_bytes=22 * MIB),
        cost_estimate=SMALL_COST,
        name="attention_backward",
    )(bias, query, key, value, log_norm, grad, *tables, *tables_own)


def exchange(block, bit):
    count = lax.axis_size("rep")
    return lax.ppermute(block, "rep", [(at, at ^ bit) for at in range(count)])


def side_of(bit):
    return (lax.axis_index("rep") // bit) % 2


def after(value, *others):
    return lax.optimization_barrier((value, *others))[0]


def slices_of(parts, start, size, axis):
    return [
        lax.dynamic_slice_in_dim(part, base + start, size, axis)
        for part, base in ((part if isinstance(part, tuple) else (part, 0)) for part in parts)
    ]


def add_parts(parts):
    total = parts[0].astype(jnp.float32)
    for part in parts[1:]:
        total = total + part.astype(jnp.float32)
    return total.astype(jnp.bfloat16)


def halve(parts, bit, axis, length=None):
    length = parts[0].shape[axis] if length is None else length
    half = length // 2
    side = side_of(bit)
    sent = slices_of(parts, (1 - side) * half, half, axis)
    sent = sent[0] if len(sent) == 1 else add_parts(sent)
    kept = slices_of(parts, side * half, half, axis)
    return sent, kept + [exchange(sent, bit)]


def double(block, bit, axis):
    size = block.shape[axis]
    side = side_of(bit)
    held = lax.concatenate([block, block], axis)
    return lax.dynamic_update_slice_in_dim(held, exchange(block, bit), (1 - side) * size, axis)


def rep_bits():
    count = lax.axis_size("rep")
    return [1 << at for at in range(count.bit_length() - 1)]


def body(
    hidden_in,
    valid_mask,
    teacher,
    routes,
    attn_norm,
    w_query,
    w_key,
    w_value,
    w_output,
    ffn_norm,
    router,
    w_in,
    w_out,
):
    row_count, model_width = hidden_in.shape
    shard_count = lax.axis_size("shard")
    seq_tokens = row_count * shard_count
    all_tokens = seq_tokens * lax.axis_size("rep")
    shard_at = lax.axis_index("shard")
    tables = rope_tables(jnp.arange(seq_tokens, dtype=jnp.int32))
    tables_own = tuple(
        lax.dynamic_slice_in_dim(table, shard_at * row_count, row_count, 0) for table in tables
    )
    key_blocks = jnp.arange(seq_tokens // BLOCK, dtype=jnp.int32)
    bias = jnp.where(key_blocks <= shard_at * row_count // BLOCK, 0.0, very_low)
    bits = rep_bits()
    near, far = bits[0], bits[1:]

    def gather(block):
        return lax.all_gather(block, "shard", axis=0, tiled=True)

    def scatter(block):
        return lax.psum_scatter(block, "shard", scatter_dimension=0, tiled=True)

    kv_width = w_key.shape[1]
    query_width = w_query.shape[1]
    half_width = w_output.shape[1] // 2
    own_rows = w_query.shape[0]
    piece_rows = own_rows // lax.axis_size("rep")

    def piece_of(block, order):
        index = 0
        for at, bit in enumerate(order):
            index = index + side_of(bit) * (1 << at)
        return lax.dynamic_slice_in_dim(block, index * piece_rows, piece_rows, 0)

    order_first, order_second = far + [near], far[::-1] + [near]
    w_kv = jnp.concatenate([w_key, w_value], 1)
    input_all = gather(hidden_in)
    valid_float = valid_mask.astype(jnp.float32)
    expert_count = router.shape[1]
    small_parts = [
        jnp.concatenate([attn_norm, ffn_norm, router.reshape(-1)]).reshape(1, -1),
        routes.astype(jnp.bfloat16).reshape(1, -1),
        jnp.sum(valid_float).astype(jnp.bfloat16).reshape(1, 1),
    ]
    small_size, routes_size = small_parts[0].size, small_parts[1].size
    pieces = lax.all_gather(
        jnp.concatenate([piece_of(w_query, order_first), piece_of(w_kv, order_second)], 1),
        "shard",
        axis=0,
    )
    query_full = pieces[..., :query_width]
    kv_full = pieces[..., query_width:]
    small_parts = jnp.concatenate(small_parts, 1)
    for at, (bit_first, bit_second) in enumerate(zip(order_first[:-1], order_second[:-1])):
        if at == len(far) - 1:
            small_parts = after(small_parts, query_full, kv_full)
        query_full = double(query_full, bit_first, 1)
        kv_full = double(kv_full, bit_second, 1)
    small_all = gather(small_parts)
    query_full, kv_full = after(query_full, small_all), after(kv_full, small_all)
    query_pair = query_full, exchange(query_full, near)
    kv_pair = kv_full, exchange(kv_full, near)
    near_rows = own_rows // 2
    output_half = lax.dynamic_slice_in_dim(w_output, side_of(near) * near_rows, near_rows, 0)
    output_half = lax.all_gather(after(output_half, query_pair[0], kv_pair[0]), "shard", axis=0)
    gain_attn = small_all[:, :own_rows].reshape(-1).astype(jnp.float32)
    gain_ffn = small_all[:, own_rows : 2 * own_rows].reshape(-1)
    router_full = small_all[:, 2 * own_rows : small_size].reshape(-1, expert_count)
    routes_all = small_all[:, small_size : small_size + routes_size]
    valid_count = jnp.broadcast_to(jnp.sum(small_all[:, small_size + routes_size].astype(jnp.float32)), (8, LANES))
    for bit in bits:
        valid_count = valid_count + exchange(valid_count, bit)
    valid_count = valid_count[0, 0]
    input_float = hidden_in.astype(jnp.float32)
    scale_attn = rms_scale(input_float)
    (
        query_full, kv_full, normed_all, keys_all, values_all, normed_attn, query_rows, attended, log_norm
    ) = attention_forward(
        bias, jnp.reshape(side_of(near), (1,)), input_all, hidden_in, gain_attn[None],
        query_pair, kv_pair, tables, tables_own,
    )
    query_full = query_full.reshape(model_width, query_width)
    kv_full = kv_full.reshape(model_width, 2 * kv_width)
    output_half, attended = lax.optimization_barrier((output_half, attended))
    output_full = double(output_half, near, 1).reshape(own_rows * shard_count, -1)
    branch = dot_nn(attended, output_full)
    middle = input_float + resid_mult * branch
    scale_ffn = rms_scale(middle)
    normed_ffn = (middle * scale_ffn * gain_ffn).astype(jnp.bfloat16)
    own_experts = w_in.shape[0]
    expert_ids = jnp.arange(expert_count, dtype=jnp.bfloat16)
    chunk_rows = row_count // CHUNKS
    spans = [slice(at * chunk_rows, (at + 1) * chunk_rows) for at in range(CHUNKS)]
    tokens_in = [gather(normed_ffn[span]) for span in spans]
    routes_all = routes_all.reshape(shard_count, row_count, -1)
    gates, forward = [], []
    for span, tokens in zip(spans, tokens_in):
        logits = dot_nn(tokens, router_full)
        routes_part = routes_all[:, span].reshape(shard_count * chunk_rows, -1)
        chosen = jnp.any(routes_part[..., None] == expert_ids, 1)
        masked = jnp.where(chosen, logits, very_low)
        raised = jnp.where(chosen, jnp.exp(masked - jnp.max(masked, -1, keepdims=True)), 0.0)
        gates_part = raised / jnp.sum(raised, -1, keepdims=True)
        gates_own = lax.dynamic_slice_in_dim(gates_part, shard_at * own_experts, own_experts, 1)
        gates_own = jnp.pad(gates_own, ((0, 0), (0, LANES - own_experts)))
        gates.append(lax.dynamic_slice_in_dim(gates_part, shard_at * chunk_rows, chunk_rows, 0))
        if not forward:
            gates_own = after(gates_own, valid_count)
        forward.append((gates_own, *experts_forward(tokens, gates_own, w_in, w_out)))
    gates = jnp.concatenate(gates, 0)
    results, d_results, d_mix_out, d_mix_in, own_loss = [], [], [], [], 0.0
    for span, (_, mix_part, _, _) in zip(spans, forward):
        mixture = scatter(mix_part)
        if d_mix_out:
            mixture = after(mixture, d_mix_out[-1])
        mixture = mixture.astype(jnp.float32)
        result_part = middle[span] + resid_mult * mixture
        deviation = result_part - teacher[span].astype(jnp.float32)
        masked = valid_float[span, None] * deviation
        d_result = masked * (all_tokens / (2.0 * valid_count))
        results.append(result_part.astype(jnp.bfloat16))
        d_results.append(d_result)
        d_mix_out.append((resid_mult * d_result).astype(jnp.bfloat16))
        d_mix_in.append(gather(d_mix_out[-1]))
        own_loss = own_loss + jnp.sum(masked * deviation)
    d_result = jnp.concatenate(d_results, 0)
    kept_experts = own_experts // 2
    grad_rows = model_width + w_out.shape[1]
    flat_rows = kept_experts * grad_rows
    row_units = 2 * grad_rows // (flat_rows >> len(far))
    side = side_of(near)
    digits, rest = [], own_loss
    for _ in range(3):
        digits.append(lax.reduce_precision(rest, 8, 7))
        rest = rest - digits[-1]
    device = lax.axis_index("rep") * shard_count + shard_at
    sets = -(-lax.axis_size("rep") * shard_count // own_rows)
    place, digits = jnp.stack([side, device]), jnp.stack(digits)
    columns = w_in.shape[2]
    shapes = (own_experts, model_width, columns), (own_experts, grad_rows - model_width, columns)
    half_units = row_units * flat_rows // grad_rows // 4
    second_at = (1, 0) if kept_experts > 1 else (0, 2 * half_units)
    targets = {}
    for across in range(2):
        for core in range(2):
            spot = []
            for bit, (expert, unit) in ((far[0], (0, 0)), (far[-1], second_at)):
                half = side_of(bit) if across == 0 else 1 - side_of(bit)
                owner = side if core == 0 else 1 - side
                spot += [owner * kept_experts + expert, unit + half * half_units]
            targets[across, core] = jnp.stack(spot)
    order = jnp.arange(kept_experts, dtype=jnp.int32)
    order_sent = order + (1 - side) * kept_experts
    order_kept = order + side * kept_experts
    d_rows, d_gates, backward = [], [], []
    for d_mix, (gates_own, _, gate_up, hidden_gated), tokens in zip(d_mix_in, forward, tokens_in):
        if not backward:
            gates_own = after(gates_own, place, digits, *targets.values())
        if len(backward) == CHUNKS - 1:
            order_all = jnp.concatenate([order_sent, order_kept])
            partial_grads = experts_grads(order_all, backward, False, row_units)[0]
            gates_own = after(gates_own, partial_grads)
        d_rows_part, d_gate_up, d_gates_part = experts_backward(
            d_mix, gates_own, gate_up, w_in, w_out
        )
        d_rows.append(scatter(d_rows_part))
        d_gates.append(d_gates_part)
        backward.append((tokens, d_mix, d_gate_up, hidden_gated))
    first_rows = d_rows[0]
    d_rows = jnp.concatenate(d_rows, 0).astype(jnp.float32)
    sent = experts_grads(order_sent, backward[-1:], True, row_units, partial_grads, 0)
    unit_rows = flat_rows // 2 >> len(far)
    sent = [part.reshape(-1, unit_rows, columns) for part in sent]
    other = [exchange(part, near) for part in sent]
    kept = experts_grads(
        after(order_kept, *sent), backward[-1:], False, row_units, partial_grads, kept_experts
    )
    kept = after(kept[0].reshape(-1, unit_rows, columns), first_rows)
    half_rows = flat_rows // 2 // unit_rows
    if kept_experts > 1:
        other_first = jnp.concatenate(other[: kept_experts // 2], 0)
        other_second = jnp.concatenate(other[kept_experts // 2 :], 0)
        spots = ((kept, 0), (other_first, 0)), ((kept, half_rows), (other_second, 0))
    else:
        spots = ((kept, 0), (other[0], 0)), ((kept, half_rows), (other[0], half_rows))
    moe_sent_first, moe_first = halve(spots[0], far[0], 0, half_rows)
    moe_sent_second, moe_second = halve(spots[1], far[-1], 0, half_rows)
    d_gates = [after(part, moe_sent_first, moe_sent_second) for part in d_gates]
    d_gates = [
        part[:, :own_experts].reshape(shard_count, chunk_rows, own_experts) for part in d_gates
    ]
    d_gates = jnp.concatenate(d_gates, 1).reshape(shard_count * row_count, own_experts)
    d_gates = lax.all_to_all(d_gates, "shard", split_axis=0, concat_axis=1, tiled=True)
    d_rows = after(d_rows, moe_sent_first, moe_sent_second)
    d_logits = (gates * (d_gates - jnp.sum(gates * d_gates, -1, keepdims=True))).astype(
        jnp.bfloat16
    )
    d_normed_ffn = d_rows + dot_nt(d_logits, router_full)
    grad_router = dot_tn(d_logits, normed_ffn)
    d_norm_mid, grad_gain_ffn = norm_back(d_normed_ffn, middle, scale_ffn, gain_ffn)
    d_middle = d_result + d_norm_mid
    d_branch = (resid_mult * d_middle).astype(jnp.bfloat16)
    d_attended = dot_nt(d_branch, output_full).astype(
        jnp.bfloat16
    )
    query_grad_rows, kv_grad_all = attention_backward(
        bias, query_rows, keys_all, values_all, log_norm, d_attended, tables, tables_own
    )
    query_grad_rows, kv_grad_all, moe_first[-1], moe_second[-1] = lax.optimization_barrier(
        (query_grad_rows, kv_grad_all, moe_first[-1], moe_second[-1])
    )
    d_normed_kv, d_normed_query, sent_first, kept_first, sent_second, kept_second = attention_grads(
        place, digits, sets, shard_count, normed_attn, query_grad_rows,
        normed_all, kv_grad_all, attended, d_branch, grad_gain_ffn[None], grad_router,
        query_full, kv_full, input_all, hidden_in
    )
    kv_scattered = scatter(d_normed_kv)
    d_normed_query = after(d_normed_query, sent_first, sent_second)
    d_normed_attn = kv_scattered.astype(jnp.float32) + d_normed_query
    d_norm_in, _ = norm_back(d_normed_attn, input_float, scale_attn, gain_attn)
    d_input = d_middle + d_norm_in
    for bit_first, bit_second in zip(far[1:], far[::-1][1:]):
        _, moe_first = halve(moe_first, bit_first, 0)
        _, moe_second = halve(moe_second, bit_second, 0)
    def by_piece(block):
        return block.reshape(shard_count, -1, piece_rows, block.shape[2])

    sent_first, sent_second, moe_first[-1], moe_second[-1] = lax.optimization_barrier(
        (sent_first, sent_second, moe_first[-1], moe_second[-1])
    )
    moe_first, moe_second = add_parts(moe_first), add_parts(moe_second)
    sent_first, sent_second = lax.optimization_barrier(
        (sent_first, sent_second, moe_first, moe_second)
    )[:2]
    first = [by_piece(kept_first), exchange(by_piece(sent_first), near)]
    second = [by_piece(kept_second), exchange(by_piece(sent_second), near)]
    for bit_first, bit_second in zip(far[:0:-1], far[:-1]):
        moe_first = double(moe_first, bit_first, 0)
        moe_second = double(moe_second, bit_second, 0)
    for bit_first, bit_second in zip(far, far[::-1]):
        _, first = halve(first, bit_first, 1)
        _, second = halve(second, bit_second, 1)
        if bit_first == far[0]:
            first[-1] = after(first[-1], moe_first, moe_second)
            second[-1] = after(second[-1], moe_first, moe_second)
    first[-1] = after(first[-1], kv_scattered)
    moe_first = after(moe_first, first[-1], second[-1])
    moe_second = after(moe_second, first[-1], second[-1])
    own_first, own_second = moe_first, moe_second
    far_first, far_second = exchange(own_first, far[0]), exchange(own_second, far[-1])
    near_own = exchange(own_first, near), exchange(own_second, near)
    joined = jnp.concatenate([add_parts(first), add_parts(second)], 3)
    joined = joined.reshape(shard_count, piece_rows, -1)
    joined = lax.psum_scatter(joined, "shard", scatter_dimension=0)
    def put(held, pieces, *where):
        pieces = [piece.reshape(-1, columns) for piece in pieces]
        return widen(targets[where], *pieces, shapes, row_units, held)

    held = put([], (own_first, own_second), 0, 0)
    held = put(held, near_own, 0, 1)
    *held, joined, d_input = lax.optimization_barrier((*held, joined, d_input))
    gathered = lax.all_gather(joined, "rep", axis=0)
    *held, far_first, far_second = lax.optimization_barrier((*held, far_first, far_second))
    near_far = exchange(far_first, near), exchange(far_second, near)
    held = put(held, (far_first, far_second), 1, 0)
    held = put(held, near_far, 1, 1)
    sum_in, sum_out = held

    def row_of(at, order):
        return sum(((at // bit) % 2) << (len(order) - 1 - turn) for turn, bit in enumerate(order))

    pairs = tuple(
        (row_of(at, [near] + far), row_of(at, [near] + far[::-1])) for at in range(lax.axis_size("rep"))
    )
    sum_query, sum_key, sum_value, sum_output, sum_router, sum_gains, loss = finish(
        gathered, pairs, (query_width, half_width, kv_width), 3 * sets, expert_count
    )
    loss = loss[0, 0] / (model_width * valid_count)
    return (
        jnp.concatenate(results, 0),
        loss,
        d_input,
        sum_gains[0],
        sum_query,
        sum_key,
        sum_value,
        sum_output,
        sum_gains[1],
        sum_router,
        sum_in,
        sum_out,
    )


def solution(mesh):
    in_specs = (
        P(("rep", "shard"), None),
        P(("rep", "shard")),
        P(("rep", "shard"), None),
        P(("rep", "shard"), None),
        P("shard"),
        P("shard", None),
        P("shard", None),
        P("shard", None),
        P("shard", None),
        P("shard"),
        P("shard", None),
        P("shard", None, None),
        P("shard", None, None),
    )
    out_specs = (
        P(("rep", "shard"), None),
        P(),
        P(("rep", "shard"), None),
        P("shard"),
        P("shard", None),
        P("shard", None),
        P("shard", None),
        P("shard", None),
        P("shard"),
        P("shard", None),
        P("shard", None, None),
        P("shard", None, None),
    )
    return jax.shard_map(body, mesh=mesh, in_specs=in_specs, out_specs=out_specs, check_vma=False)
```

```python
import functools

import jax
import jax.numpy as jnp
from jax import lax
from jax.experimental import pallas as pl
from jax.experimental.pallas import tpu as pltpu
from jax.sharding import PartitionSpec as P

HEADS = 16
KV_HEADS = 8
HEAD_DIM = 64
TOP = 8
BLOCK = 256
CHUNKS = 2
SMALL_COST = pl.CostEstimate(flops=1000000, bytes_accessed=100000, transcendentals=0)


norm_eps = 1e-06
resid_mult = 0.22
attn_mult = 0.015625
rope_base = 10000.0
very_low = -1e30


def rope_tables(positions):
    half_dim = HEAD_DIM // 2
    frequency = rope_base ** (-jnp.arange(half_dim, dtype=jnp.float32) / half_dim)
    angles = positions.astype(jnp.float32)[:, None] * frequency[None, :]
    cosine, sine = jnp.cos(angles), jnp.sin(angles)
    return (
        jnp.concatenate([cosine] * 4, 1),
        jnp.concatenate([-sine, sine, -sine, sine], 1),
    )


def rms_scale(values):
    return lax.rsqrt(jnp.mean(values * values, axis=-1, keepdims=True) + norm_eps)


def norm_back(d_normed, values, scale_vals, gain_vec):
    scaled_grad = d_normed * gain_vec
    d_gain = jnp.sum(d_normed * values * scale_vals, 0)
    d_values = scale_vals * (
        scaled_grad
        - values * scale_vals * scale_vals * jnp.mean(scaled_grad * values, axis=-1, keepdims=True)
    )
    return (d_values, d_gain)


LANES = 128
ROW_STEP = 256
EXPERT_STEP = 512


def row_chunks(count):
    step = min(count, EXPERT_STEP)
    return [pl.ds(at, step) for at in range(0, count, step)]


def pick_lane(values, lane):
    lanes = lax.broadcasted_iota(jnp.int32, values.shape, 1)
    return jnp.sum(jnp.where(lanes == lane, values, 0.0), axis=1, keepdims=True)


def dot_nn(left, right):
    return jnp.dot(left, right, preferred_element_type=jnp.float32)


def dot_nt(left, right):
    return lax.dot_general(left, right, (((1,), (1,)), ((), ())), preferred_element_type=jnp.float32)


def dot_tn(left, right):
    return lax.dot_general(left, right, (((0,), (0,)), ((), ())), preferred_element_type=jnp.float32)


def experts_forward_kernel(x_ref, gate_ref, in_ref, out_ref, mix_ref, gate_up_ref, hidden_ref, total):
    expert = pl.program_id(0)
    units = out_ref.shape[1]

    @pl.when(expert == 0)
    def _():
        total[...] = jnp.zeros_like(total)

    for rows in row_chunks(x_ref.shape[0]):
        gate_up = dot_nn(x_ref[rows, :], in_ref[0])
        gate_up_ref[0, rows, :] = gate_up
        gate_vals = gate_up[:, :units]
        silu_gate = gate_vals / (1.0 + jnp.exp(-gate_vals))
        weight = pick_lane(gate_ref[rows, :], expert)
        hidden = (silu_gate * gate_up[:, units:] * weight).astype(jnp.bfloat16)
        hidden_ref[0, rows, :] = hidden
        total[rows, :] += dot_nn(hidden, out_ref[0])

    @pl.when(expert == pl.num_programs(0) - 1)
    def _():
        mix_ref[...] = total[...].astype(mix_ref.dtype)


def experts_forward(tokens, gates_own, w_in, w_out):
    count, width = tokens.shape
    experts, units = w_out.shape[0], w_out.shape[1]
    return pl.pallas_call(
        experts_forward_kernel,
        grid=(experts,),
        in_specs=[
            pl.BlockSpec((count, width), lambda e: (0, 0)),
            pl.BlockSpec((count, LANES), lambda e: (0, 0)),
            pl.BlockSpec((1, width, 2 * units), lambda e: (e, 0, 0)),
            pl.BlockSpec((1, units, width), lambda e: (e, 0, 0)),
        ],
        out_specs=[
            pl.BlockSpec((count, width), lambda e: (0, 0)),
            pl.BlockSpec((1, count, 2 * units), lambda e: (e, 0, 0)),
            pl.BlockSpec((1, count, units), lambda e: (e, 0, 0)),
        ],
        out_shape=[
            jax.ShapeDtypeStruct((count, width), jnp.bfloat16),
            jax.ShapeDtypeStruct((experts, count, 2 * units), jnp.float32),
            jax.ShapeDtypeStruct((experts, count, units), jnp.bfloat16),
        ],
        scratch_shapes=[pltpu.VMEM((count, width), jnp.float32)],
        compiler_params=pltpu.CompilerParams(vmem_limit_bytes=VMEM_BYTES),
        cost_estimate=SMALL_COST,
        name="experts_forward",
    )(tokens, gates_own, w_in, w_out)


def experts_backward_kernel(
    dmix_ref, gate_ref, gate_up_ref, in_ref, out_ref, drows_ref, dgate_up_ref, dgates_ref, total
):
    expert = pl.program_id(0)
    units = out_ref.shape[1]
    lanes = lax.broadcasted_iota(jnp.int32, (1, LANES), 1)

    @pl.when(expert == 0)
    def _():
        total[...] = jnp.zeros_like(total)
        dgates_ref[...] = jnp.zeros_like(dgates_ref)

    for rows in row_chunks(dmix_ref.shape[0]):
        pulled = dot_nt(dmix_ref[rows, :], out_ref[0])
        gate_vals = gate_up_ref[0, rows, :units]
        up_vals = gate_up_ref[0, rows, units:]
        sigmoid = 1.0 / (1.0 + jnp.exp(-gate_vals))
        silu_gate = gate_vals * sigmoid
        weight = pick_lane(gate_ref[rows, :], expert)
        d_up = pulled * silu_gate
        own = jnp.sum(d_up * up_vals, axis=1, keepdims=True)
        own = jnp.where(lanes == expert, own, 0.0)
        d_up = d_up * weight
        d_gate = (pulled * weight) * up_vals * (sigmoid + silu_gate * (1.0 - sigmoid))
        dgate_up_ref[0, rows, :units] = d_gate.astype(jnp.bfloat16)
        dgate_up_ref[0, rows, units:] = d_up.astype(jnp.bfloat16)
        total[rows, :] += dot_nt(dgate_up_ref[0, rows, :], in_ref[0])
        dgates_ref[rows, :] += own

    @pl.when(expert == pl.num_programs(0) - 1)
    def _():
        drows_ref[...] = total[...].astype(drows_ref.dtype)


def experts_backward(d_mix, gates_own, gate_up, w_in, w_out):
    count, width = d_mix.shape
    experts, units = w_out.shape[0], w_out.shape[1]
    return pl.pallas_call(
        experts_backward_kernel,
        grid=(experts,),
        in_specs=[
            pl.BlockSpec((count, width), lambda e: (0, 0)),
            pl.BlockSpec((count, LANES), lambda e: (0, 0)),
            pl.BlockSpec((1, count, 2 * units), lambda e: (e, 0, 0)),
            pl.BlockSpec((1, width, 2 * units), lambda e: (e, 0, 0)),
            pl.BlockSpec((1, units, width), lambda e: (e, 0, 0)),
        ],
        out_specs=[
            pl.BlockSpec((count, width), lambda e: (0, 0)),
            pl.BlockSpec((1, count, 2 * units), lambda e: (e, 0, 0)),
            pl.BlockSpec((count, LANES), lambda e: (0, 0)),
        ],
        out_shape=[
            jax.ShapeDtypeStruct((count, width), jnp.bfloat16),
            jax.ShapeDtypeStruct((experts, count, 2 * units), jnp.bfloat16),
            jax.ShapeDtypeStruct((count, LANES), jnp.float32),
        ],
        scratch_shapes=[pltpu.VMEM((count, width), jnp.float32)],
        compiler_params=pltpu.CompilerParams(vmem_limit_bytes=VMEM_BYTES),
        cost_estimate=SMALL_COST,
        name="experts_backward",
    )(d_mix, gates_own, gate_up, w_in, w_out)


def experts_grads_kernel(outputs, units, based, order_ref, *refs):
    grads_refs, refs = refs[-outputs:], refs[:-outputs]
    base_ref, refs = (refs[0], refs[1:]) if based else (None, refs)
    count = len(refs) // 4
    width = refs[0].shape[1]
    grad_in, grad_out = None, None
    for at in range(count):
        x_ref, dmix_ref, dgate_up_ref, hidden_ref = refs[4 * at : 4 * at + 4]
        part_in = dot_tn(x_ref[...], dgate_up_ref[0])
        part_out = dot_tn(hidden_ref[0], dmix_ref[...])
        grad_in = part_in if grad_in is None else grad_in + part_in
        grad_out = part_out if grad_out is None else grad_out + part_out
    tall, short = width // units, grad_out.shape[0] // units

    def put(ref):
        for at in range(units):
            start = at * (tall + short)
            for first, size, value in (
                (start, tall, grad_in[at * tall : (at + 1) * tall]),
                (start + tall, short, grad_out[at * short : (at + 1) * short]),
            ):
                span = slice(first, first + size)
                if based:
                    value = value + base_ref[0, span, :].astype(jnp.float32)
                ref[span, :] = value.astype(jnp.bfloat16)

    if outputs == 1:
        put(grads_refs[0].at[0])
        return
    for at in range(outputs):
        pl.when(pl.program_id(0) == at)(functools.partial(put, grads_refs[at]))


def experts_grads(order, chunks, apart, row_units, base=None, base_at=0):
    count, width = chunks[0][0].shape
    units = chunks[0][3].shape[2]
    experts = order.shape[0]
    specs = [
        pl.BlockSpec((count, width), lambda e, order: (0, 0)),
        pl.BlockSpec((count, width), lambda e, order: (0, 0)),
        pl.BlockSpec((1, count, 2 * units), lambda e, order: (order[e], 0, 0)),
        pl.BlockSpec((1, count, units), lambda e, order: (order[e], 0, 0)),
    ]
    rows, columns = width + units, 2 * units
    base_specs = []
    if base is not None:
        base_specs = [pl.BlockSpec((1, rows, columns), lambda e, order: (base_at + e, 0, 0))]
    if apart and experts > 1:
        outputs = experts
        out_specs = [pl.BlockSpec((rows, columns), lambda e, order: (0, 0))] * experts
        out_shape = [jax.ShapeDtypeStruct((rows, columns), jnp.bfloat16)] * experts
    else:
        outputs = 1
        out_specs = [pl.BlockSpec((1, rows, columns), lambda e, order: (e, 0, 0))]
        out_shape = [jax.ShapeDtypeStruct((experts, rows, columns), jnp.bfloat16)]
    grads = pl.pallas_call(
        functools.partial(experts_grads_kernel, outputs, row_units, base is not None),
        grid_spec=pltpu.PrefetchScalarGridSpec(
            num_scalar_prefetch=1,
            grid=(experts,),
            in_specs=base_specs + specs * len(chunks),
            out_specs=out_specs,
        ),
        out_shape=out_shape,
        compiler_params=pltpu.CompilerParams(vmem_limit_bytes=48 * MIB),
        cost_estimate=SMALL_COST,
        name="experts_grads",
    )(order, *([] if base is None else [base]), *[part for chunk in chunks for part in chunk])
    return grads


def widen_kernel(steps, spot_ref, first_ref, second_ref, *refs):
    gin_ref, gout_ref = refs[-2:]
    tall = gin_ref.shape[1]

    def put(piece_ref):
        gin_ref[0] = piece_ref[:tall, :].astype(jnp.float32)
        gout_ref[0] = piece_ref[tall:, :].astype(jnp.float32)

    at = pl.program_id(0)
    pl.when(at < steps)(functools.partial(put, first_ref))
    pl.when(at >= steps)(functools.partial(put, second_ref))


def widen(spot, first, second, shapes, units, held):
    rows, columns = shapes[0][1] + shapes[1][1], first.shape[1]
    unit = rows // units
    steps = first.shape[0] // unit

    def place(at, spot):
        late = at >= steps
        expert = jnp.where(late, spot[2], spot[0])
        return (expert, jnp.where(late, spot[3] + at - steps, spot[1] + at), 0)

    return pl.pallas_call(
        functools.partial(widen_kernel, steps),
        grid_spec=pltpu.PrefetchScalarGridSpec(
            num_scalar_prefetch=1,
            grid=(2 * steps,),
            in_specs=[
                pl.BlockSpec((unit, columns), lambda at, spot: (jnp.minimum(at, steps - 1), 0)),
                pl.BlockSpec((unit, columns), lambda at, spot: (jnp.maximum(at - steps, 0), 0)),
            ]
            + [pl.BlockSpec(memory_space=pl.ANY)] * len(held),
            out_specs=[
                pl.BlockSpec((1, shape[1] // units, columns), place) for shape in shapes
            ],
        ),
        out_shape=[jax.ShapeDtypeStruct(shape, jnp.float32) for shape in shapes],
        input_output_aliases={3 + at: at for at in range(len(held))},
        compiler_params=pltpu.CompilerParams(vmem_limit_bytes=20 * MIB),
        cost_estimate=SMALL_COST,
        name="widen",
    )(spot, first, second, *held)


def finish_kernel(
    spots, widths, digits, piece_ref, query_ref, key_ref, value_ref, output_ref, router_ref, gain_ref,
    loss_ref, small_ref
):
    query_width, half, kv_width = widths
    experts = router_ref.shape[1]
    rows = piece_ref.shape[1]
    for at, (first, second) in enumerate(spots):
        first_at = slice(first * rows, (first + 1) * rows)
        second_at = slice(second * rows, (second + 1) * rows)
        block = piece_ref[at].astype(jnp.float32)
        query_ref[first_at, :] = block[:, :query_width]
        start = query_width + half
        output_ref[first_at, :half] = block[:, query_width:start]
        small_ref[first_at, :] = block[:, start : start + LANES]
        start = start + LANES
        key_ref[second_at, :] = block[:, start : start + kv_width]
        value_ref[second_at, :] = block[:, start + kv_width : start + 2 * kv_width]
        output_ref[second_at, half:] = block[:, start + 2 * kv_width :]
    router_ref[...] = small_ref[:, :experts]
    turned = small_ref[...].T
    gain_ref[...] = turned[experts : experts + 8]
    row = lax.broadcasted_iota(jnp.int32, turned.shape, 0) - experts - 2
    loss = jnp.sum(jnp.where((row >= 0) & (row < digits), turned, 0.0))
    loss_ref[...] = jnp.full(loss_ref.shape, loss, jnp.float32)


def finish(pieces, spots, widths, digits, experts):
    count, rows, _ = pieces.shape
    query_width, half, kv_width = widths
    return pl.pallas_call(
        functools.partial(finish_kernel, spots, widths, digits),
        in_specs=[whole_spec()],
        out_specs=[whole_spec()] * 7,
        out_shape=[
            jax.ShapeDtypeStruct((count * rows, columns), jnp.float32)
            for columns in (query_width, kv_width, kv_width, 2 * half, experts)
        ]
        + [jax.ShapeDtypeStruct((8, columns), jnp.float32) for columns in (count * rows, LANES)],
        scratch_shapes=[pltpu.VMEM((count * rows, LANES), jnp.float32)],
        compiler_params=pltpu.CompilerParams(vmem_limit_bytes=20 * MIB),
        cost_estimate=SMALL_COST,
        name="finish",
    )(pieces)


def attention_grads_kernel(
    sets,
    side_ref, digits_ref, normed_ref, dquery_ref, all_ref, dkv_ref, attended_ref, dbranch_ref,
    gain_ref, router_ref,
    wq_ref, wkv_ref, input_ref, own_ref,
    dnormed_kv_ref, dnormed_query_ref, sent_first, kept_first, sent_second, kept_second,
    first_ref, second_ref
):
    query_width = dquery_ref.shape[1]
    half = dbranch_ref.shape[1] // 2
    kv_width = dkv_ref.shape[1]
    shards, rows = kept_first.shape[0], kept_first.shape[1]

    def gain_of(d_normed, block):
        values = block.astype(jnp.float32)
        scale = lax.rsqrt(jnp.mean(values * values, axis=-1, keepdims=True) + norm_eps)
        return jnp.sum(d_normed * values * scale, axis=0, keepdims=True)

    def put(ref, columns, value):
        ref[:, :, columns] = value.astype(jnp.bfloat16).reshape(shards, 2 * rows, -1)

    d_normed = dot_nt(dquery_ref[...], wq_ref[...])
    dnormed_query_ref[...] = d_normed
    gain = gain_of(d_normed, own_ref[...])
    for start in range(0, all_ref.shape[0], ROW_STEP):
        span = pl.ds(start, ROW_STEP)
        d_normed = dot_nt(dkv_ref[span, :], wkv_ref[...])
        dnormed_kv_ref[span, :] = d_normed.astype(jnp.bfloat16)
        gain = gain + gain_of(d_normed, input_ref[span, :])
    put(second_ref, slice(0, kv_width), dot_tn(all_ref[...], dkv_ref[...]))
    put(first_ref, slice(0, query_width), dot_tn(normed_ref[...], dquery_ref[...]))
    grad_output = dot_tn(attended_ref[...], dbranch_ref[...])
    put(first_ref, slice(query_width, query_width + half), grad_output[:, :half])
    put(second_ref, slice(kv_width, kv_width + half), grad_output[:, half:])
    experts, width = router_ref.shape
    row = lax.broadcasted_iota(jnp.int32, (LANES - experts, width), 0)
    spot = lax.broadcasted_iota(jnp.int32, row.shape, 1) % (2 * rows)
    rest = jnp.where(row == 0, gain, jnp.where(row == 1, gain_ref[...], 0.0))
    for at in range(digits_ref.shape[0]):
        for turn in range(sets):
            here = (row == 2 + at * sets + turn) & (spot == side_ref[1] - 2 * rows * turn)
            rest = jnp.where(here, digits_ref[at], rest)
    small = jnp.concatenate([router_ref[...], rest], 0).T
    put(first_ref, slice(query_width + half, first_ref.shape[2]), small)
    kept_at = pl.ds(pl.multiple_of(side_ref[0] * rows, rows), rows)
    sent_at = pl.ds(pl.multiple_of((1 - side_ref[0]) * rows, rows), rows)
    sent_first[...] = first_ref[:, sent_at, :]
    sent_second[...] = second_ref[:, sent_at, :]
    kept_first[...] = first_ref[:, kept_at, :]
    kept_second[...] = second_ref[:, kept_at, :]


def attention_grads(
    side, digits, sets, shards, normed, d_query, normed_all, d_kv, attended, d_branch, gain, router,
    w_query, w_kv, input_all, hidden_in
):
    width = normed.shape[1]
    half = d_branch.shape[1] // 2
    rows = width // shards // 2
    widths = (d_query.shape[1] + half + LANES, d_kv.shape[1] + half)
    return pl.pallas_call(
        functools.partial(attention_grads_kernel, sets),
        in_specs=[pl.BlockSpec(memory_space=pltpu.SMEM)] * 2 + [whole_spec()] * 12,
        out_specs=[whole_spec()] * 6,
        out_shape=[
            jax.ShapeDtypeStruct(input_all.shape, jnp.bfloat16),
            jax.ShapeDtypeStruct(hidden_in.shape, jnp.float32),
        ]
        + [
            jax.ShapeDtypeStruct((shards, rows, columns), jnp.bfloat16)
            for columns in (widths[0], widths[0], widths[1], widths[1])
        ],
        scratch_shapes=[
            pltpu.VMEM((shards, 2 * rows, columns), jnp.bfloat16) for columns in widths
        ],
        compiler_params=pltpu.CompilerParams(vmem_limit_bytes=60 * MIB),
        cost_estimate=SMALL_COST,
        name="attention_grads",
    )(
        side, digits, normed, d_query, normed_all, d_kv, attended, d_branch, gain, router,
        w_query, w_kv, input_all, hidden_in,
    )


MIB = 1024 * 1024
VMEM_BYTES = 60 * MIB


def swap_halves(values):
    lanes = lax.broadcasted_iota(jnp.int32, values.shape, 1)
    ahead = pltpu.roll(values, LANES - HEAD_DIM // 2, 1)
    behind = pltpu.roll(values, HEAD_DIM // 2, 1)
    return jnp.where(lanes % HEAD_DIM < HEAD_DIM // 2, ahead, behind)


def stack_heads(block, parity):
    values = block.astype(jnp.float32)
    lanes = lax.broadcasted_iota(jnp.int32, values.shape, 1)
    low = jnp.where(lanes < HEAD_DIM, values, 0.0)
    high = values - low
    if parity == 0:
        high = pltpu.roll(high, HEAD_DIM, 1)
    else:
        low = pltpu.roll(low, HEAD_DIM, 1)
    return jnp.concatenate([low, high], 0).astype(jnp.bfloat16)


def unstack_heads(stacked, parity):
    rows = stacked.shape[0] // 2
    low, high = stacked[:rows], stacked[rows:]
    if parity == 0:
        high = pltpu.roll(high, HEAD_DIM, 1)
    else:
        low = pltpu.roll(low, HEAD_DIM, 1)
    lanes = lax.broadcasted_iota(jnp.int32, low.shape, 1)
    return jnp.where(lanes < HEAD_DIM, low, high)


def lane_block(at):
    return pl.ds(pl.multiple_of(at * LANES, LANES), LANES)


def attention_forward_kernel(
    bias_ref, side_ref, input_ref, own_ref, gain_ref, query_held, query_other, kv_held, kv_other,
    cos_ref, sin_ref, cos_own_ref, sin_own_ref,
    wq_out, wkv_out, normed_out, key_out, value_out, normed_own_ref, query_ref, attended_ref, norm_ref,
    all_ref, wq_parts, wkv_parts, normed_ref, key_ref, value_ref, scores, row_sems, in_sems, out_sems
):
    tokens, width = all_ref.shape
    kv_width = key_ref.shape[1]
    key_rows = tokens // bias_ref.shape[0]
    half_rows = query_held.shape[1]
    held_at = pl.ds(pl.multiple_of(side_ref[0] * half_rows, half_rows), half_rows)
    other_at = pl.ds(pl.multiple_of((1 - side_ref[0]) * half_rows, half_rows), half_rows)
    row_copies = []
    for at in range(tokens // ROW_STEP):
        span = pl.ds(at * ROW_STEP, ROW_STEP)
        copy = pltpu.make_async_copy(input_ref.at[span, :], all_ref.at[span, :], row_sems.at[at])
        copy.start()
        row_copies.append(copy)
    weight_copies = []
    for at, (source, target) in enumerate(
        (
            (kv_held, wkv_parts.at[:, held_at, :]),
            (kv_other, wkv_parts.at[:, other_at, :]),
            (query_held, wq_parts.at[:, held_at, :]),
            (query_other, wq_parts.at[:, other_at, :]),
        )
    ):
        copy = pltpu.make_async_copy(source, target, in_sems.at[at])
        copy.start()
        weight_copies.append(copy)
    wq_ref = wq_parts.reshape(width, wq_parts.shape[2])
    wkv_ref = wkv_parts.reshape(width, wkv_parts.shape[2])

    def normed_rows(block):
        values = block.astype(jnp.float32)
        scale = lax.rsqrt(jnp.mean(values * values, axis=-1, keepdims=True) + norm_eps)
        return (values * scale * gain_ref[...]).astype(jnp.bfloat16)

    normed_own = normed_rows(own_ref[...])
    normed_own_ref[...] = normed_own
    for at, copy in enumerate(row_copies):
        copy.wait()
        span = pl.ds(at * ROW_STEP, ROW_STEP)
        normed_ref[span, :] = normed_rows(all_ref[span, :])
    out_copies = [pltpu.make_async_copy(normed_ref, normed_out, out_sems.at[0])]
    out_copies[0].start()
    for copy in weight_copies:
        copy.wait()
    for at, (source, target) in enumerate(((wq_parts, wq_out), (wkv_parts, wkv_out))):
        out_copies.append(pltpu.make_async_copy(source, target, out_sems.at[1 + at]))
        out_copies[-1].start()

    def project(at, carry):
        rows = pl.ds(pl.multiple_of(at * ROW_STEP, ROW_STEP), ROW_STEP)
        linear = dot_nn(normed_ref[rows, :], wkv_ref[...])
        for col in range(0, kv_width, LANES):
            part = linear[:, col : col + LANES]
            turned = part * cos_ref[rows, :] + swap_halves(part) * sin_ref[rows, :]
            key_ref[rows, col : col + LANES] = turned.astype(jnp.bfloat16)
        value_ref[rows, :] = linear[:, kv_width:].astype(jnp.bfloat16)
        return carry

    lax.fori_loop(0, tokens // ROW_STEP, project, 0)
    for at, (source, target) in enumerate(((key_ref, key_out), (value_ref, value_out))):
        out_copies.append(pltpu.make_async_copy(source, target, out_sems.at[3 + at]))
        out_copies[-1].start()
    linear = dot_nn(normed_own, wq_ref[...])
    for col in range(0, wq_ref.shape[1], LANES):
        part = linear[:, col : col + LANES]
        turned = part * cos_own_ref[...] + swap_halves(part) * sin_own_ref[...]
        query_ref[:, col : col + LANES] = (turned.astype(jnp.bfloat16).astype(jnp.float32) * attn_mult).astype(jnp.bfloat16)

    def attend(pair, carry):
        lanes = lane_block(pair)
        turned_values = value_ref[:, lanes].astype(jnp.float32).T.astype(jnp.bfloat16)
        for parity in range(2):
            group = 2 * pair + parity
            stacked = stack_heads(query_ref[:, lane_block(group)], parity)
            top = None
            for at in range(bias_ref.shape[0]):
                rows = pl.ds(at * key_rows, key_rows)
                part = dot_nt(key_ref[rows, lanes], stacked)
                scores[rows, :] = part
                high = jnp.max(part, axis=0, keepdims=True) + bias_ref[at]
                top = high if top is None else jnp.maximum(top, high)
            total, gathered = None, None
            for at in range(bias_ref.shape[0]):
                rows = pl.ds(at * key_rows, key_rows)
                raised = jnp.exp(scores[rows, :] - (top - bias_ref[at]))
                part = jnp.sum(raised, axis=0, keepdims=True)
                mixed = dot_nn(
                    turned_values[:, at * key_rows : (at + 1) * key_rows], raised.astype(jnp.bfloat16)
                )
                total = part if total is None else total + part
                gathered = mixed if gathered is None else gathered + mixed
            gathered = (gathered / total).T
            attended_ref[:, lane_block(group)] = unstack_heads(gathered, parity).astype(jnp.bfloat16)
            norm_ref[pl.ds(group, 1), :] = top + jnp.log(total)
        return carry

    lax.fori_loop(0, kv_width // LANES, attend, 0)
    for copy in out_copies:
        copy.wait()


def far_spec():
    return pl.BlockSpec(memory_space=pl.ANY)


def whole_spec():
    return pl.BlockSpec(memory_space=pltpu.VMEM)


def attention_forward(bias, side, input_all, hidden_in, gain, query_pair, kv_pair, tables, tables_own):
    tokens, width = input_all.shape
    rows = hidden_in.shape[0]
    shards, half_rows, query_width = query_pair[0].shape
    kv_width = kv_pair[0].shape[2] // 2
    return pl.pallas_call(
        attention_forward_kernel,
        in_specs=[pl.BlockSpec(memory_space=pltpu.SMEM)] * 2
        + [far_spec()]
        + [whole_spec()] * 2
        + [far_spec()] * 4
        + [whole_spec()] * 4,
        out_specs=[far_spec()] * 5 + [whole_spec()] * 4,
        out_shape=[
            jax.ShapeDtypeStruct((shards, 2 * half_rows, query_width), jnp.bfloat16),
            jax.ShapeDtypeStruct((shards, 2 * half_rows, 2 * kv_width), jnp.bfloat16),
            jax.ShapeDtypeStruct((tokens, width), jnp.bfloat16),
            jax.ShapeDtypeStruct((tokens, kv_width), jnp.bfloat16),
            jax.ShapeDtypeStruct((tokens, kv_width), jnp.bfloat16),
            jax.ShapeDtypeStruct((rows, width), jnp.bfloat16),
            jax.ShapeDtypeStruct((rows, query_width), jnp.bfloat16),
            jax.ShapeDtypeStruct((rows, query_width), jnp.bfloat16),
            jax.ShapeDtypeStruct((KV_HEADS, 2 * rows), jnp.float32),
        ],
        scratch_shapes=[
            pltpu.VMEM((tokens, width), jnp.bfloat16),
            pltpu.VMEM((shards, 2 * half_rows, query_width), jnp.bfloat16),
            pltpu.VMEM((shards, 2 * half_rows, 2 * kv_width), jnp.bfloat16),
            pltpu.VMEM((tokens, width), jnp.bfloat16),
            pltpu.VMEM((tokens, kv_width), jnp.bfloat16),
            pltpu.VMEM((tokens, kv_width), jnp.bfloat16),
            pltpu.VMEM((tokens, 2 * rows), jnp.float32),
            pltpu.SemaphoreType.DMA((tokens // ROW_STEP,)),
            pltpu.SemaphoreType.DMA((4,)),
            pltpu.SemaphoreType.DMA((5,)),
        ],
        compiler_params=pltpu.CompilerParams(vmem_limit_bytes=VMEM_BYTES),
        cost_estimate=SMALL_COST,
        name="attention_forward",
    )(bias, side, input_all, hidden_in, gain, *query_pair, *kv_pair, *tables, *tables_own)


def attention_backward_kernel(
    bias_ref, query_ref, key_ref, value_ref, norm_ref, grad_ref, cos_ref, sin_ref, cos_own_ref, sin_own_ref,
    dquery_ref, dkv_ref, probs, dprobs, dkeys, dvalues
):
    tokens, kv_width = key_ref.shape
    key_rows = tokens // bias_ref.shape[0]

    def pull(pair, carry):
        lanes = lane_block(pair)
        turned_keys = key_ref[:, lanes].astype(jnp.float32).T.astype(jnp.bfloat16)
        for parity in range(2):
            group = 2 * pair + parity
            stacked = stack_heads(query_ref[:, lane_block(group)], parity)
            stacked_grad = stack_heads(grad_ref[:, lane_block(group)], parity)
            log_norm = norm_ref[pl.ds(group, 1), :]
            total = None
            for at in range(bias_ref.shape[0]):
                rows = pl.ds(at * key_rows, key_rows)
                part = dot_nt(key_ref[rows, lanes], stacked)
                prob = jnp.exp(part - (log_norm - bias_ref[at]))
                d_prob = dot_nt(value_ref[rows, lanes], stacked_grad)
                probs[rows, :] = prob
                dprobs[rows, :] = d_prob
                d_value = dot_nn(prob.astype(jnp.bfloat16), stacked_grad)
                dvalues[rows, :] = d_value if parity == 0 else dvalues[rows, :] + d_value
                weighted = jnp.sum(prob * d_prob, axis=0, keepdims=True)
                total = weighted if total is None else total + weighted
            d_query = None
            for at in range(bias_ref.shape[0]):
                rows = pl.ds(at * key_rows, key_rows)
                d_score = (probs[rows, :] * (dprobs[rows, :] - total)).astype(jnp.bfloat16)
                d_key = dot_nn(d_score, stacked)
                dkeys[rows, :] = d_key if parity == 0 else dkeys[rows, :] + d_key
                part = dot_nn(turned_keys[:, at * key_rows : (at + 1) * key_rows], d_score)
                d_query = part if d_query is None else d_query + part
            part = unstack_heads(d_query.T, parity) * attn_mult
            turned = part * cos_own_ref[...] - swap_halves(part) * sin_own_ref[...]
            dquery_ref[:, lane_block(group)] = turned.astype(jnp.bfloat16)
        part = dkeys[...]
        turned = part * cos_ref[...] - swap_halves(part) * sin_ref[...]
        dkv_ref[:, lanes] = turned.astype(jnp.bfloat16)
        dkv_ref[:, lane_block(pair + kv_width // LANES)] = dvalues[...].astype(jnp.bfloat16)
        return carry

    lax.fori_loop(0, kv_width // LANES, pull, 0)


def attention_backward(bias, query, key, value, log_norm, grad, tables, tables_own):
    tokens, kv_width = key.shape
    rows, width = query.shape
    return pl.pallas_call(
        attention_backward_kernel,
        in_specs=[pl.BlockSpec(memory_space=pltpu.SMEM)] + [whole_spec()] * 9,
        out_specs=[whole_spec()] * 2,
        out_shape=[
            jax.ShapeDtypeStruct((rows, width), jnp.bfloat16),
            jax.ShapeDtypeStruct((tokens, 2 * kv_width), jnp.bfloat16),
        ],
        scratch_shapes=[
            pltpu.VMEM((tokens, 2 * rows), jnp.float32),
            pltpu.VMEM((tokens, 2 * rows), jnp.float32),
            pltpu.VMEM((tokens, LANES), jnp.float32),
            pltpu.VMEM((tokens, LANES), jnp.float32),
        ],
        compiler_params=pltpu.CompilerParams(vmem_limit_bytes=28 * MIB),
        cost_estimate=SMALL_COST,
        name="attention_backward",
    )(bias, query, key, value, log_norm, grad, *tables, *tables_own)


def exchange(block, bit):
    count = lax.axis_size("rep")
    return lax.ppermute(block, "rep", [(at, at ^ bit) for at in range(count)])


def side_of(bit):
    return (lax.axis_index("rep") // bit) % 2


def after(value, *others):
    return lax.optimization_barrier((value, *others))[0]


def slices_of(parts, start, size, axis):
    return [
        lax.dynamic_slice_in_dim(part, base + start, size, axis)
        for part, base in ((part if isinstance(part, tuple) else (part, 0)) for part in parts)
    ]


def add_parts(parts):
    total = parts[0].astype(jnp.float32)
    for part in parts[1:]:
        total = total + part.astype(jnp.float32)
    return total.astype(jnp.bfloat16)


def halve(parts, bit, axis, length=None):
    length = parts[0].shape[axis] if length is None else length
    half = length // 2
    side = side_of(bit)
    sent = slices_of(parts, (1 - side) * half, half, axis)
    sent = sent[0] if len(sent) == 1 else add_parts(sent)
    kept = slices_of(parts, side * half, half, axis)
    return sent, kept + [exchange(sent, bit)]


def double(block, bit, axis):
    size = block.shape[axis]
    side = side_of(bit)
    held = lax.concatenate([block, block], axis)
    return lax.dynamic_update_slice_in_dim(held, exchange(block, bit), (1 - side) * size, axis)


def rep_bits():
    count = lax.axis_size("rep")
    return [1 << at for at in range(count.bit_length() - 1)]


def body(
    hidden_in,
    valid_mask,
    teacher,
    routes,
    attn_norm,
    w_query,
    w_key,
    w_value,
    w_output,
    ffn_norm,
    router,
    w_in,
    w_out,
):
    row_count, model_width = hidden_in.shape
    shard_count = lax.axis_size("shard")
    seq_tokens = row_count * shard_count
    all_tokens = seq_tokens * lax.axis_size("rep")
    shard_at = lax.axis_index("shard")
    tables = rope_tables(jnp.arange(seq_tokens, dtype=jnp.int32))
    tables_own = tuple(
        lax.dynamic_slice_in_dim(table, shard_at * row_count, row_count, 0) for table in tables
    )
    key_blocks = jnp.arange(seq_tokens // BLOCK, dtype=jnp.int32)
    bias = jnp.where(key_blocks <= shard_at * row_count // BLOCK, 0.0, very_low)
    bits = rep_bits()
    near, far = bits[0], bits[1:]

    def gather(block):
        return lax.all_gather(block, "shard", axis=0, tiled=True)

    def scatter(block):
        return lax.psum_scatter(block, "shard", scatter_dimension=0, tiled=True)

    kv_width = w_key.shape[1]
    query_width = w_query.shape[1]
    half_width = w_output.shape[1] // 2
    own_rows = w_query.shape[0]
    piece_rows = own_rows // lax.axis_size("rep")

    def piece_of(block, order):
        index = 0
        for at, bit in enumerate(order):
            index = index + side_of(bit) * (1 << at)
        return lax.dynamic_slice_in_dim(block, index * piece_rows, piece_rows, 0)

    order_first, order_second = far + [near], far[::-1] + [near]
    w_kv = jnp.concatenate([w_key, w_value], 1)
    input_all = gather(hidden_in)
    valid_float = valid_mask.astype(jnp.float32)
    expert_count = router.shape[1]
    small_parts = [
        jnp.concatenate([attn_norm, ffn_norm, router.reshape(-1)]).reshape(1, -1),
        routes.astype(jnp.bfloat16).reshape(1, -1),
        jnp.sum(valid_float).astype(jnp.bfloat16).reshape(1, 1),
    ]
    small_size, routes_size = small_parts[0].size, small_parts[1].size
    pieces = lax.all_gather(
        jnp.concatenate([piece_of(w_query, order_first), piece_of(w_kv, order_second)], 1),
        "shard",
        axis=0,
    )
    query_full = pieces[..., :query_width]
    kv_full = pieces[..., query_width:]
    small_parts = jnp.concatenate(small_parts, 1)
    for at, (bit_first, bit_second) in enumerate(zip(order_first[:-1], order_second[:-1])):
        if at == len(far) - 1:
            small_parts = after(small_parts, query_full, kv_full)
        query_full = double(query_full, bit_first, 1)
        kv_full = double(kv_full, bit_second, 1)
    small_all = gather(small_parts)
    query_full, kv_full = after(query_full, small_all), after(kv_full, small_all)
    query_pair = query_full, exchange(query_full, near)
    kv_pair = kv_full, exchange(kv_full, near)
    near_rows = own_rows // 2
    output_half = lax.dynamic_slice_in_dim(w_output, side_of(near) * near_rows, near_rows, 0)
    output_half = lax.all_gather(after(output_half, query_pair[0], kv_pair[0]), "shard", axis=0)
    gain_attn = small_all[:, :own_rows].reshape(-1).astype(jnp.float32)
    gain_ffn = small_all[:, own_rows : 2 * own_rows].reshape(-1)
    router_full = small_all[:, 2 * own_rows : small_size].reshape(-1, expert_count)
    routes_all = small_all[:, small_size : small_size + routes_size]
    valid_count = jnp.broadcast_to(jnp.sum(small_all[:, small_size + routes_size].astype(jnp.float32)), (8, LANES))
    for bit in bits:
        valid_count = valid_count + exchange(valid_count, bit)
    valid_count = valid_count[0, 0]
    input_float = hidden_in.astype(jnp.float32)
    scale_attn = rms_scale(input_float)
    (
        query_full, kv_full, normed_all, keys_all, values_all, normed_attn, query_rows, attended, log_norm
    ) = attention_forward(
        bias, jnp.reshape(side_of(near), (1,)), input_all, hidden_in, gain_attn[None],
        query_pair, kv_pair, tables, tables_own,
    )
    query_full = query_full.reshape(model_width, query_width)
    kv_full = kv_full.reshape(model_width, 2 * kv_width)
    output_half, attended = lax.optimization_barrier((output_half, attended))
    output_full = double(output_half, near, 1).reshape(own_rows * shard_count, -1)
    branch = dot_nn(attended, output_full)
    middle = input_float + resid_mult * branch
    scale_ffn = rms_scale(middle)
    normed_ffn = (middle * scale_ffn * gain_ffn).astype(jnp.bfloat16)
    own_experts = w_in.shape[0]
    expert_ids = jnp.arange(expert_count, dtype=jnp.bfloat16)
    chunk_rows = row_count // CHUNKS
    spans = [slice(at * chunk_rows, (at + 1) * chunk_rows) for at in range(CHUNKS)]
    tokens_in = [gather(normed_ffn[span]) for span in spans]
    routes_all = routes_all.reshape(shard_count, row_count, -1)
    gates, forward = [], []
    for span, tokens in zip(spans, tokens_in):
        logits = dot_nn(tokens, router_full)
        routes_part = routes_all[:, span].reshape(shard_count * chunk_rows, -1)
        chosen = jnp.any(routes_part[..., None] == expert_ids, 1)
        masked = jnp.where(chosen, logits, very_low)
        raised = jnp.where(chosen, jnp.exp(masked - jnp.max(masked, -1, keepdims=True)), 0.0)
        gates_part = raised / jnp.sum(raised, -1, keepdims=True)
        gates_own = lax.dynamic_slice_in_dim(gates_part, shard_at * own_experts, own_experts, 1)
        gates_own = jnp.pad(gates_own, ((0, 0), (0, LANES - own_experts)))
        gates.append(lax.dynamic_slice_in_dim(gates_part, shard_at * chunk_rows, chunk_rows, 0))
        if not forward:
            gates_own = after(gates_own, valid_count)
        forward.append((gates_own, *experts_forward(tokens, gates_own, w_in, w_out)))
    gates = jnp.concatenate(gates, 0)
    results, d_results, d_mix_out, d_mix_in, own_loss = [], [], [], [], 0.0
    for span, (_, mix_part, _, _) in zip(spans, forward):
        mixture = scatter(mix_part)
        if d_mix_out:
            mixture = after(mixture, d_mix_out[-1])
        mixture = mixture.astype(jnp.float32)
        result_part = middle[span] + resid_mult * mixture
        deviation = result_part - teacher[span].astype(jnp.float32)
        masked = valid_float[span, None] * deviation
        d_result = masked * (all_tokens / (2.0 * valid_count))
        results.append(result_part.astype(jnp.bfloat16))
        d_results.append(d_result)
        d_mix_out.append((resid_mult * d_result).astype(jnp.bfloat16))
        d_mix_in.append(gather(d_mix_out[-1]))
        own_loss = own_loss + jnp.sum(masked * deviation)
    d_result = jnp.concatenate(d_results, 0)
    kept_experts = own_experts // 2
    grad_rows = model_width + w_out.shape[1]
    flat_rows = kept_experts * grad_rows
    row_units = 2 * grad_rows // (flat_rows >> len(far))
    side = side_of(near)
    digits, rest = [], own_loss
    for _ in range(3):
        digits.append(lax.reduce_precision(rest, 8, 7))
        rest = rest - digits[-1]
    device = lax.axis_index("rep") * shard_count + shard_at
    sets = -(-lax.axis_size("rep") * shard_count // own_rows)
    place, digits = jnp.stack([side, device]), jnp.stack(digits)
    columns = w_in.shape[2]
    shapes = (own_experts, model_width, columns), (own_experts, grad_rows - model_width, columns)
    half_units = row_units * flat_rows // grad_rows // 4
    second_at = (1, 0) if kept_experts > 1 else (0, 2 * half_units)
    targets = {}
    for across in range(2):
        for core in range(2):
            spot = []
            for bit, (expert, unit) in ((far[0], (0, 0)), (far[-1], second_at)):
                half = side_of(bit) if across == 0 else 1 - side_of(bit)
                owner = side if core == 0 else 1 - side
                spot += [owner * kept_experts + expert, unit + half * half_units]
            targets[across, core] = jnp.stack(spot)
    order = jnp.arange(kept_experts, dtype=jnp.int32)
    order_sent = order + (1 - side) * kept_experts
    order_kept = order + side * kept_experts
    d_rows, d_gates, backward = [], [], []
    for d_mix, (gates_own, _, gate_up, hidden_gated), tokens in zip(d_mix_in, forward, tokens_in):
        if not backward:
            gates_own = after(gates_own, place, digits, *targets.values())
        if len(backward) == CHUNKS - 1:
            order_all = jnp.concatenate([order_sent, order_kept])
            partial_grads = experts_grads(order_all, backward, False, row_units)[0]
            gates_own = after(gates_own, partial_grads)
        d_rows_part, d_gate_up, d_gates_part = experts_backward(
            d_mix, gates_own, gate_up, w_in, w_out
        )
        d_rows.append(scatter(d_rows_part))
        d_gates.append(d_gates_part)
        backward.append((tokens, d_mix, d_gate_up, hidden_gated))
    first_rows = d_rows[0]
    d_rows = jnp.concatenate(d_rows, 0).astype(jnp.float32)
    sent = experts_grads(order_sent, backward[-1:], True, row_units, partial_grads, 0)
    unit_rows = flat_rows // 2 >> len(far)
    sent = [part.reshape(-1, unit_rows, columns) for part in sent]
    other = [exchange(part, near) for part in sent]
    kept = experts_grads(
        after(order_kept, *sent), backward[-1:], False, row_units, partial_grads, kept_experts
    )
    kept = after(kept[0].reshape(-1, unit_rows, columns), first_rows)
    half_rows = flat_rows // 2 // unit_rows
    if kept_experts > 1:
        other_first = jnp.concatenate(other[: kept_experts // 2], 0)
        other_second = jnp.concatenate(other[kept_experts // 2 :], 0)
        spots = ((kept, 0), (other_first, 0)), ((kept, half_rows), (other_second, 0))
    else:
        spots = ((kept, 0), (other[0], 0)), ((kept, half_rows), (other[0], half_rows))
    moe_sent_first, moe_first = halve(spots[0], far[0], 0, half_rows)
    moe_sent_second, moe_second = halve(spots[1], far[-1], 0, half_rows)
    d_gates = [after(part, moe_sent_first, moe_sent_second) for part in d_gates]
    d_gates = [
        part[:, :own_experts].reshape(shard_count, chunk_rows, own_experts) for part in d_gates
    ]
    d_gates = jnp.concatenate(d_gates, 1).reshape(shard_count * row_count, own_experts)
    d_gates = lax.all_to_all(d_gates, "shard", split_axis=0, concat_axis=1, tiled=True)
    d_rows = after(d_rows, moe_sent_first, moe_sent_second)
    d_logits = (gates * (d_gates - jnp.sum(gates * d_gates, -1, keepdims=True))).astype(
        jnp.bfloat16
    )
    d_normed_ffn = d_rows + dot_nt(d_logits, router_full)
    grad_router = dot_tn(d_logits, normed_ffn)
    d_norm_mid, grad_gain_ffn = norm_back(d_normed_ffn, middle, scale_ffn, gain_ffn)
    d_middle = d_result + d_norm_mid
    d_branch = (resid_mult * d_middle).astype(jnp.bfloat16)
    d_attended = dot_nt(d_branch, output_full).astype(
        jnp.bfloat16
    )
    query_grad_rows, kv_grad_all = attention_backward(
        bias, query_rows, keys_all, values_all, log_norm, d_attended, tables, tables_own
    )
    query_grad_rows, kv_grad_all, moe_first[-1], moe_second[-1] = lax.optimization_barrier(
        (query_grad_rows, kv_grad_all, moe_first[-1], moe_second[-1])
    )
    d_normed_kv, d_normed_query, sent_first, kept_first, sent_second, kept_second = attention_grads(
        place, digits, sets, shard_count, normed_attn, query_grad_rows,
        normed_all, kv_grad_all, attended, d_branch, grad_gain_ffn[None], grad_router,
        query_full, kv_full, input_all, hidden_in
    )
    kv_scattered = scatter(d_normed_kv)
    d_normed_query = after(d_normed_query, sent_first, sent_second)
    d_normed_attn = kv_scattered.astype(jnp.float32) + d_normed_query
    d_norm_in, _ = norm_back(d_normed_attn, input_float, scale_attn, gain_attn)
    d_input = d_middle + d_norm_in
    for bit_first, bit_second in zip(far[1:], far[::-1][1:]):
        _, moe_first = halve(moe_first, bit_first, 0)
        _, moe_second = halve(moe_second, bit_second, 0)
    def by_piece(block):
        return block.reshape(shard_count, -1, piece_rows, block.shape[2])

    sent_first, sent_second, moe_first[-1], moe_second[-1] = lax.optimization_barrier(
        (sent_first, sent_second, moe_first[-1], moe_second[-1])
    )
    moe_first, moe_second = add_parts(moe_first), add_parts(moe_second)
    sent_first, sent_second = lax.optimization_barrier(
        (sent_first, sent_second, moe_first, moe_second)
    )[:2]
    first = [by_piece(kept_first), exchange(by_piece(sent_first), near)]
    second = [by_piece(kept_second), exchange(by_piece(sent_second), near)]
    for bit_first, bit_second in zip(far[:0:-1], far[:-1]):
        moe_first = double(moe_first, bit_first, 0)
        moe_second = double(moe_second, bit_second, 0)
    for bit_first, bit_second in zip(far, far[::-1]):
        _, first = halve(first, bit_first, 1)
        _, second = halve(second, bit_second, 1)
        if bit_first == far[0]:
            first[-1] = after(first[-1], moe_first, moe_second)
            second[-1] = after(second[-1], moe_first, moe_second)
    first[-1] = after(first[-1], kv_scattered)
    moe_first = after(moe_first, first[-1], second[-1])
    moe_second = after(moe_second, first[-1], second[-1])
    own_first, own_second = moe_first, moe_second
    far_first, far_second = exchange(own_first, far[0]), exchange(own_second, far[-1])
    near_own = exchange(own_first, near), exchange(own_second, near)
    joined = jnp.concatenate([add_parts(first), add_parts(second)], 3)
    joined = joined.reshape(shard_count, piece_rows, -1)
    joined = lax.psum_scatter(joined, "shard", scatter_dimension=0)
    def put(held, pieces, *where):
        pieces = [piece.reshape(-1, columns) for piece in pieces]
        return widen(targets[where], *pieces, shapes, row_units, held)

    held = put([], (own_first, own_second), 0, 0)
    held = put(held, near_own, 0, 1)
    *held, joined, d_input = lax.optimization_barrier((*held, joined, d_input))
    gathered = lax.all_gather(joined, "rep", axis=0)
    *held, far_first, far_second = lax.optimization_barrier((*held, far_first, far_second))
    near_far = exchange(far_first, near), exchange(far_second, near)
    held = put(held, (far_first, far_second), 1, 0)
    held = put(held, near_far, 1, 1)
    sum_in, sum_out = held

    def row_of(at, order):
        return sum(((at // bit) % 2) << (len(order) - 1 - turn) for turn, bit in enumerate(order))

    pairs = tuple(
        (row_of(at, [near] + far), row_of(at, [near] + far[::-1])) for at in range(lax.axis_size("rep"))
    )
    sum_query, sum_key, sum_value, sum_output, sum_router, sum_gains, loss = finish(
        gathered, pairs, (query_width, half_width, kv_width), 3 * sets, expert_count
    )
    loss = loss[0, 0] / (model_width * valid_count)
    return (
        jnp.concatenate(results, 0),
        loss,
        d_input,
        sum_gains[0],
        sum_query,
        sum_key,
        sum_value,
        sum_output,
        sum_gains[1],
        sum_router,
        sum_in,
        sum_out,
    )


def solution(mesh):
    in_specs = (
        P(("rep", "shard"), None),
        P(("rep", "shard")),
        P(("rep", "shard"), None),
        P(("rep", "shard"), None),
        P("shard"),
        P("shard", None),
        P("shard", None),
        P("shard", None),
        P("shard", None),
        P("shard"),
        P("shard", None),
        P("shard", None, None),
        P("shard", None, None),
    )
    out_specs = (
        P(("rep", "shard"), None),
        P(),
        P(("rep", "shard"), None),
        P("shard"),
        P("shard", None),
        P("shard", None),
        P("shard", None),
        P("shard", None),
        P("shard"),
        P("shard", None),
        P("shard", None, None),
        P("shard", None, None),
    )
    return jax.shard_map(body, mesh=mesh, in_specs=in_specs, out_specs=out_specs, check_vma=False)
```
